128 devices in a mesh: dp: 4 (over z_hi, core), row: 8 (over y, z_lo), col: 4 (over x).
Axes of the slice: x: 4, y: 4, z: 4 (z_hi: 2, z_lo: 2; z = z_hi * 2 + z_lo), core: 2. Of those that a mesh axis runs over, the one named last changes fastest.
Arguments:
- stream: float32 [2048, 8, 1536], P('col', 'dp', 'row'), may hold values from -35 to 35
- cotangent: float32 [2048, 8, 1536], P('col', 'dp', 'row'), may hold values from -6 to 6
- segments: int32 [8, 2048], P('dp'), may hold values from 0 to 34, as said below
- positions: int32 [8, 2048], P('dp'), may hold values from 0 to 799, as said below
- qkv_weight: float32 [1536, 3072], P('row', 'col'), may hold values from -0.15625 to 0.15625
- qkv_first: float32 [1536, 3072], P('row', 'col'), may hold values from -80 to 80
- qkv_second: float32 [1536, 3072], P('row', 'col'), may hold values from 491.52 to 3276.8
- out_weight: float32 [1536, 1536], P('col', 'row'), may hold values from -1.25 to 1.25
- out_first: float32 [1536, 1536], P('col', 'row'), may hold values from -8 to 8
- out_second: float32 [1536, 1536], P('col', 'row'), may hold values from 4.9152 to 32.768
- gate_up_weight: float32 [1536, 2, 4096], P('row', None, 'col'), may hold values from -0.15625 to 0.15625
- gate_up_first: float32 [1536, 2, 4096], P('row', None, 'col'), may hold values from -32 to 32
- gate_up_second: float32 [1536, 2, 4096], P('row', None, 'col'), may hold values from 65.536 to 409.6
- down_weight: float32 [4096, 1536], P('col', 'row'), may hold values from -0.09375 to 0.09375
- down_first: float32 [4096, 1536], P('col', 'row'), may hold values from -48 to 48
- down_second: float32 [4096, 1536], P('col', 'row'), may hold values from 180.224 to 1146.88
- gains: float32 [2, 1536], P(None, 'row'), may hold values from 0.5 to 1.5
- gains_first: float32 [2, 1536], P(None, 'row'), may hold values from -80 to 80
- gains_second: float32 [2, 1536], P(None, 'row'), may hold values from 491.52 to 3276.8
Outputs:
- output: float32 [2048, 8, 1536], P('col', 'dp', 'row')
- stream_grad: float32 [2048, 8, 1536], P('col', 'dp', 'row')
- qkv_first_new: float32 [1536, 3072], P('row', 'col')
- qkv_second_new: float32 [1536, 3072], P('row', 'col')
- qkv_weight_new: float32 [1536, 3072], P('row', 'col')
- out_first_new: float32 [1536, 1536], P('col', 'row')
- out_second_new: float32 [1536, 1536], P('col', 'row')
- out_weight_new: float32 [1536, 1536], P('col', 'row')
- gate_up_first_new: float32 [1536, 2, 4096], P('row', None, 'col')
- gate_up_second_new: float32 [1536, 2, 4096], P('row', None, 'col')
- gate_up_weight_new: float32 [1536, 2, 4096], P('row', None, 'col')
- down_first_new: float32 [4096, 1536], P('col', 'row')
- down_second_new: float32 [4096, 1536], P('col', 'row')
- down_weight_new: float32 [4096, 1536], P('col', 'row')
- gains_first_new: float32 [2, 1536], P(None, 'row')
- gains_second_new: float32 [2, 1536], P(None, 'row')
- gains_new: float32 [2, 1536], P(None, 'row')
The draws below stay inside these ranges and needn't reach their ends.
Inputs may be any that keep to these rules, and one draw needn't show every extreme that they name: segments[s, t] numbers the documents of sequence s in increasing order: 0, 1, 2 and so on, except that the last document of every sequence has the number 2048 // 60; each document holds 60 to 800 tokens except that the last of a sequence may be cut short; every sequence holds a document of exactly 800 tokens. positions[s, t] is t minus the index of the first token of its document.
All inputs are finite; a program needn't handle non-finite values.
Results may differ from the reference program's by a relative error of at most 0.014.
Values may be sent and summed in bfloat16 or wider, within the bound.
A program may use at most 192 MiB of HBM per device.

```python
import math
import jax
import jax.numpy as jnp
from jax import lax

D = 1536
FF = 4096
HQ = 16
KVH = 8
HS = 96
LEN = 2048
DOC_MOST = 800
DOC_LEAST = 60
STEP = 10
SEQS = 8
TOKENS = 16384


def packed_tables(key):
    count_docs = LEN // DOC_LEAST + 1
    base_sizes = jax.random.randint(jax.random.fold_in(key, 11), (SEQS, count_docs), DOC_LEAST, DOC_MOST + 1)
    slot_count = (LEN - DOC_MOST) // DOC_MOST + 1
    chosen = jax.random.randint(jax.random.fold_in(key, 12), (SEQS, 1), 0, slot_count)
    doc_sizes = jnp.where(jnp.arange(count_docs, dtype=jnp.int32)[None, :] == chosen, DOC_MOST, base_sizes)
    doc_ends = jnp.cumsum(doc_sizes, axis=1)
    places = jnp.arange(LEN, dtype=jnp.int32)
    passed = doc_ends[:, :, None] <= places[None, None, :]
    numbered = jnp.sum(passed.astype(jnp.int32), axis=1).astype(jnp.int32)
    last_number = jnp.max(numbered, axis=1, keepdims=True)
    segment_table = jnp.where(numbered == last_number, LEN // DOC_LEAST, numbered).astype(jnp.int32)
    doc_start = jnp.max(jnp.where(passed, doc_ends[:, :, None], 0), axis=1)
    return (segment_table, (places[None, :] - doc_start).astype(jnp.int32))


def draw_segments(key, part):
    segment_table, position_table = packed_tables(key)
    return segment_table


def draw_positions(key, part):
    segment_table, position_table = packed_tables(key)
    return position_table


def draw_stream(key, part):
    key = jax.random.fold_in(key, 1)
    values = jnp.clip(jax.random.normal(key, (LEN, SEQS, D), jnp.float32), -6.0, 6.0)
    rising = 3.0
    column = jnp.exp(jnp.log(rising) * (jnp.arange(D, dtype=jnp.float32) / D - 0.5))
    row_scale = jnp.exp(jax.random.uniform(jax.random.fold_in(key, 2), (LEN, SEQS, 1), jnp.float32, -1.2, 1.2))
    return values * column * row_scale


def block_scale(rng, shape, split, least, top_value):
    level = 1.0
    for position, shards_of in split:
        heights = jax.random.uniform(jax.random.fold_in(jax.random.fold_in(rng, 6), position), (shards_of,), jnp.float32, least / len(split), top_value / len(split))
        level = level * jnp.repeat(jnp.exp(heights), shape[position] // shards_of).reshape((-1,) + (1,) * (len(shape) - 1 - position))
    return level


def centred(rng, dims, width, most, shards=(), kind=jnp.bfloat16):
    loudness = block_scale(rng, dims, shards, -0.22, 0.18) if shards else 1.0
    array = jax.random.normal(rng, dims, jnp.float32) * width * loudness
    return jnp.minimum(jnp.maximum(array, -most), most).astype(kind)


def setup_inputs(seed: int = 0) -> dict:
    keys = jax.random.split(jax.random.key(seed), 20)
    stream = draw_stream(jax.random.fold_in(keys[19], 71), 0)
    cotangent = centred(keys[1], (LEN, SEQS, D), 1.0, 6.0, ((0, 4), (1, 4), (2, 8)), jnp.float32)
    segments = draw_segments(jax.random.fold_in(keys[19], 71), 0)
    positions = draw_positions(jax.random.fold_in(keys[19], 71), 0)
    qkv_weight = centred(keys[4], (D, KVH * (HQ // KVH + 2) * HS), D ** -0.5, 0.15625, ((0, 8), (1, 4)), jnp.float32)
    qkv_first = centred(keys[5], (D, KVH * (HQ // KVH + 2) * HS), (0.11 * TOKENS ** 0.5), 80.0, ((0, 8), (1, 4)), jnp.float32)
    qkv_second = jnp.clip(jnp.exp(math.log(3276.8) - 1.89712 * jax.random.uniform(keys[6], (D, KVH * (HQ // KVH + 2) * HS), jnp.float32) ** block_scale(keys[6], (D, KVH * (HQ // KVH + 2) * HS), ((0, 8), (1, 4)), -0.2, 0.2)), 491.52, 3276.8)
    out_weight = centred(keys[7], (HQ * HS, D), (max(HQ * HS // 64, 1)) ** -0.5, 1.25, ((0, 4), (1, 8)), jnp.float32)
    out_first = centred(keys[8], (HQ * HS, D), (0.011 * TOKENS ** 0.5), 8.0, ((0, 4), (1, 8)), jnp.float32)
    out_second = jnp.clip(jnp.exp(math.log(32.768) - 1.89712 * jax.random.uniform(keys[9], (HQ * HS, D), jnp.float32) ** block_scale(keys[9], (HQ * HS, D), ((0, 4), (1, 8)), -0.2, 0.2)), 4.9152, 32.768)
    gate_up_weight = centred(keys[10], (D, 2, FF), D ** -0.5, 0.15625, ((0, 8), (2, 4)), jnp.float32)
    gate_up_first = centred(keys[11], (D, 2, FF), (0.04 * TOKENS ** 0.5), 32.0, ((0, 8), (2, 4)), jnp.float32)
    gate_up_second = jnp.clip(jnp.exp(math.log(409.6) - 1.8325814 * jax.random.uniform(keys[12], (D, 2, FF), jnp.float32) ** block_scale(keys[12], (D, 2, FF), ((0, 8), (2, 4)), -0.2, 0.2)), 65.536, 409.6)
    down_weight = centred(keys[13], (FF, D), FF ** -0.5, 0.09375, ((0, 4), (1, 8)), jnp.float32)
    down_first = centred(keys[14], (FF, D), (0.066 * TOKENS ** 0.5), 48.0, ((0, 4), (1, 8)), jnp.float32)
    down_second = jnp.clip(jnp.exp(math.log(1146.88) - 1.8506 * jax.random.uniform(keys[15], (FF, D), jnp.float32) ** block_scale(keys[15], (FF, D), ((0, 4), (1, 8)), -0.2, 0.2)), 180.224, 1146.88)
    gains = jnp.clip(1.0 + 0.1 * jax.random.normal(keys[16], (2, D), jnp.float32), 0.5, 1.5)
    gains_first = centred(keys[17], (2, D), (0.11 * TOKENS ** 0.5), 80.0, ((1, 8),), jnp.float32)
    gains_second = jnp.clip(jnp.exp(math.log(3276.8) - 1.89712 * jax.random.uniform(keys[18], (2, D), jnp.float32) ** block_scale(keys[18], (2, D), ((1, 8),), -0.2, 0.2)), 491.52, 3276.8)
    return dict(stream=stream, cotangent=cotangent, segments=segments, positions=positions, qkv_weight=qkv_weight, qkv_first=qkv_first, qkv_second=qkv_second, out_weight=out_weight, out_first=out_first, out_second=out_second, gate_up_weight=gate_up_weight, gate_up_first=gate_up_first, gate_up_second=gate_up_second, down_weight=down_weight, down_first=down_first, down_second=down_second, gains=gains, gains_first=gains_first, gains_second=gains_second)


@jax.custom_vjp
def low(v):
    return lax.optimization_barrier(v.astype(jnp.bfloat16)).astype(jnp.float32)

@jax.custom_vjp
def low_back(v):
    return v

def low_keep(v):
    return (low(v), None)

def low_pass(kept, grad):
    return (grad,)

def back_keep(v):
    return (v, None)

def back_low(kept, grad):
    return (low(grad),)
low.defvjp(low_keep, low_pass)
low_back.defvjp(back_keep, back_low)
norm_epsilon = 1e-05
rope_theta = 100000.0
masked_score = -1e+30
beta_first = 0.9
beta_second = 0.95
adam_epsilon = 1e-08
weight_decay = 0.1
highest = lax.Precision.HIGHEST

def rms_scale(values, gain_row):
    return values * lax.rsqrt(lax.optimization_barrier(jnp.mean(values * values, axis=-1, keepdims=True)) + norm_epsilon) * gain_row

def rotate(values, angles_at):
    half_width = values.shape[-1] // 2
    frequency = rope_theta ** (-2.0 * jnp.arange(half_width, dtype=jnp.float32) / values.shape[-1])
    angles = angles_at[..., None].astype(jnp.float32) * frequency
    cosine = jnp.cos(angles)
    sine_part = jnp.sin(angles)
    front_half = values[..., :half_width]
    behind = values[..., half_width:]
    return jnp.concatenate([front_half * cosine - behind * sine_part, behind * cosine + front_half * sine_part], axis=-1)

def attention_block(query_rows, key_rows, value_rows, query_segment, key_segment, query_index):
    scores = low_back(jnp.einsum('bgne,lge->gnbl', query_rows, key_rows, precision=highest) * HS ** (-0.5))
    key_index = jnp.arange(key_rows.shape[0], dtype=jnp.int32)
    allowed = (query_segment[:, None] == key_segment[None, :]) & (query_index[:, None] >= key_index[None, :])
    scores = jnp.where(allowed, scores, masked_score)
    top_score = lax.optimization_barrier(jnp.max(scores, axis=-1, keepdims=True))
    weights = jnp.exp(scores - top_score)
    shares = weights / lax.optimization_barrier(jnp.sum(weights, axis=-1, keepdims=True))
    return jnp.einsum('gnbl,lge->bgne', low(shares), value_rows, precision=highest)

def layer(stream_rows, qkv_weight, out_weight, gate_up_weight, down_weight, gains, segment_row, position_row):
    group_query = HQ // KVH
    normed_one = low(rms_scale(stream_rows, gains[0]))
    qkv_values = low_back(jnp.dot(normed_one, low(qkv_weight), precision=highest))
    qkv_parts = qkv_values.reshape(LEN, KVH, group_query + 2, HS)
    query_rows = low(rotate(qkv_parts[:, :, :group_query], position_row[:, None, None]))
    key_rows = low(rotate(qkv_parts[:, :, group_query], position_row[:, None]))
    value_rows = low(qkv_parts[:, :, group_query + 1])
    block_size = min(512, LEN)
    token_index = jnp.arange(LEN, dtype=jnp.int32)

    def one_block(block_number):
        begin = (block_number * block_size).astype(jnp.int32)
        return attention_block(lax.dynamic_slice_in_dim(query_rows, begin, block_size, 0), key_rows, value_rows, lax.dynamic_slice_in_dim(segment_row, begin, block_size, 0), segment_row, lax.dynamic_slice_in_dim(token_index, begin, block_size, 0))
    attended = lax.map(jax.checkpoint(one_block), jnp.arange(LEN // block_size, dtype=jnp.int32))
    heads_out = low(low_back(attended.reshape(LEN, HQ * HS)))
    attn_branch = low_back(jnp.dot(heads_out, low(out_weight), precision=highest))
    middle = stream_rows + attn_branch
    normed_two = low(rms_scale(middle, gains[1]))
    hidden = jnp.dot(normed_two, low(gate_up_weight.reshape(D, 2 * FF)), precision=highest)
    gate_part = low_back(hidden[:, :FF])
    up_part = low_back(hidden[:, FF:])
    activated = low(jax.nn.silu(gate_part) * up_part)
    ffn_branch = low_back(jnp.dot(activated, low(down_weight), precision=highest))
    return middle + ffn_branch

def adamw_update(weight, moment_one, moment_two, gradient, step_rate, decay_rate):
    moment_one = beta_first * moment_one + (1.0 - beta_first) * gradient
    moment_two = beta_second * moment_two + (1.0 - beta_second) * gradient * gradient
    corrected = moment_one / (1.0 - beta_first ** STEP) / (jnp.sqrt(moment_two / (1.0 - beta_second ** STEP)) + adam_epsilon)
    return (moment_one, moment_two, weight - step_rate * (corrected + decay_rate * weight))

def step_rates():
    return (2.0 / D ** 0.5, 2.0 / max(HQ * HS // 64, 1) ** 0.5, 2.0 / D ** 0.5, 2.0 / FF ** 0.5, 0.4)

def reference(stream, cotangent, segments, positions, qkv_weight, qkv_first, qkv_second, out_weight, out_first, out_second, gate_up_weight, gate_up_first, gate_up_second, down_weight, down_first, down_second, gains, gains_first, gains_second):
    params = (qkv_weight, out_weight, gate_up_weight, down_weight, gains)

    def one_sequence(running, pieces):
        stream_rows, grad_rows, segment_row, position_row = pieces

        def forward(rows_in, qkv_in, out_in, gate_up_in, down_in, gains_in):
            return layer(rows_in, qkv_in, out_in, gate_up_in, down_in, gains_in, segment_row, position_row)
        result, backward = jax.vjp(forward, stream_rows, qkv_weight, out_weight, gate_up_weight, down_weight, gains)
        gradients = backward(grad_rows)
        updated = tuple((before + gradient for before, gradient in zip(running, gradients[1:])))
        return (updated, (result, gradients[0]))
    start_totals = tuple((jnp.zeros(weight_in.shape, jnp.float32) for weight_in in params))
    summed, (outputs, stream_grads) = lax.scan(one_sequence, start_totals, (jnp.moveaxis(stream, 1, 0), jnp.moveaxis(cotangent, 1, 0), segments, positions))
    output = jnp.moveaxis(outputs, 0, 1)
    stream_grad = jnp.moveaxis(stream_grads, 0, 1)
    rate_qkv, rate_out, rate_gate_up, rate_down, rate_gains = step_rates()
    qkv_first_new, qkv_second_new, qkv_weight_new = adamw_update(qkv_weight, qkv_first, qkv_second, summed[0], rate_qkv, weight_decay)
    out_first_new, out_second_new, out_weight_new = adamw_update(out_weight, out_first, out_second, summed[1], rate_out, weight_decay)
    gate_up_first_new, gate_up_second_new, gate_up_weight_new = adamw_update(gate_up_weight, gate_up_first, gate_up_second, summed[2], rate_gate_up, weight_decay)
    down_first_new, down_second_new, down_weight_new = adamw_update(down_weight, down_first, down_second, summed[3], rate_down, weight_decay)
    gains_first_new, gains_second_new, gains_new = adamw_update(gains, gains_first, gains_second, summed[4], rate_gains, 0.0)
    return (output, stream_grad, qkv_first_new, qkv_second_new, qkv_weight_new, out_first_new, out_second_new, out_weight_new, gate_up_first_new, gate_up_second_new, gate_up_weight_new, down_first_new, down_second_new, down_weight_new, gains_first_new, gains_second_new, gains_new)
```

```python
import functools

import jax
import jax.numpy as jnp
from jax import lax
from jax.experimental import pallas as pl
from jax.experimental.pallas import tpu as pltpu
from jax.sharding import PartitionSpec as P

D = 1536
FF = 4096
HQ = 16
KVH = 8
HS = 96
STEP = 10
LEN = 2048
WINDOW = 1024

norm_epsilon = 1e-05
rope_theta = 100000.0
beta_first = 0.9
beta_second = 0.95
adam_epsilon = 1e-08
weight_decay = 0.1
score_scale = HS**-0.5

MESH = pl.DeviceIdType.MESH
BF = jnp.bfloat16
F32 = jnp.float32
VM = pl.BlockSpec(memory_space=pltpu.VMEM)
ANY = pl.BlockSpec(memory_space=pl.ANY)


class Place:
    def __init__(self):
        self.dp = lax.axis_index("dp")
        self.row = lax.axis_index("row")
        self.x = lax.axis_index("col")
        self.zh = lax.div(self.dp, 2)
        self.core = lax.rem(self.dp, 2)
        self.y = lax.div(self.row, 2)
        self.zl = lax.rem(self.row, 2)
        self.z = self.zh * 2 + self.zl

    def at(self, dx=0, dy=0, dz=0, dcore=0):
        x = lax.rem(self.x + (dx + 4), 4)
        y = lax.rem(self.y + (dy + 4), 4)
        z = lax.rem(self.z + (dz + 4), 4)
        core = lax.rem(self.core + dcore, 2)
        return (lax.div(z, 2) * 2 + core, y * 2 + lax.rem(z, 2), x)

    def pair(self):
        return self.at(dcore=1)

    def in_row(self, step):
        return (self.dp, lax.rem(self.row + step, 8), self.x)

    def in_dp(self, step):
        return (lax.rem(self.dp + step, 4), self.row, self.x)


def greet(devices):
    barrier = pltpu.get_barrier_semaphore()
    for device in devices:
        pl.semaphore_signal(barrier, inc=1, device_id=device, device_id_type=MESH)
    pl.semaphore_wait(barrier, len(devices))


class Wire:
    def __init__(self, send, recv, local=None):
        self.send, self.recv, self.local = send, recv, local
        self.sent, self.open, self.near = [], {}, []

    def copy(self, src, dst, device):
        n = len(self.sent)
        made = pltpu.make_async_remote_copy(
            src_ref=src,
            dst_ref=dst,
            send_sem=self.send.at[n],
            recv_sem=self.recv.at[n],
            device_id=device,
            device_id_type=MESH,
        )
        made.start()
        self.sent.append(made)
        self.open[n] = made
        return n

    def arrive(self, *numbers):
        for n in numbers:
            self.open.pop(n).wait_recv()

    def stay(self, src, dst):
        made = pltpu.make_async_copy(src, dst, self.local.at[len(self.near)])
        made.start()
        self.near.append(made)

    def finish(self):
        self.arrive(*list(self.open))
        for made in self.sent:
            made.wait_send()
        for made in self.near:
            made.wait()


def around(me):
    return lax.rem(me + 3, 4), lax.rem(me + 1, 4), lax.rem(me + 2, 4)


def ring_gather(wire, me, right, left, own, slot, on_block=None):
    l, r, o = around(me)
    first = wire.copy(own(0), slot(me, 0), right), wire.copy(own(1), slot(me, 1), left)
    second = wire.copy(own(1), slot(me, 1), right), wire.copy(own(0), slot(me, 0), left)
    yield
    wire.arrive(first[0])
    far0 = wire.copy(slot(l, 0), slot(l, 0), right)
    wire.arrive(first[1])
    far1 = wire.copy(slot(r, 1), slot(r, 1), left)
    yield
    wire.arrive(second[0])
    if on_block:
        on_block(l)
    wire.arrive(second[1])
    if on_block:
        on_block(r)
    yield
    wire.arrive(far0, far1)
    if on_block:
        on_block(o)


def leading(ref):
    found = [()]
    for size in ref.shape[:-2]:
        found = [index + (n,) for index in found for n in range(size)]
    return found


def add_parts(out, refs):
    for index in leading(out):
        at = index + (slice(None), slice(None))
        total = refs[0][at].astype(F32)
        for ref in refs[1:]:
            total = total + ref[at].astype(F32)
        out[at] = total.astype(out.dtype)


def ring_sum(wire, me, right, left, part, far, near, out):
    l, r, o = around(me)

    def send(srcs, dsts, device):
        return [wire.copy(a, b, device) for a, b in zip(srcs, dsts)]

    far0 = send(part(o, 0), far(0), right)
    far1 = send(part(o, 1), far(1), left)
    to_right = send(part(r, 1), near(0, 1), right)
    to_left = send(part(l, 0), near(1, 0), left)
    yield
    wire.arrive(*far0)
    for a, b in zip(far(0), part(r, 0)):
        add_parts(a, [a, b])
    to_right += send(far(0), near(0, 0), right)
    wire.arrive(*far1)
    for a, b in zip(far(1), part(l, 1)):
        add_parts(a, [a, b])
    to_left += send(far(1), near(1, 1), left)
    yield
    wire.arrive(*to_right, *to_left)
    for h in range(2):
        for a, b, c, total in zip(part(me, h), near(0, h), near(1, h), out(h)):
            add_parts(total, [a, b, c])


def side_by_side(*flows):
    flows = list(flows)
    while flows:
        for flow in list(flows):
            try:
                next(flow)
            except StopIteration:
                flows.remove(flow)


def rows(ref, start, size, multiple):
    return ref.at[pl.ds(pl.multiple_of(start, multiple), size)]


def weight_gather(wire, here, own, whole):
    core, zl = here.core, here.zl
    right, left = here.at(dy=1), here.at(dy=-1)
    up, down = here.at(dz=1), here.at(dz=-1)
    l, r, o = around(here.y)

    def mine(j):
        start = (core * 64, core * 64 + 32, 128 + core * 32, 144 + core * 32)[j]
        return rows(own, start, (32, 32, 16, 16)[j], 16)

    def piece(y, j, lo):
        block = y * 2 + lo
        main, rest = block * 128 + core * 64, 1024 + block * 64 + core * 32
        start = (main, main + 32, rest, rest + 16)[j]
        return rows(whole, start, (32, 32, 16, 16)[j], 16)

    def to_pair(y, lo):
        block = y * 2 + lo
        for view in (
            rows(whole, block * 128 + core * 64, 64, 64),
            rows(whole, 1024 + block * 64 + core * 32, 32, 32),
        ):
            wire.copy(view, view, here.pair())

    def over(y, js, device, src=None):
        return [wire.copy((src or (lambda j: piece(y, j, zl)))(j), piece(y, j, zl), device) for j in js]

    y = here.y
    wire.stay(own.at[pl.ds(0, 128)], rows(whole, here.row * 128, 128, 128))
    wire.stay(own.at[pl.ds(128, 64)], rows(whole, 1024 + here.row * 64, 64, 64))
    r_first, l_first = over(y, (0, 2), right, mine), over(y, (1, 3), left, mine)
    r_next, l_next = over(y, (1, 3), right, mine), over(y, (0, 2), left, mine)
    z_own = over(y, (0, 2), up, mine) + over(y, (1, 3), down, mine)
    yield
    wire.arrive(*r_first)
    far = over(l, (0, 2), right)
    wire.arrive(*l_first)
    far += over(r, (1, 3), left)
    z_l = over(l, (0, 2), up)
    z_r = over(r, (1, 3), down)
    yield
    wire.arrive(*r_next)
    z_l += over(l, (1, 3), down)
    to_pair(l, zl)
    wire.arrive(*l_next)
    z_r += over(r, (0, 2), up)
    to_pair(r, zl)
    yield
    wire.arrive(*far)
    z_o = over(o, (0, 2), up) + over(o, (1, 3), down)
    to_pair(o, zl)
    yield
    for block, numbers in ((y, z_own), (l, z_l), (r, z_r), (o, z_o)):
        wire.arrive(*numbers)
        to_pair(block, 1 - zl)
        yield


class Shared:
    def __init__(self, wire, here, own, out):
        self.wire, self.here, self.own, self.out = wire, here, own, out

    def half(self, ref, h):
        return ref.at[pl.ds(64 * h, 64)]

    def flow(self):
        here, wire = self.here, self.wire
        wire.stay(self.own, self.out.at[here.x])
        wire.copy(self.own, self.out.at[here.x + 4], here.pair())

        def on_block(i):
            wire.copy(self.out.at[i], self.out.at[i + 4], here.pair())

        yield from ring_gather(
            wire,
            here.x,
            here.at(dx=1),
            here.at(dx=-1),
            lambda h: self.half(self.own, h),
            lambda i, h: self.half(self.out.at[i], h),
            on_block,
        )


def x_sum(wire, here, part, far, near, out):
    return ring_sum(
        wire,
        here.x,
        here.at(dx=1),
        here.at(dx=-1),
        lambda i, h: [part.at[i, pl.ds(64 * h, 64)]],
        lambda h: [far.at[h]],
        lambda s, h: [near.at[s, pl.ds(64 * h, 64)]],
        lambda h: [out.at[pl.ds(64 * h, 64)]],
    )


def x_sum_scratch():
    return [pltpu.VMEM((2, 64, D), BF), pltpu.VMEM((2, 128, D), BF)]


HIGHS = (64, 32)


def grad_scratch(width, cut):
    shapes = []
    for columns in (cut, width - cut):
        for high in HIGHS:
            shapes += [
                pltpu.VMEM((2, 2, high, columns), BF),
                pltpu.VMEM((2, 2, 2, high, columns), BF),
                pltpu.VMEM((2, 2, high, columns), BF),
                pltpu.VMEM((2, high // 2, columns), BF),
                pltpu.VMEM((2, 2, high // 2, columns), BF),
            ]
    return shapes + [pltpu.VMEM((96, width), BF)]


def grad_flows(wire, here, grads, scratch, width, cut):
    fin = scratch[-1]
    ends = (0, 64, 96)

    def flow(order, buffers):
        columns = pl.ds(0, cut) if order == 0 else pl.ds(cut, width - cut)
        y_ring = (here.y, here.at(dy=1), here.at(dy=-1))
        z_ring = (here.z, here.at(dz=1), here.at(dz=-1))

        def of_z(ref, i, h):
            return ref.at[pl.ds(2 * h, 2), lax.rem(i, 2), lax.div(i, 2), :, columns]

        def of_y(ref, i, h):
            return ref.at[i, h, :, :, columns]

        far = lambda h: [b[0].at[h] for b in buffers]
        near = lambda s, h: [b[1].at[s, h] for b in buffers]
        mid = lambda h: [b[2].at[h] for b in buffers]
        first, second = (z_ring, y_ring) if order == 0 else (y_ring, z_ring)
        pick = of_z if order == 0 else of_y
        yield from ring_sum(
            wire, *first, lambda i, h: [pick(g, i, h) for g in grads], far, near,
            lambda h: [b[2].at[h] for b in buffers],
        )
        yield

        def part(i, h):
            lead = (lax.div(i, 2), lax.rem(i, 2)) if order == 0 else (lax.rem(i, 2), lax.div(i, 2))
            return [
                b[2].at[lead[0], lead[1], pl.ds(high // 2 * h, high // 2)]
                for b, high in zip(buffers, HIGHS)
            ]

        yield from ring_sum(
            wire, *second, part,
            lambda h: [b[3].at[h] for b in buffers],
            lambda s, h: [b[4].at[s, h] for b in buffers],
            lambda h: [
                fin.at[pl.ds(start + high // 2 * h, high // 2), columns]
                for start, high in zip(ends, HIGHS)
            ],
        )

    buffers = [scratch[5 * n : 5 * n + 5] for n in range(4)]
    return flow(0, buffers[:2]), flow(1, buffers[2:])


def grad_share(wire, here, fin, out, width):
    columns = pl.ds(pl.multiple_of(here.core * width, 128), width)
    mine = out.at[here.zh, :, columns]
    other = out.at[1 - here.zh, :, columns]
    wire.stay(fin, mine)
    wire.copy(fin, mine, here.pair())
    n = wire.copy(fin, mine, here.at(dz=2))
    yield
    wire.arrive(n)
    wire.copy(other, other, here.pair())


def swap_rows(wire, here, src, dst):
    return [
        wire.copy(src.at[lax.rem(here.row + s, 8)], dst.at[here.row], here.in_row(s))
        for s in range(1, 8)
    ]


def widened(ref, start, size):
    at = pl.ds(start, size)
    main = [ref[r, at, 0:128] for r in range(8)]
    rest = [ref[2 * j, at, 128:256] + ref[2 * j + 1, at, 128:256] for j in range(4)]
    return jnp.concatenate(main + rest, axis=1)


def narrowed(out, value):
    for r in range(8):
        out[r, :, 0:128] = value[:, 128 * r : 128 * r + 128]
        j = 1024 + 128 * (r // 2)
        out[r, :, 128:256] = value[:, j : j + 128]


def ring_partners(here):
    return [here.at(dx=1), here.at(dx=-1)]


def plane_partners(here):
    return [here.at(dy=1), here.at(dy=-1), here.at(dz=1), here.at(dz=-1)]


def enter_kernel(
    xin, cin, win, h1_all, w_all, xtok, ctok, gtok, xbuf, cbuf, h1own, send, recv, local
):
    here = Place()
    wire = Wire(send, recv, local)
    greet(
        [here.in_row(s) for s in range(1, 8)]
        + ring_partners(here)
        + [here.at(dz=1), here.at(dz=-1), here.pair()]
    )
    xs = swap_rows(wire, here, xin, xbuf)
    weights = weight_gather(wire, here, win, w_all)
    next(weights)
    cs = swap_rows(wire, here, cin, cbuf)
    xbuf[here.row] = xin[here.row]
    cbuf[here.row] = cin[here.row]
    wire.arrive(*xs)
    x = widened(xbuf, 0, 128)
    xtok[...] = x
    g = widened(xbuf, 128, 16).astype(F32)
    gains = g[0:2] + g[2:4]
    gtok[...] = gains
    x = x.astype(F32)
    scale = lax.rsqrt(jnp.mean(x * x, axis=1, keepdims=True) + norm_epsilon)
    h1own[...] = (x * scale * gains[0:1]).astype(BF)
    side_by_side(Shared(wire, here, h1own, h1_all).flow(), weights)
    wire.arrive(*cs)
    ctok[...] = widened(cbuf, 0, 128)
    wire.finish()


def enter(xin, cin, win):
    columns = win.shape[1]
    n = 80
    return pl.pallas_call(
        enter_kernel,
        out_shape=[
            jax.ShapeDtypeStruct((8, 128, D), BF),
            jax.ShapeDtypeStruct((D, columns), BF),
            jax.ShapeDtypeStruct((128, D), BF),
            jax.ShapeDtypeStruct((128, D), BF),
            jax.ShapeDtypeStruct((2, D), F32),
        ],
        in_specs=[VM, VM, ANY],
        out_specs=[ANY, ANY, VM, VM, VM],
        scratch_shapes=[
            pltpu.VMEM((8, 144, 256), BF),
            pltpu.VMEM((8, 128, 256), BF),
            pltpu.VMEM((128, D), BF),
            pltpu.SemaphoreType.DMA((n,)),
            pltpu.SemaphoreType.DMA((n,)),
            pltpu.SemaphoreType.DMA((4,)),
        ],
        compiler_params=pltpu.CompilerParams(
            collective_id=1, has_side_effects=True, vmem_limit_bytes=24 << 20
        ),
        name="enter",
    )(xin, cin, win)


def keys_kernel(kv_own, ctok, kv_all, c_all, send, recv, local):
    here = Place()
    wire = Wire(send, recv, local)
    greet(ring_partners(here) + [here.at(dy=1), here.at(dy=-1), here.pair()])
    wire.stay(kv_own, kv_all.at[:, here.y])
    keys = ring_gather(
        wire,
        here.y,
        here.at(dy=1),
        here.at(dy=-1),
        lambda h: kv_own.at[pl.ds(2 * h, 2)],
        lambda i, h: kv_all.at[pl.ds(2 * h, 2), i],
    )
    side_by_side(keys, Shared(wire, here, ctok, c_all).flow())
    wire.finish()


def gather_keys(kv_own, ctok):
    return pl.pallas_call(
        keys_kernel,
        out_shape=[
            jax.ShapeDtypeStruct((4, 4, 128, 4 * HS), BF),
            jax.ShapeDtypeStruct((8, 128, D), BF),
        ],
        in_specs=[ANY, ANY],
        out_specs=[ANY, ANY],
        scratch_shapes=[
            pltpu.SemaphoreType.DMA((24,)),
            pltpu.SemaphoreType.DMA((24,)),
            pltpu.SemaphoreType.DMA((4,)),
        ],
        compiler_params=pltpu.CompilerParams(collective_id=2, has_side_effects=True),
        name="keys",
    )(kv_own, ctok)


def middle_kernel(
    part, xtok, gtok, win, middle, h2_all, w_all, far, near, h2own, send, recv, local
):
    here = Place()
    wire = Wire(send, recv, local)
    greet(ring_partners(here) + plane_partners(here) + [here.pair()])

    def chain():
        yield from x_sum(wire, here, part, far, near, middle)
        value = middle[...] + xtok[...].astype(F32)
        middle[...] = value
        scale = lax.rsqrt(jnp.mean(value * value, axis=1, keepdims=True) + norm_epsilon)
        h2own[...] = (value * scale * gtok[1:2]).astype(BF)
        yield from Shared(wire, here, h2own, h2_all).flow()

    side_by_side(chain(), weight_gather(wire, here, win, w_all))
    wire.finish()


def to_middle(part, xtok, gtok, win):
    columns = win.shape[1]
    return pl.pallas_call(
        middle_kernel,
        out_shape=[
            jax.ShapeDtypeStruct((128, D), F32),
            jax.ShapeDtypeStruct((8, 128, D), BF),
            jax.ShapeDtypeStruct((D, columns), BF),
        ],
        in_specs=[VM, VM, VM, ANY],
        out_specs=[VM, ANY, ANY],
        scratch_shapes=x_sum_scratch()
        + [
            pltpu.VMEM((128, D), BF),
            pltpu.SemaphoreType.DMA((64,)),
            pltpu.SemaphoreType.DMA((64,)),
            pltpu.SemaphoreType.DMA((4,)),
        ],
        compiler_params=pltpu.CompilerParams(
            collective_id=3, has_side_effects=True, vmem_limit_bytes=24 << 20
        ),
        name="middle",
    )(part, xtok, gtok, win)


def swap_units_kernel(count, *refs):
    arrays, outs, (send, recv, local) = refs[:count], refs[count : 2 * count], refs[2 * count :]
    here = Place()
    wire = Wire(send, recv, local)
    greet([here.pair()])
    for a, out in zip(arrays, outs):
        if len(a.shape) == 2:
            width = a.shape[1] // 2
            pick = lambda k: a.at[:, pl.ds(pl.multiple_of(k * width, 128), width)]
        else:
            pick = lambda k: a.at[k]
        wire.copy(pick(1 - here.core), out.at[1], here.pair())
        wire.stay(pick(here.core), out.at[0])
    wire.finish()


def swap_units(arrays, number):
    count = len(arrays)
    shapes = [
        (2, a.shape[0], a.shape[1] // 2) if a.ndim == 2 else (2, *a.shape[1:]) for a in arrays
    ]
    return pl.pallas_call(
        functools.partial(swap_units_kernel, count),
        out_shape=[jax.ShapeDtypeStruct(s, BF) for s in shapes],
        in_specs=[ANY] * count,
        out_specs=[ANY] * count,
        scratch_shapes=[pltpu.SemaphoreType.DMA((count,))] * 3,
        compiler_params=pltpu.CompilerParams(collective_id=number, has_side_effects=True),
        name="swap_units",
    )(*arrays)


def turn_kernel(width, cut, *refs):
    part, middle, gtok, ctok, main, rest, after, gain, d_all, gout = refs[:10]
    far, near, summed, down = refs[10:14]
    scratch, (send, recv, local) = refs[14:-3], refs[-3:]
    here = Place()
    wire = Wire(send, recv, local)
    greet(
        ring_partners(here) + plane_partners(here) + [here.at(dz=2), here.pair()]
    )
    zy, yz = grad_flows(wire, here, (main, rest), scratch, width, cut)

    def chain():
        yield from x_sum(wire, here, part, far, near, summed)
        value, grad = middle[...], summed[...]
        scale = lax.rsqrt(jnp.mean(value * value, axis=1, keepdims=True) + norm_epsilon)
        n2 = value * scale
        gain[...] = jnp.broadcast_to(jnp.sum(grad * n2, axis=0, keepdims=True), gain.shape)
        e2 = grad * gtok[1:2]
        inner = jnp.mean(e2 * n2, axis=1, keepdims=True)
        left = scale * (e2 - n2 * inner)
        after[...] = left
        down[...] = (left + ctok[...].astype(F32)).astype(BF)
        yield from Shared(wire, here, down, d_all).flow()

    side_by_side(chain(), zy, yz)
    side_by_side(grad_share(wire, here, scratch[-1], gout, width))
    wire.finish()


def turn(part, middle, gtok, ctok, main, rest):
    width = main.shape[-1]
    cut = width // 2
    return pl.pallas_call(
        functools.partial(turn_kernel, width, cut),
        out_shape=[
            jax.ShapeDtypeStruct((128, D), F32),
            jax.ShapeDtypeStruct((8, D), F32),
            jax.ShapeDtypeStruct((8, 128, D), BF),
            jax.ShapeDtypeStruct((2, 96, 2 * width), BF),
        ],
        in_specs=[VM] * 6,
        out_specs=[VM, VM, ANY, ANY],
        scratch_shapes=x_sum_scratch()
        + [pltpu.VMEM((128, D), F32), pltpu.VMEM((128, D), BF)]
        + grad_scratch(width, cut)
        + [
            pltpu.SemaphoreType.DMA((80,)),
            pltpu.SemaphoreType.DMA((80,)),
            pltpu.SemaphoreType.DMA((4,)),
        ],
        compiler_params=pltpu.CompilerParams(
            collective_id=4, has_side_effects=True, vmem_limit_bytes=40 << 20
        ),
        name="turn",
    )(part, middle, gtok, ctok, main, rest)


def key_grads_kernel(
    dkv, part, middle, xtok, dkv_own, branch, far, near, summed, kfar, knear, send, recv
):
    here = Place()
    wire = Wire(send, recv)
    greet(ring_partners(here) + [here.at(dy=1), here.at(dy=-1)])
    keys = ring_sum(
        wire,
        here.y,
        here.at(dy=1),
        here.at(dy=-1),
        lambda i, h: [dkv.at[pl.ds(2 * h, 2), i]],
        lambda h: [kfar.at[h]],
        lambda s, h: [knear.at[s, h]],
        lambda h: [dkv_own.at[pl.ds(2 * h, 2)]],
    )
    side_by_side(keys, x_sum(wire, here, part, far, near, summed))
    branch[...] = (summed[...] + (middle[...] - xtok[...].astype(F32))).astype(BF)
    wire.finish()


def key_grads(dkv, part, middle, xtok):
    return pl.pallas_call(
        key_grads_kernel,
        out_shape=[
            jax.ShapeDtypeStruct((4, 128, 4 * HS), F32),
            jax.ShapeDtypeStruct((128, D), BF),
        ],
        in_specs=[VM] * 4,
        out_specs=[VM] * 2,
        scratch_shapes=x_sum_scratch()
        + [
            pltpu.VMEM((128, D), F32),
            pltpu.VMEM((2, 2, 128, 4 * HS), BF),
            pltpu.VMEM((2, 2, 2, 128, 4 * HS), BF),
            pltpu.SemaphoreType.DMA((16,)),
            pltpu.SemaphoreType.DMA((16,)),
        ],
        compiler_params=pltpu.CompilerParams(
            collective_id=5, has_side_effects=True, vmem_limit_bytes=24 << 20
        ),
        name="key_grads",
    )(dkv, part, middle, xtok)


def leave_kernel(width, cut, *refs):
    part, xtok, after, gtok, branch, gain, main, rest = refs[:8]
    o_all, s_all, gout, gains_out = refs[8:12]
    far, near, summed, osend, ssend, gsend, grow, gcol, gdp = refs[12:21]
    scratch, (send, recv, local) = refs[21:-3], refs[-3:]
    here = Place()
    wire = Wire(send, recv, local)
    greet(
        [here.in_row(s) for s in range(1, 8)]
        + ring_partners(here)
        + [here.at(dz=1), here.at(dz=-1), here.at(dx=2)]
        + [here.in_dp(s) for s in range(1, 4)]
    )
    narrowed(osend, branch[...])
    zy, yz = grad_flows(wire, here, (main, rest), scratch, width, cut)

    def chain():
        yield from x_sum(wire, here, part, far, near, summed)
        value, grad = xtok[...].astype(F32), summed[...]
        scale = lax.rsqrt(jnp.mean(value * value, axis=1, keepdims=True) + norm_epsilon)
        n1 = value * scale
        gains = jnp.concatenate(
            [jnp.sum(grad * n1, axis=0, keepdims=True), gain[0:1], jnp.zeros((6, D), F32)], axis=0
        )
        narrowed(gsend, gains)
        g = swap_rows(wire, here, gsend, grow)
        e1 = grad * gtok[0:1]
        inner = jnp.mean(e1 * n1, axis=1, keepdims=True)
        left = scale * (e1 - n1 * inner) + after[...]
        narrowed(ssend, left.astype(BF))
        wire.stay(ssend.at[here.row], s_all.at[here.row])
        swap_rows(wire, here, ssend, s_all)
        yield
        wire.arrive(*g)
        grow[here.row] = gsend[here.row]
        total = grow[0]
        for n in range(1, 8):
            total = total + grow[n]
        gcol[here.x] = total
        g = [
            wire.copy(gcol.at[here.x], gcol.at[here.x], here.at(dx=s)) for s in range(1, 4)
        ]
        yield
        wire.arrive(*g)
        gdp[here.dp] = ((gcol[0] + gcol[1]) + gcol[2]) + gcol[3]
        g = [wire.copy(gdp.at[here.dp], gdp.at[here.dp], here.in_dp(s)) for s in range(1, 4)]
        yield
        wire.arrive(*g)
        gains_out[...] = ((gdp[0] + gdp[1]) + gdp[2]) + gdp[3]

    steps = chain()
    next(steps)
    next(zy)
    next(yz)
    wire.stay(osend.at[here.row], o_all.at[here.row])
    swap_rows(wire, here, osend, o_all)
    side_by_side(steps, zy, yz)
    side_by_side(grad_share(wire, here, scratch[-1], gout, width))
    wire.finish()


def leave(part, xtok, after, gtok, branch, gain, main, rest):
    width = main.shape[-1]
    cut = 256
    return pl.pallas_call(
        functools.partial(leave_kernel, width, cut),
        out_shape=[
            jax.ShapeDtypeStruct((8, 128, 256), BF),
            jax.ShapeDtypeStruct((8, 128, 256), BF),
            jax.ShapeDtypeStruct((2, 96, 2 * width), BF),
            jax.ShapeDtypeStruct((8, 256), F32),
        ],
        in_specs=[VM] * 8,
        out_specs=[ANY, ANY, ANY, VM],
        scratch_shapes=x_sum_scratch()
        + [
            pltpu.VMEM((128, D), F32),
            pltpu.VMEM((8, 128, 256), BF),
            pltpu.VMEM((8, 128, 256), BF),
            pltpu.VMEM((8, 8, 256), F32),
            pltpu.VMEM((8, 8, 256), F32),
            pltpu.VMEM((4, 8, 256), F32),
            pltpu.VMEM((4, 8, 256), F32),
        ]
        + grad_scratch(width, cut)
        + [
            pltpu.SemaphoreType.DMA((96,)),
            pltpu.SemaphoreType.DMA((96,)),
            pltpu.SemaphoreType.DMA((4,)),
        ],
        compiler_params=pltpu.CompilerParams(
            collective_id=6, has_side_effects=True, vmem_limit_bytes=40 << 20
        ),
        name="leave",
    )(part, xtok, after, gtok, branch, gain, main, rest)


def windows(y):
    return ((0, 512), (0, WINDOW), (128 * (1 + y), WINDOW), (128 * (5 + y), WINDOW))


def dot(a, b, left, right):
    return lax.dot_general(a, b, (((left,), (right,)), ((), ())), preferred_element_type=F32)


def allowed_keys(table, c, start, count):
    key = start + lax.broadcasted_iota(jnp.int32, (count, 256), 0)
    return (key >= table[2 * c : 2 * c + 1]) & (key <= table[2 * c + 1 : 2 * c + 2])


def both_heads(ref, at):
    return jnp.concatenate([ref[at, 0:256], ref[at, 256:512]], axis=0)


def attend_kernel(q, kv, table, heads, log_total):
    y = lax.div(lax.axis_index("row"), 2)
    lane = lax.broadcasted_iota(jnp.int32, (256, 256), 1)
    for c, (start, count) in enumerate(windows(y)):
        keys = pl.ds(start if isinstance(start, int) else pl.multiple_of(start, 128), count)
        at = pl.ds(128 * c, 128)
        allowed = allowed_keys(table, c, start, count)
        q_both = both_heads(q, at)
        made = []
        for g in range(2):
            n = 2 * c + g
            q_one = jnp.where((lane >= HS) == (g == 1), q_both, jnp.zeros_like(q_both))
            scores = dot(kv[keys, 0:256], q_one, 1, 1) * score_scale
            scores = jnp.where(allowed, scores, -1e30)
            top = jnp.max(scores, axis=0, keepdims=True)
            weights = jnp.exp(scores - top)
            total = jnp.sum(weights, axis=0, keepdims=True)
            shares = (weights * (1.0 / total)).astype(BF)
            made.append(dot(shares, kv[keys, 128:384], 0, 0))
            log_total[n : n + 1] = top + jnp.log(total)
        out = jnp.where(lane < 64 + HS, made[0], made[1])
        out = jnp.where(lane < 64, 0.0, out).astype(BF)
        heads[at, 0:256] = out[:128]
        heads[at, 256:512] = out[128:]


def attend(q, kv, table):
    return pl.pallas_call(
        attend_kernel,
        out_shape=[
            jax.ShapeDtypeStruct((512, 512), BF),
            jax.ShapeDtypeStruct((8, 256), F32),
        ],
        in_specs=[VM] * 3,
        out_specs=[VM] * 2,
        compiler_params=pltpu.CompilerParams(vmem_limit_bytes=40 << 20),
        name="attend",
    )(q, kv, table)


def attend_back_kernel(q, kv, table, log_total, dout, dq, dkv, total):
    y = lax.div(lax.axis_index("row"), 2)
    lane = lax.broadcasted_iota(jnp.int32, (256, 256), 1)
    total[...] = jnp.zeros_like(total)
    for c, (start, count) in enumerate(windows(y)):
        keys = pl.ds(start if isinstance(start, int) else pl.multiple_of(start, 128), count)
        at = pl.ds(128 * c, 128)
        allowed = allowed_keys(table, c, start, count)
        q_both, d_both = both_heads(q, at), both_heads(dout, at)
        made = []
        for g in range(2):
            n = 2 * c + g
            q_one = jnp.where((lane >= HS) == (g == 1), q_both, jnp.zeros_like(q_both))
            d_one = jnp.where((lane >= 64 + HS) == (g == 1), d_both, jnp.zeros_like(d_both))
            scores = dot(kv[keys, 0:256], q_one, 1, 1) * score_scale
            shares = jnp.where(allowed, jnp.exp(scores - log_total[n : n + 1]), 0.0)
            dshares = dot(kv[keys, 128:384], d_one, 1, 1)
            inner = jnp.sum(shares * dshares, axis=0, keepdims=True)
            dscores = (shares * (dshares - inner)).astype(BF)
            made.append(dot(dscores, kv[keys, 0:256], 0, 0))
            total[keys, 0:256] += dot(dscores, q_one, 1, 0) * score_scale
            total[keys, 128:384] += dot(shares.astype(BF), d_one, 1, 0)
        out = jnp.where(lane < HS, made[0], made[1]) * score_scale
        dq[at, 0:256] = out[:128]
        dq[at, 256:512] = out[128:]
    dkv[...] = total[...].astype(BF)


def attend_back(q, kv, table, log_total, dout):
    return pl.pallas_call(
        attend_back_kernel,
        out_shape=[
            jax.ShapeDtypeStruct((512, 512), F32),
            jax.ShapeDtypeStruct((LEN, 4 * HS), BF),
        ],
        in_specs=[VM] * 5,
        out_specs=[VM] * 2,
        scratch_shapes=[pltpu.VMEM((LEN, 4 * HS), F32)],
        compiler_params=pltpu.CompilerParams(vmem_limit_bytes=48 << 20),
        name="attend_back",
    )(q, kv, table, log_total, dout)


def turned(values, cosine, sine):
    half = values.shape[-1] // 2
    front, behind = values[..., :half], values[..., half:]
    return jnp.concatenate(
        [front * cosine - behind * sine, behind * cosine + front * sine], axis=-1
    )


def adamw_update(weight, moment_one, moment_two, gradient, step_rate, decay_rate):
    moment_one = beta_first * moment_one + (1.0 - beta_first) * gradient
    moment_two = beta_second * moment_two + (1.0 - beta_second) * gradient * gradient
    corrected = (
        moment_one
        / (1.0 - beta_first**STEP)
        / (jnp.sqrt(moment_two / (1.0 - beta_second**STEP)) + adam_epsilon)
    )
    return (moment_one, moment_two, weight - step_rate * (corrected + decay_rate * weight))


def step_rates():
    return (2.0 / D**0.5, 2.0 / max(HQ * HS // 64, 1) ** 0.5, 2.0 / D**0.5, 2.0 / FF**0.5, 0.4)


def mm(a, b, form):
    return jnp.einsum(form, a, b, preferred_element_type=F32)


def body(
    stream,
    cotangent,
    segments,
    positions,
    qkv_weight,
    qkv_first,
    qkv_second,
    out_weight,
    out_first,
    out_second,
    gate_up_weight,
    gate_up_first,
    gate_up_second,
    down_weight,
    down_first,
    down_second,
    gains,
    gains_first,
    gains_second,
):
    row = lax.axis_index("row")
    zl, y = row % 2, row // 2
    odd = zl == 1

    def packed(values):
        main, rest = values[..., :128], values[..., 128:]
        none = jnp.zeros_like(rest)
        tile = jnp.where(
            odd, jnp.concatenate([none, rest], -1), jnp.concatenate([rest, none], -1)
        )
        return jnp.concatenate([main, tile], -1).astype(BF)

    def by_row(values):
        return values.reshape(4, 128, 2, 192).transpose(0, 2, 1, 3).reshape(8, 128, 192)

    def unpacked(tiles):
        tiles = tiles.astype(F32)
        rest = jnp.where(odd, tiles[..., 192:256], tiles[..., 128:192])
        both = jnp.concatenate([tiles[..., :128], rest], -1)
        return both.reshape(4, 2, 128, 192).transpose(0, 2, 1, 3).reshape(512, 2, 192)

    high = lax.reduce_precision(gains, 8, 7)
    gain_rows = jnp.concatenate([high, gains - high, jnp.zeros((12, 192), F32)], 0)
    xin = jnp.concatenate(
        [packed(by_row(stream)), jnp.broadcast_to(packed(gain_rows), (8, 16, 256))], 1
    )
    cin = packed(by_row(cotangent))
    qkv_low = qkv_weight.astype(BF).reshape(192, 2, 4, HS)
    out_low = out_weight.astype(BF).reshape(2, 2, HS, 192).transpose(1, 0, 2, 3)
    out_low = jnp.pad(out_low.reshape(2, 2 * HS, 192), ((0, 0), (64, 0), (0, 0))).reshape(512, 192)
    first_weights = jnp.concatenate(
        [
            qkv_low[:, :, :2].transpose(0, 2, 1, 3).reshape(192, 384),
            qkv_low[:, :, 2:].transpose(0, 2, 1, 3).reshape(192, 384),
            out_low.T,
        ],
        1,
    )
    second_weights = jnp.concatenate(
        [gate_up_weight.reshape(192, 2048).astype(BF), down_weight.astype(BF).T], 1
    )

    h1_all, w1, xtok, ctok, gtok = enter(xin, cin, first_weights)
    wq, wo = w1[:, :768], w1[:, 768:]

    place = lax.dynamic_index_in_dim(positions, zl, 0, keepdims=False).reshape(4, 4, 128)
    place = lax.dynamic_index_in_dim(place, y, 1, keepdims=False)
    token = (
        jnp.arange(4, dtype=jnp.int32)[:, None] * 512
        + y * 128
        + jnp.arange(128, dtype=jnp.int32)[None, :]
    )
    table = jnp.stack([token - place, token], 1)
    table = jnp.concatenate([table, table], -1).reshape(8, 256)
    frequency = rope_theta ** (-2.0 * jnp.arange(HS // 2, dtype=F32) / HS)
    angles = place.reshape(512)[:, None].astype(F32) * frequency
    cosine, sine = jnp.cos(angles), jnp.sin(angles)

    qkv = mm(h1_all[:4].reshape(512, D), wq, "td,dz->tz").reshape(512, 8, HS)
    rotated = turned(qkv[:, :6], cosine[:, None], sine[:, None]).astype(BF)
    q = jnp.pad(rotated[:, :4].reshape(512, 2, 2 * HS), ((0, 0), (0, 0), (0, 64))).reshape(512, 512)
    kv_own = jnp.concatenate([rotated[:, 4:], qkv[:, 6:].astype(BF)], 1).reshape(4, 128, 4 * HS)
    kv_all, c_all = gather_keys(kv_own, ctok)
    kv_all = kv_all.reshape(LEN, 4 * HS)
    heads, log_total = attend(q, kv_all, table)
    attn_part = mm(heads, wo, "tz,dz->td").astype(BF).reshape(4, 128, D)

    middle, h2_all, w2 = to_middle(attn_part, xtok, gtok, second_weights)
    w_gate_up, w_down = w2[:, :2048], w2[:, 2048:]
    hidden = mm(h2_all[:4].reshape(512, D), w_gate_up, "td,dz->tz")
    gate, up = hidden[:, :1024], hidden[:, 1024:]
    sigmoid_gate = jax.nn.sigmoid(gate)
    silu_gate = gate * sigmoid_gate
    act = (silu_gate * up).astype(BF)
    act_grad = mm(c_all[:4].reshape(512, D), w_down, "td,dz->tz")
    gate_grad = (act_grad * up * sigmoid_gate * (1.0 + gate * (1.0 - sigmoid_gate))).astype(BF)
    up_grad = (act_grad * silu_gate).astype(BF)
    hidden_grad = jnp.concatenate([gate_grad, up_grad], -1)
    h2_grad_part = mm(hidden_grad, w_gate_up, "tz,dz->td").astype(BF).reshape(4, 128, D)
    ffn_part = mm(act, w_down, "tz,dz->td").astype(BF).reshape(4, 128, D)

    def weight_grads(pairs):
        parts = []
        for cut, high in ((slice(0, 1024), 64), (slice(1024, 1536), 32)):
            made = [
                mm(tokens.reshape(1024, D)[:, cut], units.reshape(1024, -1), "td,tz->dz").astype(BF)
                for tokens, units in pairs
            ]
            parts.append(jnp.concatenate(made, 1).reshape(4, 2, 2, high, -1))
        return parts

    gate_both, up_both, act_both = swap_units([gate_grad, up_grad, act], 7)
    main2, rest2 = weight_grads(
        [(h2_all, jnp.concatenate([gate_both, up_both], -1)), (c_all, act_both)]
    )
    after, gain_two, d_all, grads2 = turn(h2_grad_part, middle, gtok, ctok, main2, rest2)

    dout = mm(d_all[:4].reshape(512, D), wo, "td,dz->tz").astype(BF)
    dq, dkv = attend_back(q, kv_all, table, log_total, dout)
    dkv_own, branch = key_grads(dkv.reshape(4, 4, 128, 4 * HS), ffn_part, middle, xtok)
    dkv_own = dkv_own.reshape(512, 4, HS)
    dqk = jnp.concatenate(
        [dq.reshape(512, 2, 256)[:, :, : 2 * HS].reshape(512, 4, HS), dkv_own[:, :2]], 1
    )
    dqk = turned(dqk, cosine[:, None], -sine[:, None])
    dqkv = jnp.concatenate([dqk, dkv_own[:, 2:]], 1).reshape(512, 768).astype(BF)
    h1_grad_part = mm(dqkv, wq, "tz,dz->td").astype(BF).reshape(4, 128, D)
    dqkv_both, heads_both = swap_units([dqkv, heads], 8)
    main1, rest1 = weight_grads([(h1_all, dqkv_both), (d_all, heads_both)])
    o_tiles, s_tiles, grads1, gains_tile = leave(
        h1_grad_part, xtok, after, gtok, branch, gain_two, main1, rest1
    )
    output = stream + unpacked(o_tiles)
    stream_grad = cotangent + unpacked(s_tiles)

    def own_block(grads):
        grads = grads.reshape(2, 96, 2, -1)
        block = jnp.concatenate([grads[0, :64], grads[1, :64], grads[0, 64:], grads[1, 64:]], 0)
        return block.astype(F32)

    block1, block2 = own_block(grads1), own_block(grads2)
    qkv_total = block1[:, :, :384].reshape(192, 2, 2, 2, HS)
    qkv_total = qkv_total.transpose(0, 3, 1, 2, 4).reshape(192, 768)
    out_total = block1[:, :, 448:640].reshape(192, 2, 2, HS).transpose(2, 1, 3, 0).reshape(384, 192)
    gate_up_total = jnp.stack(
        [block2[:, :, :512].reshape(192, 1024), block2[:, :, 512:1024].reshape(192, 1024)], 1
    )
    down_total = block2[:, :, 1024:].reshape(192, 1024).T
    gains_rest = jnp.where(odd, gains_tile[:2, 192:256], gains_tile[:2, 128:192])
    gains_total = jnp.concatenate([gains_tile[:2, :128], gains_rest], 1)

    rate_qkv, rate_out, rate_gate_up, rate_down, rate_gains = step_rates()
    qkv_new = adamw_update(qkv_weight, qkv_first, qkv_second, qkv_total, rate_qkv, weight_decay)
    out_new = adamw_update(out_weight, out_first, out_second, out_total, rate_out, weight_decay)
    gate_up_new = adamw_update(
        gate_up_weight, gate_up_first, gate_up_second, gate_up_total, rate_gate_up, weight_decay
    )
    down_new = adamw_update(
        down_weight, down_first, down_second, down_total, rate_down, weight_decay
    )
    gains_new = adamw_update(gains, gains_first, gains_second, gains_total, rate_gains, 0.0)
    return (output, stream_grad, *qkv_new, *out_new, *gate_up_new, *down_new, *gains_new)


def solution(mesh):
    tokens = P("col", "dp", "row")
    table = P("dp", None)
    wide, tall, pairs, both = P("row", "col"), P("col", "row"), P("row", None, "col"), P(None, "row")
    weights = (wide,) * 3 + (tall,) * 3 + (pairs,) * 3 + (tall,) * 3 + (both,) * 3
    return jax.shard_map(
        body,
        mesh=mesh,
        in_specs=(tokens, tokens, table, table, *weights),
        out_specs=(tokens, tokens, *weights),
        check_vma=False,
    )
```

```python
import functools

import jax
import jax.numpy as jnp
from jax import lax
from jax.experimental import pallas as pl
from jax.experimental.pallas import tpu as pltpu
from jax.sharding import PartitionSpec as P

D = 1536
FF = 4096
HQ = 16
KVH = 8
HS = 96
STEP = 10
LEN = 2048
WINDOW = 1024

norm_epsilon = 1e-05
rope_theta = 100000.0
beta_first = 0.9
beta_second = 0.95
adam_epsilon = 1e-08
weight_decay = 0.1
score_scale = HS**-0.5

MESH = pl.DeviceIdType.MESH
BF = jnp.bfloat16
F32 = jnp.float32
VM = pl.BlockSpec(memory_space=pltpu.VMEM)
ANY = pl.BlockSpec(memory_space=pl.ANY)


class Place:
    def __init__(self):
        self.dp = lax.axis_index("dp")
        self.row = lax.axis_index("row")
        self.x = lax.axis_index("col")
        self.zh = lax.div(self.dp, 2)
        self.core = lax.rem(self.dp, 2)
        self.y = lax.div(self.row, 2)
        self.zl = lax.rem(self.row, 2)
        self.z = self.zh * 2 + self.zl

    def at(self, dx=0, dy=0, dz=0, dcore=0):
        x = lax.rem(self.x + (dx + 4), 4)
        y = lax.rem(self.y + (dy + 4), 4)
        z = lax.rem(self.z + (dz + 4), 4)
        core = lax.rem(self.core + dcore, 2)
        return (lax.div(z, 2) * 2 + core, y * 2 + lax.rem(z, 2), x)

    def pair(self):
        return self.at(dcore=1)

    def in_row(self, step):
        return (self.dp, lax.rem(self.row + step, 8), self.x)

    def in_dp(self, step):
        return (lax.rem(self.dp + step, 4), self.row, self.x)


def greet(devices):
    barrier = pltpu.get_barrier_semaphore()
    for device in devices:
        pl.semaphore_signal(barrier, inc=1, device_id=device, device_id_type=MESH)
    pl.semaphore_wait(barrier, len(devices))


class Wire:
    def __init__(self, send, recv, local=None):
        self.send, self.recv, self.local = send, recv, local
        self.sent, self.open, self.near, self.stays = [], {}, [], 0

    def copy(self, src, dst, device):
        n = len(self.sent)
        made = pltpu.make_async_remote_copy(
            src_ref=src,
            dst_ref=dst,
            send_sem=self.send.at[n],
            recv_sem=self.recv.at[n],
            device_id=device,
            device_id_type=MESH,
        )
        made.start()
        self.sent.append(made)
        self.open[n] = made
        return n

    def arrive(self, *numbers):
        for n in numbers:
            self.open.pop(n).wait_recv()

    def stay(self, src, dst):
        made = pltpu.make_async_copy(src, dst, self.local.at[self.stays])
        self.stays += 1
        made.start()
        self.near.append(made)
        return made

    def there(self, *stays):
        for made in stays:
            self.near = [other for other in self.near if other is not made]
            made.wait()

    def settle(self):
        self.arrive(*list(self.open))

    def finish(self):
        self.settle()
        for made in self.sent:
            made.wait_send()
        self.there(*list(self.near))


def around(me):
    return lax.rem(me + 3, 4), lax.rem(me + 1, 4), lax.rem(me + 2, 4)


def as_list(refs):
    return refs if isinstance(refs, list) else [refs]


def ring_gather(wire, me, right, left, own, slot, on_block=None):
    l, r, o = around(me)

    def send(src, dst, device):
        return [wire.copy(a, b, device) for a, b in zip(as_list(src), as_list(dst))]

    first = send(own(0), slot(me, 0), right), send(own(1), slot(me, 1), left)
    second = send(own(1), slot(me, 1), right), send(own(0), slot(me, 0), left)
    yield
    wire.arrive(*first[0])
    far0 = send(slot(l, 0), slot(l, 0), right)
    wire.arrive(*first[1])
    far1 = send(slot(r, 1), slot(r, 1), left)
    yield
    wire.arrive(*second[0])
    if on_block:
        on_block(l)
    wire.arrive(*second[1])
    if on_block:
        on_block(r)
    yield
    wire.arrive(*far0, *far1)
    if on_block:
        on_block(o)


def leading(ref):
    found = [()]
    for size in ref.shape[:-2]:
        found = [index + (n,) for index in found for n in range(size)]
    return found


def add_parts(out, refs):
    for index in leading(out):
        at = index + (slice(None), slice(None))
        total = refs[0][at].astype(F32)
        for ref in refs[1:]:
            total = total + ref[at].astype(F32)
        out[at] = total.astype(out.dtype)


def ring_sum(wire, me, right, left, part, far, near, out):
    l, r, o = around(me)

    def send(srcs, dsts, device):
        return [wire.copy(a, b, device) for a, b in zip(srcs, dsts)]

    far0 = send(part(o, 0), far(0), right)
    far1 = send(part(o, 1), far(1), left)
    to_right = send(part(r, 1), near(0, 1), right)
    to_left = send(part(l, 0), near(1, 0), left)
    yield
    wire.arrive(*far0)
    for a, b in zip(far(0), part(r, 0)):
        add_parts(a, [a, b])
    to_right += send(far(0), near(0, 0), right)
    wire.arrive(*far1)
    for a, b in zip(far(1), part(l, 1)):
        add_parts(a, [a, b])
    to_left += send(far(1), near(1, 1), left)
    yield
    wire.arrive(*to_right, *to_left)
    for h in range(2):
        for a, b, c, total in zip(part(me, h), near(0, h), near(1, h), out(h)):
            add_parts(total, [a, b, c])


def side_by_side(*flows):
    flows = list(flows)
    while flows:
        for flow in list(flows):
            try:
                next(flow)
            except StopIteration:
                flows.remove(flow)


def rows(ref, start, size, multiple):
    return ref.at[pl.ds(pl.multiple_of(start, multiple), size)]


def weight_gather(wire, here, own, whole):
    core, zl = here.core, here.zl
    right, left = here.at(dy=1), here.at(dy=-1)
    up, down = here.at(dz=1), here.at(dz=-1)
    l, r, o = around(here.y)

    def mine(j):
        start = (core * 64, core * 64 + 32, 128 + core * 32, 144 + core * 32)[j]
        return rows(own, start, (32, 32, 16, 16)[j], 16)

    def piece(y, j, lo):
        block = y * 2 + lo
        main, rest = block * 128 + core * 64, 1024 + block * 64 + core * 32
        start = (main, main + 32, rest, rest + 16)[j]
        return rows(whole, start, (32, 32, 16, 16)[j], 16)

    def to_pair(y, lo):
        block = y * 2 + lo
        for view in (
            rows(whole, block * 128 + core * 64, 64, 64),
            rows(whole, 1024 + block * 64 + core * 32, 32, 32),
        ):
            wire.copy(view, view, here.pair())

    def over(y, js, device, src=None):
        return [wire.copy((src or (lambda j: piece(y, j, zl)))(j), piece(y, j, zl), device) for j in js]

    y = here.y
    kept = (
        wire.stay(own.at[pl.ds(0, 128)], rows(whole, here.row * 128, 128, 128)),
        wire.stay(own.at[pl.ds(128, 64)], rows(whole, 1024 + here.row * 64, 64, 64)),
    )
    r_first, l_first = over(y, (0, 2), right, mine), over(y, (1, 3), left, mine)
    r_next, l_next = over(y, (1, 3), right, mine), over(y, (0, 2), left, mine)
    z_own = over(y, (0, 2), up, mine) + over(y, (1, 3), down, mine)
    yield
    wire.arrive(*r_first)
    far = over(l, (0, 2), right)
    wire.arrive(*l_first)
    far += over(r, (1, 3), left)
    z_l = over(l, (0, 2), up)
    z_r = over(r, (1, 3), down)
    yield
    wire.arrive(*r_next)
    z_l += over(l, (1, 3), down)
    to_pair(l, zl)
    wire.arrive(*l_next)
    z_r += over(r, (0, 2), up)
    to_pair(r, zl)
    yield
    wire.arrive(*far)
    z_o = over(o, (0, 2), up) + over(o, (1, 3), down)
    to_pair(o, zl)
    yield
    for block, numbers in ((y, z_own), (l, z_l), (r, z_r), (o, z_o)):
        wire.arrive(*numbers)
        to_pair(block, 1 - zl)
        yield
    wire.there(*kept)


def share(wire, here, out):
    half = lambda i, h: out.at[i, pl.ds(64 * h, 64)]

    def to_pair(i):
        wire.copy(out.at[i], out.at[i + 4], here.pair())

    to_pair(here.x)
    yield from ring_gather(
        wire,
        here.x,
        here.at(dx=1),
        here.at(dx=-1),
        lambda h: half(here.x, h),
        half,
        to_pair,
    )


def x_sum(wire, here, part, far, near, out):
    return ring_sum(
        wire,
        here.x,
        here.at(dx=1),
        here.at(dx=-1),
        lambda i, h: [part.at[i, pl.ds(64 * h, 64)]],
        lambda h: [far.at[h]],
        lambda s, h: [near.at[s, pl.ds(64 * h, 64)]],
        lambda h: [out.at[pl.ds(64 * h, 64)]],
    )


def x_sum_scratch():
    return [pltpu.VMEM((2, 64, D), BF), pltpu.VMEM((2, 128, D), BF)]


HIGHS = (64, 32)


def grad_scratch(width, cut):
    shapes = []
    for columns in (cut, width - cut):
        for high in HIGHS:
            shapes += [
                pltpu.VMEM((2, 2, high, columns), BF),
                pltpu.VMEM((2, 2, 2, high, columns), BF),
                pltpu.VMEM((2, 2, high, columns), BF),
                pltpu.VMEM((2, high // 2, columns), BF),
                pltpu.VMEM((2, 2, high // 2, columns), BF),
            ]
    return shapes + [pltpu.VMEM((96, width), BF)]


def grad_flows(wire, here, grads, scratch, width, cut):
    fin = scratch[-1]
    ends = (0, 64, 96)

    def flow(order, buffers):
        columns = pl.ds(0, cut) if order == 0 else pl.ds(cut, width - cut)
        y_ring = (here.y, here.at(dy=1), here.at(dy=-1))
        z_ring = (here.z, here.at(dz=1), here.at(dz=-1))

        def of_z(ref, i, h):
            return ref.at[pl.ds(2 * h, 2), lax.rem(i, 2), lax.div(i, 2), :, columns]

        def of_y(ref, i, h):
            return ref.at[i, h, :, :, columns]

        far = lambda h: [b[0].at[h] for b in buffers]
        near = lambda s, h: [b[1].at[s, h] for b in buffers]
        mid = lambda h: [b[2].at[h] for b in buffers]
        first, second = (z_ring, y_ring) if order == 0 else (y_ring, z_ring)
        pick = of_z if order == 0 else of_y
        yield from ring_sum(
            wire, *first, lambda i, h: [pick(g, i, h) for g in grads], far, near,
            lambda h: [b[2].at[h] for b in buffers],
        )
        yield

        def part(i, h):
            lead = (lax.div(i, 2), lax.rem(i, 2)) if order == 0 else (lax.rem(i, 2), lax.div(i, 2))
            return [
                b[2].at[lead[0], lead[1], pl.ds(high // 2 * h, high // 2)]
                for b, high in zip(buffers, HIGHS)
            ]

        yield from ring_sum(
            wire, *second, part,
            lambda h: [b[3].at[h] for b in buffers],
            lambda s, h: [b[4].at[s, h] for b in buffers],
            lambda h: [
                fin.at[pl.ds(start + high // 2 * h, high // 2), columns]
                for start, high in zip(ends, HIGHS)
            ],
        )

    buffers = [scratch[5 * n : 5 * n + 5] for n in range(4)]
    return flow(0, buffers[:2]), flow(1, buffers[2:])


def grad_share(wire, here, fin, out, width):
    columns = pl.ds(pl.multiple_of(here.core * width, 128), width)
    mine = out.at[here.zh, :, columns]
    other = out.at[1 - here.zh, :, columns]
    wire.stay(fin, mine)
    wire.copy(fin, mine, here.pair())
    n = wire.copy(fin, mine, here.at(dz=2))
    yield
    wire.arrive(n)
    wire.copy(other, other, here.pair())


def swap_rows(wire, here, src, dst):
    return [
        wire.copy(src.at[lax.rem(here.row + s, 8)], dst.at[here.row], here.in_row(s))
        for s in range(1, 8)
    ]


def widened(ref, start, size):
    at = pl.ds(start, size)
    main = [ref[r, at, 0:128] for r in range(8)]
    rest = [ref[2 * j, at, 128:256] + ref[2 * j + 1, at, 128:256] for j in range(4)]
    return jnp.concatenate(main + rest, axis=1)


def narrowed(out, value):
    for r in range(8):
        out[r, :, 0:128] = value[:, 128 * r : 128 * r + 128]
        j = 1024 + 128 * (r // 2)
        out[r, :, 128:256] = value[:, j : j + 128]


def ring_partners(here):
    return [here.at(dx=1), here.at(dx=-1)]


def plane_partners(here):
    return [here.at(dy=1), here.at(dy=-1), here.at(dz=1), here.at(dz=-1)]


def dot(a, b, left=1, right=0):
    return lax.dot_general(a, b, (((left,), (right,)), ((), ())), preferred_element_type=F32)


def turned(values, cosine, sine):
    lane = lax.broadcasted_iota(jnp.int32, values.shape, 1)
    front = lax.rem(lane, HS) < HS // 2
    ahead, back = pltpu.roll(values, 256 - HS // 2, 1), pltpu.roll(values, HS // 2, 1)
    return values * cosine + jnp.where(front, -ahead, back) * sine


def packed_pair(a, b):
    return jnp.concatenate([a[:, :128], a[:, 128:] + b[:, :128], b[:, 128:]], axis=1)


def windows(y):
    return ((0, 4), (0, 8), (1 + y, 8), (5 + y, 8))


def allowed_keys(table, c, start, count):
    key = start * 128 + lax.broadcasted_iota(jnp.int32, (count * 128, 256), 0)
    return (key >= table[2 * c : 2 * c + 1]) & (key <= table[2 * c + 1 : 2 * c + 2])


def both_heads(ref, at):
    return jnp.concatenate([ref[at, 0:256], ref[at, 256:512]], axis=0)


def attend(here, q, kv, table, heads, log_total):
    lane = lax.broadcasted_iota(jnp.int32, (256, 256), 1)
    for c, (start, count) in enumerate(windows(here.y)):
        at = pl.ds(128 * c, 128)
        allowed = allowed_keys(table, c, start, count)
        q_both = both_heads(q, at)
        k = kv[pl.ds(start, count), :, 0:256].reshape(count * 128, 256)
        v = kv[pl.ds(start, count), :, 128:384].reshape(count * 128, 256)
        made = []
        for g in range(2):
            n = 2 * c + g
            q_one = jnp.where((lane >= HS) == (g == 1), q_both, jnp.zeros_like(q_both))
            scores = dot(k, q_one, 1, 1) * score_scale
            scores = jnp.where(allowed, scores, -1e30)
            top = jnp.max(scores, axis=0, keepdims=True)
            weights = jnp.exp(scores - top)
            total = jnp.sum(weights, axis=0, keepdims=True)
            shares = (weights * (1.0 / total)).astype(BF)
            made.append(dot(shares, v, 0, 0))
            log_total[n : n + 1] = top + jnp.log(total)
        out = jnp.where(lane < 64 + HS, made[0], made[1])
        out = jnp.where(lane < 64, 0.0, out).astype(BF)
        heads[at, 0:256] = out[:128]
        heads[at, 256:512] = out[128:]


def attend_back(here, q, kv, table, log_total, dout, dq, total):
    lane = lax.broadcasted_iota(jnp.int32, (256, 256), 1)
    total[...] = jnp.zeros_like(total)
    for c, (start, count) in enumerate(windows(here.y)):
        at = pl.ds(128 * c, 128)
        blocks = pl.ds(start, count)
        allowed = allowed_keys(table, c, start, count)
        q_both, d_both = both_heads(q, at), both_heads(dout, at)
        k = kv[blocks, :, 0:256].reshape(count * 128, 256)
        v = kv[blocks, :, 128:384].reshape(count * 128, 256)
        made = []
        for g in range(2):
            n = 2 * c + g
            q_one = jnp.where((lane >= HS) == (g == 1), q_both, jnp.zeros_like(q_both))
            d_one = jnp.where((lane >= 64 + HS) == (g == 1), d_both, jnp.zeros_like(d_both))
            scores = dot(k, q_one, 1, 1) * score_scale
            shares = jnp.where(allowed, jnp.exp(scores - log_total[n : n + 1]), 0.0)
            dshares = dot(v, d_one, 1, 1)
            inner = jnp.sum(shares * dshares, axis=0, keepdims=True)
            dscores = (shares * (dshares - inner)).astype(BF)
            made.append(dot(dscores, k, 0, 0))
            dk = dot(dscores, q_one) * score_scale
            dv = dot(shares.astype(BF), d_one)
            total[blocks, :, 0:256] += dk.reshape(count, 128, 256)
            total[blocks, :, 128:384] += dv.reshape(count, 128, 256)
        out = jnp.where(lane < HS, made[0], made[1]) * score_scale
        dq[at, 0:256] = out[:128]
        dq[at, 256:512] = out[128:]


def tokens_of(ref, pair=0):
    return ref[4 * pair : 4 * pair + 4].reshape(512, D)


def columns(n, size=256):
    return pl.ds(pl.multiple_of(n * size, size), size)


def back_to_width(units, at, weights, weight_at, out):
    @pl.loop(0, D // 256)
    def _(n):
        made = dot(units[:, at], weights[columns(n), weight_at], 1, 1)
        out[:, :, columns(n)] = made.astype(BF).reshape(4, 128, 256)


def weight_grads(tokens, own, pair, main, rest, at):
    def made(n):
        total = dot(tokens[0:4, :, columns(n)].reshape(512, 256), own[0][:, own[1]], 0, 0)
        return total + dot(tokens[4:8, :, columns(n)].reshape(512, 256), pair[0][:, pair[1]], 0, 0)

    @pl.loop(0, 4)
    def _(n):
        value = made(n)
        main[n, :, :, :, at] = value.astype(BF).reshape(2, 2, 64, value.shape[1])

    @pl.loop(0, 2)
    def _(n):
        value = made(n + 4)
        rest[pl.ds(2 * n, 2), :, :, :, at] = value.astype(BF).reshape(2, 2, 2, 32, value.shape[1])


def norm_back(value, grad, gain):
    scale = lax.rsqrt(jnp.mean(value * value, axis=1, keepdims=True) + norm_epsilon)
    unit = value * scale
    scaled = grad * gain
    inner = jnp.mean(scaled * unit, axis=1, keepdims=True)
    return scale * (scaled - unit * inner), jnp.sum(grad * unit, axis=0, keepdims=True)


def normed(value, gain):
    scale = lax.rsqrt(jnp.mean(value * value, axis=1, keepdims=True) + norm_epsilon)
    return (value * scale * gain).astype(BF)


def key_block(c, y):
    return 4 * c + y


def enter_kernel(
    xin, cin, win, place, frequency, table,
    part, h1_out, w_out, c_out, kv_out, q, heads, log_total, cosine, sine, xtok, ctok, gtok,
    xbuf, cbuf, h1_all, c_all, w_all, kv_own, kv_all, qkv, send, recv, local,
):
    here = Place()
    wire = Wire(send, recv, local)
    greet(
        [here.in_row(s) for s in range(1, 8)]
        + ring_partners(here)
        + [here.at(dz=1), here.at(dz=-1), here.pair()]
    )
    xs = swap_rows(wire, here, xin, xbuf)
    weights = weight_gather(wire, here, win, w_all)
    next(weights)
    cs = swap_rows(wire, here, cin, cbuf)
    xbuf[here.row] = xin[here.row]
    cbuf[here.row] = cin[here.row]
    lane = lax.broadcasted_iota(jnp.int32, (512, 256), 1)
    angles = place[...] * frequency[0:1]
    cosine[...] = jnp.where(lane < 2 * HS, jnp.cos(angles), 0.0)
    sine[...] = jnp.where(lane < 2 * HS, jnp.sin(angles), 0.0)

    wire.arrive(*xs)
    x = widened(xbuf, 0, 128)
    xtok[...] = x
    g = widened(xbuf, 128, 16).astype(F32)
    gains = g[0:2] + g[2:4]
    gtok[...] = gains
    h1_all[here.x] = normed(x.astype(F32), gains[0:1])
    side_by_side(share(wire, here, h1_all), weights)
    wire.settle()
    c_value = widened(cbuf, 0, 128)
    ctok[...] = c_value
    c_all[here.x] = c_value
    cs_flow = share(wire, here, c_all)
    next(cs_flow)
    wire.stay(h1_all, h1_out)
    wire.stay(w_all, w_out)

    @pl.loop(0, 3)
    def _(n):
        qkv[:, columns(n)] = dot(tokens_of(h1_all), w_all[:, columns(n)])

    lane = lax.broadcasted_iota(jnp.int32, (128, 256), 1)
    for c in range(4):
        at = pl.ds(128 * c, 128)
        turn = cosine[at], sine[at]
        key = turned(qkv[at, 384:640], *turn)
        value = jnp.where(lane < 64, 0.0, qkv[at, 512:768])
        kv = packed_pair(key, value).astype(BF)
        kv_own[c] = kv
        kv_all[key_block(c, here.y)] = kv

    def halves(ref_at):
        return lambda h: [ref_at(2 * h), ref_at(2 * h + 1)]

    slot = lambda i, h: [kv_all.at[key_block(2 * h + n, i)] for n in range(2)]
    keys = ring_gather(
        wire, here.y, here.at(dy=1), here.at(dy=-1), halves(lambda c: kv_own.at[c]), slot
    )
    next(keys)
    for c in range(4):
        at = pl.ds(128 * c, 128)
        turn = cosine[at], sine[at]
        q[at, 0:256] = turned(qkv[at, 0:256], *turn).astype(BF)
        second = pltpu.roll(qkv[at, 128:384], 192, 1)
        q[at, 256:512] = turned(second, *turn).astype(BF)
    side_by_side(cs_flow, keys)
    attend(here, q, kv_all, table, heads, log_total)
    back_to_width(heads, slice(None), w_all, slice(768, 1280), part)
    wire.settle()
    wire.stay(kv_all, kv_out)
    wire.stay(c_all, c_out)
    wire.finish()


def shape(dtype, *sizes):
    return jax.ShapeDtypeStruct(sizes, dtype)


def signals(*counts):
    return [pltpu.SemaphoreType.DMA((n,)) for n in counts]


def settings(number):
    return pltpu.CompilerParams(
        collective_id=number, has_side_effects=True, vmem_limit_bytes=60 << 20
    )


def enter(xin, cin, win, place, frequency, table):
    return pl.pallas_call(
        enter_kernel,
        out_shape=[
            shape(BF, 4, 128, D),
            shape(BF, 8, 128, D),
            shape(BF, D, 1280),
            shape(BF, 8, 128, D),
            shape(BF, 16, 128, 384),
            shape(BF, 512, 512),
            shape(BF, 512, 512),
            shape(F32, 8, 256),
            shape(F32, 512, 256),
            shape(F32, 512, 256),
            shape(BF, 128, D),
            shape(BF, 128, D),
            shape(F32, 2, D),
        ],
        in_specs=[VM, VM, ANY, VM, VM, VM],
        out_specs=[VM] + [ANY] * 4 + [VM] * 8,
        scratch_shapes=[
            pltpu.VMEM((8, 144, 256), BF),
            pltpu.VMEM((8, 128, 256), BF),
            pltpu.VMEM((8, 128, D), BF),
            pltpu.VMEM((8, 128, D), BF),
            pltpu.VMEM((D, 1280), BF),
            pltpu.VMEM((4, 128, 384), BF),
            pltpu.VMEM((16, 128, 384), BF),
            pltpu.VMEM((512, 768), F32),
        ]
        + signals(104, 104, 8),
        compiler_params=settings(1),
        name="enter",
    )(xin, cin, win, place, frequency, table)


def feed_kernel(width, cut, *refs):
    part, xtok, gtok, ctok, win, c_in = refs[:6]
    after, gain, rise, f_part, d_out, gout = refs[6:12]
    far, near, far2, near2, middle, summed, h2_all, c_all, w_all, units, others, part2 = refs[12:24]
    main, rest, d_all = refs[24:27]
    scratch, (send, recv, local) = refs[27:-3], refs[-3:]
    here = Place()
    wire = Wire(send, recv, local)
    greet(ring_partners(here) + plane_partners(here) + [here.at(dz=2), here.pair()])
    c_copy = wire.stay(c_in, c_all)

    def forward():
        yield from x_sum(wire, here, part, far, near, rise)
        value = rise[...] + xtok[...].astype(F32)
        middle[...] = value
        h2_all[here.x] = normed(value, gtok[1:2])
        yield from share(wire, here, h2_all)

    side_by_side(forward(), weight_gather(wire, here, win, w_all))
    wire.settle()
    wire.there(c_copy)

    def unit_tiles(first):
        @pl.loop(0, 2)
        def _(n):
            j = first * 2 + n
            gate = dot(tokens_of(h2_all), w_all[:, columns(j)])
            up = dot(tokens_of(h2_all), w_all[:, columns(j + 4)])
            dact = dot(tokens_of(c_all), w_all[:, columns(j + 8)])
            sigmoid = 1.0 / (1.0 + jnp.exp(-gate))
            silu = gate * sigmoid
            units[:, columns(j)] = (dact * up * sigmoid * (1.0 + gate * (1.0 - sigmoid))).astype(BF)
            units[:, columns(j + 4)] = (dact * silu).astype(BF)
            units[:, columns(j + 8)] = (silu * up).astype(BF)

    unit_tiles(1 - here.core)
    swaps = [
        wire.copy(
            units.at[:, columns(1 - here.core + 2 * n, 512)],
            others.at[:, pl.ds(512 * n, 512)],
            here.pair(),
        )
        for n in range(3)
    ]
    unit_tiles(here.core)
    back_to_width(units, slice(0, 2048), w_all, slice(0, 2048), part2)

    def backward():
        yield from x_sum(wire, here, part2, far2, near2, summed)
        left, gain_terms = norm_back(middle[...], summed[...], gtok[1:2])
        gain[...] = jnp.broadcast_to(gain_terms, gain.shape)
        after[...] = left
        d_all[here.x] = (left + ctok[...].astype(F32)).astype(BF)
        yield from share(wire, here, d_all)

    chain = backward()
    next(chain)
    back_to_width(units, slice(2048, 3072), w_all, slice(2048, 3072), f_part)
    next(chain)
    wire.arrive(*swaps)
    for n, tokens in enumerate((h2_all, h2_all, c_all)):
        at = pl.ds(512 * n, 512)
        weight_grads(
            tokens, (units, columns(here.core + 2 * n, 512)), (others, at), main, rest, at
        )
    zy, yz = grad_flows(wire, here, (main, rest), scratch, width, cut)
    side_by_side(chain, zy, yz)
    wire.stay(d_all.at[pl.ds(0, 4)], d_out.at[pl.ds(0, 4)])
    side_by_side(grad_share(wire, here, scratch[-1], gout, width))
    wire.settle()
    wire.stay(d_all.at[pl.ds(4, 4)], d_out.at[pl.ds(4, 4)])
    wire.finish()


def grad_arrays(width):
    return [pltpu.VMEM((4, 2, 2, high, width), BF) for high in HIGHS]


def feed(part, xtok, gtok, ctok, win, c_in):
    width, cut = 1536, 768
    return pl.pallas_call(
        functools.partial(feed_kernel, width, cut),
        out_shape=[
            shape(F32, 128, D),
            shape(F32, 8, D),
            shape(F32, 128, D),
            shape(BF, 4, 128, D),
            shape(BF, 8, 128, D),
            shape(BF, 2, 96, 2 * width),
        ],
        in_specs=[VM, VM, VM, VM, ANY, ANY],
        out_specs=[VM] * 4 + [ANY] * 2,
        scratch_shapes=x_sum_scratch()
        + x_sum_scratch()
        + [
            pltpu.VMEM((128, D), F32),
            pltpu.VMEM((128, D), F32),
            pltpu.VMEM((8, 128, D), BF),
            pltpu.VMEM((8, 128, D), BF),
            pltpu.VMEM((D, 3072), BF),
            pltpu.VMEM((512, 3072), BF),
            pltpu.VMEM((512, 1536), BF),
            pltpu.VMEM((4, 128, D), BF),
        ]
        + grad_arrays(width)
        + [pltpu.VMEM((8, 128, D), BF)]
        + grad_scratch(width, cut)
        + signals(144, 144, 8),
        compiler_params=settings(2),
        name="feed",
    )(part, xtok, gtok, ctok, win, c_in)


def leave_kernel(width, cut, *refs):
    f_part, rise, xtok, after, gtok, gain, q, heads, log_total, table, cosine, sine = refs[:12]
    d_in, w_in, kv_in, h1_in = refs[12:16]
    o_all, s_all, gout, gains_out = refs[16:20]
    d_all, w_all, kv_all, h1_all, dout, dq, total, dkv, kfar, knear, dkv_own, dqkv = refs[20:32]
    heads_in, dqkv_in, part, far, near, far2, near2, summed, osend, ssend = refs[32:42]
    gsend, grow, gcol, gdp, main, rest = refs[42:48]
    scratch, (send, recv, local) = refs[48:-3], refs[-3:]
    here = Place()
    wire = Wire(send, recv, local)
    d_copy, w_copy = wire.stay(d_in, d_all), wire.stay(w_in, w_all)
    kv_copy, h1_copy = wire.stay(kv_in, kv_all), wire.stay(h1_in, h1_all)
    greet(
        [here.in_row(s) for s in range(1, 8)]
        + ring_partners(here)
        + [here.at(dz=1), here.at(dz=-1), here.at(dx=2)]
        + [here.in_dp(s) for s in range(1, 4)]
    )
    branch_sum = x_sum(wire, here, f_part, far, near, summed)
    next(branch_sum)
    heads_swap = wire.copy(heads.at[:, columns(1 - here.core)], heads_in, here.pair())
    wire.there(d_copy, w_copy)

    @pl.loop(0, 2)
    def _(n):
        dout[:, columns(n)] = dot(tokens_of(d_all), w_all[:, columns(n + 3)]).astype(BF)

    next(branch_sum)
    wire.there(kv_copy)
    attend_back(here, q, kv_all, table, log_total, dout, dq, total)
    dkv[...] = total[...].astype(BF)
    pick = lambda h, i: [dkv.at[key_block(2 * h + n, i)] for n in range(2)]
    keys = ring_sum(
        wire,
        here.y,
        here.at(dy=1),
        here.at(dy=-1),
        lambda i, h: pick(h, i),
        lambda h: [kfar.at[h, n] for n in range(2)],
        lambda s, h: [knear.at[s, h, n] for n in range(2)],
        lambda h: [dkv_own.at[pl.ds(128 * (2 * h + n), 128)] for n in range(2)],
    )
    next(keys)
    side_by_side(branch_sum)
    narrowed(osend, (summed[...] + rise[...]).astype(BF))
    for c in range(4):
        at = pl.ds(128 * c, 128)
        turn = cosine[at], -sine[at]
        second = turned(dq[at, 256:512], *turn)
        both = packed_pair(turned(dq[at, 0:256], *turn), pltpu.roll(second, 64, 1))
        dqkv[at, 0:384] = both.astype(BF)
    next(keys)
    wire.arrive(heads_swap)
    weight_grads(
        d_all, (heads, columns(here.core)), (heads_in, slice(None)), main, rest, slice(384, 640)
    )
    side_by_side(keys)
    lane = lax.broadcasted_iota(jnp.int32, (128, 256), 1)
    for c in range(4):
        at = pl.ds(128 * c, 128)
        key = turned(dkv_own[at, 0:256], cosine[at], -sine[at])
        value = jnp.where(lane < 64, 0.0, dkv_own[at, 128:384])
        dqkv[at, 384:768] = packed_pair(key, value).astype(BF)
    dqkv_swap = wire.copy(dqkv.at[:, columns(1 - here.core, 384)], dqkv_in, here.pair())
    back_to_width(dqkv, slice(None), w_all, slice(0, 768), part)

    def chain():
        yield from x_sum(wire, here, part, far2, near2, summed)
        left, gain_terms = norm_back(xtok[...].astype(F32), summed[...], gtok[0:1])
        gains = jnp.concatenate([gain_terms, gain[0:1], jnp.zeros((6, D), F32)], axis=0)
        narrowed(gsend, gains)
        g = swap_rows(wire, here, gsend, grow)
        narrowed(ssend, (left + after[...]).astype(BF))
        wire.stay(ssend.at[here.row], s_all.at[here.row])
        swap_rows(wire, here, ssend, s_all)
        yield
        wire.arrive(*g)
        grow[here.row] = gsend[here.row]
        total = grow[0]
        for n in range(1, 8):
            total = total + grow[n]
        gcol[here.x] = total
        g = [wire.copy(gcol.at[here.x], gcol.at[here.x], here.at(dx=s)) for s in range(1, 4)]
        yield
        wire.arrive(*g)
        gdp[here.dp] = ((gcol[0] + gcol[1]) + gcol[2]) + gcol[3]
        g = [wire.copy(gdp.at[here.dp], gdp.at[here.dp], here.in_dp(s)) for s in range(1, 4)]
        yield
        wire.arrive(*g)
        gains_out[...] = ((gdp[0] + gdp[1]) + gdp[2]) + gdp[3]

    steps = chain()
    next(steps)
    wire.stay(osend.at[here.row], o_all.at[here.row])
    swap_rows(wire, here, osend, o_all)
    wire.there(h1_copy)
    wire.arrive(dqkv_swap)
    weight_grads(
        h1_all, (dqkv, columns(here.core, 384)), (dqkv_in, slice(None)), main, rest, slice(0, 384)
    )
    zy, yz = grad_flows(wire, here, (main, rest), scratch, width, cut)
    next(zy)
    next(yz)
    side_by_side(steps, zy, yz)
    side_by_side(grad_share(wire, here, scratch[-1], gout, width))
    wire.finish()


def leave(*operands):
    width, cut = 640, 256
    return pl.pallas_call(
        functools.partial(leave_kernel, width, cut),
        out_shape=[
            shape(BF, 8, 128, 256),
            shape(BF, 8, 128, 256),
            shape(BF, 2, 96, 2 * width),
            shape(F32, 8, 256),
        ],
        in_specs=[VM] * 12 + [ANY] * 4,
        out_specs=[ANY, ANY, ANY, VM],
        scratch_shapes=[
            pltpu.VMEM((8, 128, D), BF),
            pltpu.VMEM((D, 1280), BF),
            pltpu.VMEM((16, 128, 384), BF),
            pltpu.VMEM((8, 128, D), BF),
            pltpu.VMEM((512, 512), BF),
            pltpu.VMEM((512, 512), F32),
            pltpu.VMEM((16, 128, 384), F32),
            pltpu.VMEM((16, 128, 384), BF),
            pltpu.VMEM((2, 2, 128, 384), BF),
            pltpu.VMEM((2, 2, 2, 128, 384), BF),
            pltpu.VMEM((512, 384), F32),
            pltpu.VMEM((512, 768), BF),
            pltpu.VMEM((512, 256), BF),
            pltpu.VMEM((512, 384), BF),
            pltpu.VMEM((4, 128, D), BF),
        ]
        + x_sum_scratch()
        + x_sum_scratch()
        + [
            pltpu.VMEM((128, D), F32),
            pltpu.VMEM((8, 128, 256), BF),
            pltpu.VMEM((8, 128, 256), BF),
            pltpu.VMEM((8, 8, 256), F32),
            pltpu.VMEM((8, 8, 256), F32),
            pltpu.VMEM((4, 8, 256), F32),
            pltpu.VMEM((4, 8, 256), F32),
        ]
        + grad_arrays(width)
        + grad_scratch(width, cut)
        + signals(128, 128, 8),
        compiler_params=settings(3),
        name="leave",
    )(*operands)


def adamw_update(weight, moment_one, moment_two, gradient, step_rate, decay_rate):
    moment_one = beta_first * moment_one + (1.0 - beta_first) * gradient
    moment_two = beta_second * moment_two + (1.0 - beta_second) * gradient * gradient
    corrected = (
        moment_one
        / (1.0 - beta_first**STEP)
        / (jnp.sqrt(moment_two / (1.0 - beta_second**STEP)) + adam_epsilon)
    )
    return (moment_one, moment_two, weight - step_rate * (corrected + decay_rate * weight))


def step_rates():
    return (2.0 / D**0.5, 2.0 / max(HQ * HS // 64, 1) ** 0.5, 2.0 / D**0.5, 2.0 / FF**0.5, 0.4)


def body(
    stream,
    cotangent,
    segments,
    positions,
    qkv_weight,
    qkv_first,
    qkv_second,
    out_weight,
    out_first,
    out_second,
    gate_up_weight,
    gate_up_first,
    gate_up_second,
    down_weight,
    down_first,
    down_second,
    gains,
    gains_first,
    gains_second,
):
    row = lax.axis_index("row")
    zl, y = row % 2, row // 2
    odd = zl == 1

    def packed(values):
        main, rest = values[..., :128], values[..., 128:]
        none = jnp.zeros_like(rest)
        tile = jnp.where(
            odd, jnp.concatenate([none, rest], -1), jnp.concatenate([rest, none], -1)
        )
        return jnp.concatenate([main, tile], -1).astype(BF)

    def by_row(values):
        return values.reshape(4, 128, 2, 192).transpose(0, 2, 1, 3).reshape(8, 128, 192)

    def unpacked(tiles):
        tiles = tiles.astype(F32)
        rest = jnp.where(odd, tiles[..., 192:256], tiles[..., 128:192])
        both = jnp.concatenate([tiles[..., :128], rest], -1)
        return both.reshape(4, 2, 128, 192).transpose(0, 2, 1, 3).reshape(512, 2, 192)

    high = lax.reduce_precision(gains, 8, 7)
    gain_rows = jnp.concatenate([high, gains - high, jnp.zeros((12, 192), F32)], 0)
    xin = jnp.concatenate(
        [packed(by_row(stream)), jnp.broadcast_to(packed(gain_rows), (8, 16, 256))], 1
    )
    cin = packed(by_row(cotangent))
    qkv_low = qkv_weight.astype(BF).reshape(192, 2, 4, HS)
    out_low = out_weight.astype(BF).reshape(2, 2, HS, 192).transpose(1, 0, 2, 3)
    out_low = jnp.pad(out_low.reshape(2, 2 * HS, 192), ((0, 0), (64, 0), (0, 0))).reshape(512, 192)
    first_weights = jnp.concatenate(
        [
            qkv_low[:, :, :2].transpose(0, 2, 1, 3).reshape(192, 384),
            qkv_low[:, :, 2:].transpose(0, 2, 1, 3).reshape(192, 384),
            out_low.T,
        ],
        1,
    )
    second_weights = jnp.concatenate(
        [gate_up_weight.reshape(192, 2048).astype(BF), down_weight.astype(BF).T], 1
    )

    place = lax.dynamic_index_in_dim(positions, zl, 0, keepdims=False).reshape(4, 4, 128)
    place = lax.dynamic_index_in_dim(place, y, 1, keepdims=False)
    token = (
        jnp.arange(4, dtype=jnp.int32)[:, None] * 512
        + y * 128
        + jnp.arange(128, dtype=jnp.int32)[None, :]
    )
    table = jnp.stack([token - place, token], 1)
    table = jnp.concatenate([table, table], -1).reshape(8, 256)
    frequency = rope_theta ** (-2.0 * (jnp.arange(256) % (HS // 2)).astype(F32) / HS)
    frequency = jnp.broadcast_to(frequency, (8, 256))

    part, h1_all, w1, c_all, kv_all, q, heads, log_total, cosine, sine, xtok, ctok, gtok = enter(
        xin, cin, first_weights, place.reshape(512, 1).astype(F32), frequency, table
    )
    after, gain_two, rise, f_part, d_all, grads2 = feed(
        part, xtok, gtok, ctok, second_weights, c_all
    )
    o_tiles, s_tiles, grads1, gains_tile = leave(
        f_part, rise, xtok, after, gtok, gain_two, q, heads, log_total, table, cosine, sine,
        d_all, w1, kv_all, h1_all,
    )
    output = stream + unpacked(o_tiles)
    stream_grad = cotangent + unpacked(s_tiles)

    def own_block(grads):
        grads = grads.reshape(2, 96, 2, -1)
        block = jnp.concatenate([grads[0, :64], grads[1, :64], grads[0, 64:], grads[1, 64:]], 0)
        return block.astype(F32)

    block1, block2 = own_block(grads1), own_block(grads2)
    qkv_total = block1[:, :, :384].reshape(192, 2, 2, 2, HS)
    qkv_total = qkv_total.transpose(0, 3, 1, 2, 4).reshape(192, 768)
    out_total = block1[:, :, 448:640].reshape(192, 2, 2, HS).transpose(2, 1, 3, 0).reshape(384, 192)
    gate_up_total = jnp.stack(
        [block2[:, :, :512].reshape(192, 1024), block2[:, :, 512:1024].reshape(192, 1024)], 1
    )
    down_total = block2[:, :, 1024:].reshape(192, 1024).T
    gains_rest = jnp.where(odd, gains_tile[:2, 192:256], gains_tile[:2, 128:192])
    gains_total = jnp.concatenate([gains_tile[:2, :128], gains_rest], 1)

    rate_qkv, rate_out, rate_gate_up, rate_down, rate_gains = step_rates()
    qkv_new = adamw_update(qkv_weight, qkv_first, qkv_second, qkv_total, rate_qkv, weight_decay)
    out_new = adamw_update(out_weight, out_first, out_second, out_total, rate_out, weight_decay)
    gate_up_new = adamw_update(
        gate_up_weight, gate_up_first, gate_up_second, gate_up_total, rate_gate_up, weight_decay
    )
    down_new = adamw_update(
        down_weight, down_first, down_second, down_total, rate_down, weight_decay
    )
    gains_new = adamw_update(gains, gains_first, gains_second, gains_total, rate_gains, 0.0)
    return (output, stream_grad, *qkv_new, *out_new, *gate_up_new, *down_new, *gains_new)


def solution(mesh):
    tokens = P("col", "dp", "row")
    table = P("dp", None)
    wide, tall, pairs, both = P("row", "col"), P("col", "row"), P("row", None, "col"), P(None, "row")
    weights = (wide,) * 3 + (tall,) * 3 + (pairs,) * 3 + (tall,) * 3 + (both,) * 3
    return jax.shard_map(
        body,
        mesh=mesh,
        in_specs=(tokens, tokens, table, table, *weights),
        out_specs=(tokens, tokens, *weights),
        check_vma=False,
    )
```

```python
import functools

import jax
import jax.numpy as jnp
import numpy as np
from jax import lax
from jax.experimental import pallas as pl
from jax.experimental.pallas import tpu as pltpu
from jax.sharding import PartitionSpec as P

D = 1536
FF = 4096
HQ = 16
KVH = 8
HS = 96
STEP = 10
LEN = 2048
WINDOW = 1024

norm_epsilon = 1e-05
rope_theta = 100000.0
beta_first = 0.9
beta_second = 0.95
adam_epsilon = 1e-08
weight_decay = 0.1
score_scale = HS**-0.5

MESH = pl.DeviceIdType.MESH
BF = jnp.bfloat16
F32 = jnp.float32
VM = pl.BlockSpec(memory_space=pltpu.VMEM)
ANY = pl.BlockSpec(memory_space=pl.ANY)


def selection(source, count):
    chosen = np.zeros((count, len(source)), np.float32)
    chosen[source, np.arange(len(source))] = 1.0
    return jnp.asarray(chosen, BF)


def qkv_order():
    b = np.arange(768)
    return selection(b % 384 // HS * 192 + b // 384 * HS + b % HS, 768)


def out_order():
    b = np.arange(384)
    return selection(b % 192 // HS * 256 + 64 + b // 192 * HS + b % HS, 512)


class Place:
    def __init__(self):
        self.dp = lax.axis_index("dp")
        self.row = lax.axis_index("row")
        self.x = lax.axis_index("col")
        self.zh = lax.div(self.dp, 2)
        self.core = lax.rem(self.dp, 2)
        self.y = lax.div(self.row, 2)
        self.zl = lax.rem(self.row, 2)
        self.z = self.zh * 2 + self.zl

    def at(self, dx=0, dy=0, dz=0, dcore=0):
        x = lax.rem(self.x + (dx + 4), 4)
        y = lax.rem(self.y + (dy + 4), 4)
        z = lax.rem(self.z + (dz + 4), 4)
        core = lax.rem(self.core + dcore, 2)
        return (lax.div(z, 2) * 2 + core, y * 2 + lax.rem(z, 2), x)

    def pair(self):
        return self.at(dcore=1)

    def in_row(self, step):
        return (self.dp, lax.rem(self.row + step, 8), self.x)

    def in_dp(self, step):
        return (lax.rem(self.dp + step, 4), self.row, self.x)


def greet(devices):
    barrier = pltpu.get_barrier_semaphore()
    for device in devices:
        pl.semaphore_signal(barrier, inc=1, device_id=device, device_id_type=MESH)
    pl.semaphore_wait(barrier, len(devices))


class Wire:
    def __init__(self, send, recv, local=None):
        self.send, self.recv, self.local = send, recv, local
        self.sent, self.open, self.near, self.stays = [], {}, [], 0

    def copy(self, src, dst, device):
        n = len(self.sent)
        made = pltpu.make_async_remote_copy(
            src_ref=src,
            dst_ref=dst,
            send_sem=self.send.at[n],
            recv_sem=self.recv.at[n],
            device_id=device,
            device_id_type=MESH,
        )
        made.start()
        self.sent.append(made)
        self.open[n] = made
        return n

    def arrive(self, *numbers):
        for n in numbers:
            self.open.pop(n).wait_recv()

    def stay(self, src, dst):
        made = pltpu.make_async_copy(src, dst, self.local.at[self.stays])
        self.stays += 1
        made.start()
        self.near.append(made)
        return made

    def there(self, *stays):
        for made in stays:
            self.near = [other for other in self.near if other is not made]
            made.wait()

    def settle(self):
        self.arrive(*list(self.open))

    def finish(self):
        self.settle()
        for made in self.sent:
            made.wait_send()
        self.there(*list(self.near))


def around(me):
    return lax.rem(me + 3, 4), lax.rem(me + 1, 4), lax.rem(me + 2, 4)


def as_list(refs):
    return refs if isinstance(refs, list) else [refs]


def ring_gather(wire, me, right, left, own, slot, on_block=None):
    l, r, o = around(me)

    def send(src, dst, device):
        return [wire.copy(a, b, device) for a, b in zip(as_list(src), as_list(dst))]

    first = send(own(0), slot(me, 0), right), send(own(1), slot(me, 1), left)
    second = send(own(1), slot(me, 1), right), send(own(0), slot(me, 0), left)
    yield
    wire.arrive(*first[0])
    far0 = send(slot(l, 0), slot(l, 0), right)
    wire.arrive(*first[1])
    far1 = send(slot(r, 1), slot(r, 1), left)
    yield
    wire.arrive(*second[0])
    if on_block:
        on_block(l)
    wire.arrive(*second[1])
    if on_block:
        on_block(r)
    yield
    wire.arrive(*far0, *far1)
    if on_block:
        on_block(o)


def leading(ref):
    found = [()]
    for size in ref.shape[:-2]:
        found = [index + (n,) for index in found for n in range(size)]
    return found


def add_parts(out, refs):
    for index in leading(out):
        at = index + (slice(None), slice(None))
        total = refs[0][at].astype(F32)
        for ref in refs[1:]:
            total = total + ref[at].astype(F32)
        out[at] = total.astype(out.dtype)


def ring_sum(wire, me, right, left, part, far, near, out):
    l, r, o = around(me)

    def send(srcs, dsts, device):
        return [wire.copy(a, b, device) for a, b in zip(srcs, dsts)]

    far0 = send(part(o, 0), far(0), right)
    far1 = send(part(o, 1), far(1), left)
    to_right = send(part(r, 1), near(0, 1), right)
    to_left = send(part(l, 0), near(1, 0), left)
    yield
    wire.arrive(*far0)
    for a, b in zip(far(0), part(r, 0)):
        add_parts(a, [a, b])
    to_right += send(far(0), near(0, 0), right)
    wire.arrive(*far1)
    for a, b in zip(far(1), part(l, 1)):
        add_parts(a, [a, b])
    to_left += send(far(1), near(1, 1), left)
    yield
    wire.arrive(*to_right, *to_left)
    for h in range(2):
        for a, b, c, total in zip(part(me, h), near(0, h), near(1, h), out(h)):
            add_parts(total, [a, b, c])


def side_by_side(*flows):
    flows = list(flows)
    while flows:
        for flow in list(flows):
            try:
                next(flow)
            except StopIteration:
                flows.remove(flow)


def rows(ref, start, size, multiple):
    return ref.at[pl.ds(pl.multiple_of(start, multiple), size)]


def weight_gather(wire, here, own, whole):
    core, zl = here.core, here.zl
    right, left = here.at(dy=1), here.at(dy=-1)
    up, down = here.at(dz=1), here.at(dz=-1)
    l, r, o = around(here.y)

    def mine(j):
        start = (core * 64, core * 64 + 32, 128 + core * 32, 144 + core * 32)[j]
        return rows(own, start, (32, 32, 16, 16)[j], 16)

    def piece(y, j, lo):
        block = y * 2 + lo
        main, rest = block * 128 + core * 64, 1024 + block * 64 + core * 32
        start = (main, main + 32, rest, rest + 16)[j]
        return rows(whole, start, (32, 32, 16, 16)[j], 16)

    def to_pair(y, lo):
        block = y * 2 + lo
        for view in (
            rows(whole, block * 128 + core * 64, 64, 64),
            rows(whole, 1024 + block * 64 + core * 32, 32, 32),
        ):
            paired.append(wire.copy(view, view, here.pair()))

    paired = []

    def over(y, js, device, src=None):
        return [wire.copy((src or (lambda j: piece(y, j, zl)))(j), piece(y, j, zl), device) for j in js]

    y = here.y
    kept = (
        wire.stay(own.at[pl.ds(0, 128)], rows(whole, here.row * 128, 128, 128)),
        wire.stay(own.at[pl.ds(128, 64)], rows(whole, 1024 + here.row * 64, 64, 64)),
    )
    r_first, l_first = over(y, (0, 2), right, mine), over(y, (1, 3), left, mine)
    r_next, l_next = over(y, (1, 3), right, mine), over(y, (0, 2), left, mine)
    z_own = over(y, (0, 2), up, mine) + over(y, (1, 3), down, mine)
    yield
    wire.arrive(*r_first)
    far = over(l, (0, 2), right)
    wire.arrive(*l_first)
    far += over(r, (1, 3), left)
    z_l = over(l, (0, 2), up)
    z_r = over(r, (1, 3), down)
    yield
    wire.arrive(*r_next)
    z_l += over(l, (1, 3), down)
    to_pair(l, zl)
    wire.arrive(*l_next)
    z_r += over(r, (0, 2), up)
    to_pair(r, zl)
    yield
    wire.arrive(*far)
    z_o = over(o, (0, 2), up) + over(o, (1, 3), down)
    to_pair(o, zl)
    yield
    for block, numbers in ((y, z_own), (l, z_l), (r, z_r), (o, z_o)):
        wire.arrive(*numbers)
        to_pair(block, 1 - zl)
        yield
    wire.arrive(*paired)
    wire.there(*kept)


def share(wire, here, out):
    half = lambda i, h: out.at[i, pl.ds(64 * h, 64)]

    def to_pair(i):
        wire.copy(out.at[i], out.at[i + 4], here.pair())

    to_pair(here.x)
    yield from ring_gather(
        wire,
        here.x,
        here.at(dx=1),
        here.at(dx=-1),
        lambda h: half(here.x, h),
        half,
        to_pair,
    )


def x_sum(wire, here, part, far, near, out):
    return ring_sum(
        wire,
        here.x,
        here.at(dx=1),
        here.at(dx=-1),
        lambda i, h: [part.at[i, pl.ds(64 * h, 64)]],
        lambda h: [far.at[h]],
        lambda s, h: [near.at[s, pl.ds(64 * h, 64)]],
        lambda h: [out.at[pl.ds(64 * h, 64)]],
    )


def x_sum_scratch():
    return [pltpu.VMEM((2, 64, D), BF), pltpu.VMEM((2, 128, D), BF)]


HIGHS = (64, 32)


def order_columns(width, cut, order):
    return (0, cut) if order == 0 else (cut, width - cut)


def first_scratch(width, cut):
    shapes = []
    for order in range(2):
        size = order_columns(width, cut, order)[1]
        for high in HIGHS:
            shapes += [
                pltpu.VMEM((2, 2, high, size), BF),
                pltpu.VMEM((2, 2, 2, high, size), BF),
            ]
    return shapes


def half_sums(width, cut):
    return [
        (2, 2, high, order_columns(width, cut, order)[1]) for order in range(2) for high in HIGHS
    ]


def second_scratch(width, cut):
    shapes = []
    for order in range(2):
        size = order_columns(width, cut, order)[1]
        for high in HIGHS:
            shapes += [
                pltpu.VMEM((2, high // 2, size), BF),
                pltpu.VMEM((2, 2, high // 2, size), BF),
            ]
    return shapes + [pltpu.VMEM((96, width), BF)]


def rings(here):
    y_ring = (here.y, here.at(dy=1), here.at(dy=-1))
    z_ring = (here.z, here.at(dz=1), here.at(dz=-1))
    return y_ring, z_ring


def first_sums(wire, here, grads, scratch, sums, width, cut):
    def flow(order):
        at = pl.ds(*order_columns(width, cut, order))
        buffers, out = scratch[4 * order : 4 * order + 4], sums[2 * order : 2 * order + 2]

        def of_z(ref, i, h):
            return ref.at[pl.ds(2 * h, 2), lax.rem(i, 2), lax.div(i, 2), :, at]

        def of_y(ref, i, h):
            return ref.at[i, h, :, :, at]

        pick = of_z if order == 0 else of_y
        return ring_sum(
            wire,
            *rings(here)[1 - order],
            lambda i, h: [pick(g, i, h) for g in grads],
            lambda h: [b.at[h] for b in buffers[0::2]],
            lambda s, h: [b.at[s, h] for b in buffers[1::2]],
            lambda h: [b.at[h] for b in out],
        )

    return flow(0), flow(1)


def second_sums(wire, here, sums, scratch, width, cut):
    fin = scratch[-1]

    def flow(order):
        at = pl.ds(*order_columns(width, cut, order))
        buffers, terms = scratch[4 * order : 4 * order + 4], sums[2 * order : 2 * order + 2]

        def part(i, h):
            high, low = lax.div(i, 2), lax.rem(i, 2)
            lead = (high, low) if order == 0 else (low, high)
            return [
                b.at[lead[0], lead[1], pl.ds(tall // 2 * h, tall // 2)]
                for b, tall in zip(terms, HIGHS)
            ]

        return ring_sum(
            wire,
            *rings(here)[order],
            part,
            lambda h: [b.at[h] for b in buffers[0::2]],
            lambda s, h: [b.at[s, h] for b in buffers[1::2]],
            lambda h: [
                fin.at[pl.ds(start + tall // 2 * h, tall // 2), at]
                for start, tall in zip((0, 64), HIGHS)
            ],
        )

    return flow(0), flow(1)


def grad_share(wire, here, fin, out, width):
    columns = pl.ds(pl.multiple_of(here.core * width, 128), width)
    mine = out.at[here.zh, :, columns]
    other = out.at[1 - here.zh, :, columns]
    wire.stay(fin, mine)
    wire.copy(fin, mine, here.pair())
    n = wire.copy(fin, mine, here.at(dz=2))
    yield
    wire.arrive(n)
    wire.copy(other, other, here.pair())


def swap_rows(wire, here, src, dst):
    return [
        wire.copy(src.at[lax.rem(here.row + s, 8)], dst.at[here.row], here.in_row(s))
        for s in range(1, 8)
    ]


def widened(ref, start, size):
    at = pl.ds(start, size)
    main = [ref[r, at, 0:128] for r in range(8)]
    rest = [ref[2 * j, at, 128:256] + ref[2 * j + 1, at, 128:256] for j in range(4)]
    return jnp.concatenate(main + rest, axis=1)


def narrowed(out, value):
    for r in range(8):
        out[r, :, 0:128] = value[:, 128 * r : 128 * r + 128]
        j = 1024 + 128 * (r // 2)
        out[r, :, 128:256] = value[:, j : j + 128]


def ring_partners(here):
    return [here.at(dx=1), here.at(dx=-1)]


def plane_partners(here):
    return [here.at(dy=1), here.at(dy=-1), here.at(dz=1), here.at(dz=-1)]


def dot(a, b, left=1, right=0):
    return lax.dot_general(a, b, (((left,), (right,)), ((), ())), preferred_element_type=F32)


def turned(values, cosine, sine):
    lane = lax.broadcasted_iota(jnp.int32, values.shape, 1)
    front = lax.rem(lane, HS) < HS // 2
    ahead, back = pltpu.roll(values, 256 - HS // 2, 1), pltpu.roll(values, HS // 2, 1)
    return values * cosine + jnp.where(front, -ahead, back) * sine


def packed_pair(a, b):
    return jnp.concatenate([a[:, :128], a[:, 128:] + b[:, :128], b[:, 128:]], axis=1)


def windows(y):
    return ((0, 4), (0, 8), (1 + y, 8), (5 + y, 8))


def allowed_keys(table, c, start, count):
    key = start * 128 + lax.broadcasted_iota(jnp.int32, (count * 128, 256), 0)
    return (key >= table[2 * c : 2 * c + 1]) & (key <= table[2 * c + 1 : 2 * c + 2])


def both_heads(ref, at):
    return jnp.concatenate([ref[at, 0:256], ref[at, 256:512]], axis=0)


def attend(here, q, kv, table, heads, log_total):
    lane = lax.broadcasted_iota(jnp.int32, (256, 256), 1)
    for c, (start, count) in enumerate(windows(here.y)):
        at = pl.ds(128 * c, 128)
        allowed = allowed_keys(table, c, start, count)
        q_both = both_heads(q, at)
        k = kv[pl.ds(start, count), :, 0:256].reshape(count * 128, 256)
        v = kv[pl.ds(start, count), :, 128:384].reshape(count * 128, 256)
        made = []
        for g in range(2):
            n = 2 * c + g
            q_one = jnp.where((lane >= HS) == (g == 1), q_both, jnp.zeros_like(q_both))
            scores = dot(k, q_one, 1, 1) * score_scale
            scores = jnp.where(allowed, scores, -1e30)
            top = jnp.max(scores, axis=0, keepdims=True)
            weights = jnp.exp(scores - top)
            total = jnp.sum(weights, axis=0, keepdims=True)
            shares = (weights * (1.0 / total)).astype(BF)
            made.append(dot(shares, v, 0, 0))
            log_total[n : n + 1] = top + jnp.log(total)
        out = jnp.where(lane < 64 + HS, made[0], made[1])
        out = jnp.where(lane < 64, 0.0, out).astype(BF)
        heads[at, 0:256] = out[:128]
        heads[at, 256:512] = out[128:]


def attend_back(here, q, kv, table, log_total, dout, dq, total):
    lane = lax.broadcasted_iota(jnp.int32, (256, 256), 1)
    total[...] = jnp.zeros_like(total)
    for c, (start, count) in enumerate(windows(here.y)):
        at = pl.ds(128 * c, 128)
        blocks = pl.ds(start, count)
        allowed = allowed_keys(table, c, start, count)
        q_both, d_both = both_heads(q, at), both_heads(dout, at)
        k = kv[blocks, :, 0:256].reshape(count * 128, 256)
        v = kv[blocks, :, 128:384].reshape(count * 128, 256)
        made = []
        for g in range(2):
            n = 2 * c + g
            q_one = jnp.where((lane >= HS) == (g == 1), q_both, jnp.zeros_like(q_both))
            d_one = jnp.where((lane >= 64 + HS) == (g == 1), d_both, jnp.zeros_like(d_both))
            scores = dot(k, q_one, 1, 1) * score_scale
            shares = jnp.where(allowed, jnp.exp(scores - log_total[n : n + 1]), 0.0)
            dshares = dot(v, d_one, 1, 1)
            inner = jnp.sum(shares * dshares, axis=0, keepdims=True)
            dscores = (shares * (dshares - inner)).astype(BF)
            made.append(dot(dscores, k, 0, 0))
            dk = dot(dscores, q_one) * score_scale
            dv = dot(shares.astype(BF), d_one)
            total[blocks, :, 0:256] += dk.reshape(count, 128, 256)
            total[blocks, :, 128:384] += dv.reshape(count, 128, 256)
        out = jnp.where(lane < HS, made[0], made[1]) * score_scale
        dq[at, 0:256] = out[:128]
        dq[at, 256:512] = out[128:]


def tokens_of(ref, pair=0):
    return ref[4 * pair : 4 * pair + 4].reshape(512, D)


def columns(n, size=256):
    return pl.ds(pl.multiple_of(n * size, size), size)


def back_to_width(units, at, weights, weight_at, out):
    @pl.loop(0, D // 256)
    def _(n):
        made = dot(units[:, at], weights[columns(n), weight_at], 1, 1)
        out[:, :, columns(n)] = made.astype(BF).reshape(4, 128, 256)


def weight_grads(tokens, own, pair, main, rest, at):
    def made(n):
        total = dot(tokens[0:4, :, columns(n)].reshape(512, 256), own[0][:, own[1]], 0, 0)
        return total + dot(tokens[4:8, :, columns(n)].reshape(512, 256), pair[0][:, pair[1]], 0, 0)

    @pl.loop(0, 4)
    def _(n):
        value = made(n)
        main[n, :, :, :, at] = value.astype(BF).reshape(2, 2, 64, value.shape[1])

    @pl.loop(0, 2)
    def _(n):
        value = made(n + 4)
        rest[pl.ds(2 * n, 2), :, :, :, at] = value.astype(BF).reshape(2, 2, 2, 32, value.shape[1])


def norm_back(value, grad, gain):
    scale = lax.rsqrt(jnp.mean(value * value, axis=1, keepdims=True) + norm_epsilon)
    unit = value * scale
    scaled = grad * gain
    inner = jnp.mean(scaled * unit, axis=1, keepdims=True)
    return scale * (scaled - unit * inner), jnp.sum(grad * unit, axis=0, keepdims=True)


def normed(value, gain):
    scale = lax.rsqrt(jnp.mean(value * value, axis=1, keepdims=True) + norm_epsilon)
    return (value * scale * gain).astype(BF)


def key_block(c, y):
    return 4 * c + y


def pack_rows(here, out, values):
    for y in range(4):
        for zl in range(2):
            block = values[zl, :, 128 * y : 128 * y + 128]
            rest = block[128:]
            none = jnp.zeros_like(rest)
            low = jnp.where(here.zl == 0, rest, none)
            high = jnp.where(here.zl == 0, none, rest)
            tile = jnp.concatenate([block[:128], low, high], axis=0)
            out[2 * y + zl, 0:128, :] = tile.T.astype(BF)


def own_half(here, rest):
    return jnp.where(here.zl == 0, rest, pltpu.roll(rest, 64, 1))


def enter_kernel(
    stream, cotangent, qkv_weight, out_weight, gate_up, down, gains, positions, frequency, qkv_at, out_at,
    part, h1_out, wq_out, wo_out, c_out, kv_out, win_out,
    q, heads, log_total, cosine, sine, xtok, ctok, gtok, table,
    xf, cf, qf, of, gf, df, qs, os, xin, cin, wq_own, wo_own, win,
    xbuf, cbuf, h1_all, c_all, wq, wo, kv_own, kv_all, qkv, gpad, send, recv, local,
):
    here = Place()
    wire = Wire(send, recv, local)
    x_load = wire.stay(stream, xf)
    q_load = wire.stay(qkv_weight, qf), wire.stay(qkv_at, qs)
    o_load = wire.stay(out_weight, of), wire.stay(out_at, os)
    c_load = wire.stay(cotangent, cf)
    f_load = [wire.stay(gate_up.at[:, j], gf.at[j]) for j in range(2)] + [wire.stay(down, df)]
    greet(
        [here.in_row(s) for s in range(1, 8)]
        + ring_partners(here)
        + [here.at(dz=1), here.at(dz=-1), here.pair()]
    )
    gpad[...] = jnp.zeros_like(gpad)
    gpad[0:2, 0:192] = gains[...]
    g = gpad[...]
    high = g.astype(BF).astype(F32)
    rows16 = jnp.concatenate([high[0:2], (g - high)[0:2], jnp.zeros((12, 256), F32)], axis=0)
    rest = rows16[:, 128:]
    rest = jnp.where(here.zl == 0, rest, pltpu.roll(rest, 64, 1))
    rows16 = jnp.concatenate([rows16[:, :128], rest], axis=1).astype(BF)
    wire.there(x_load)
    for r in range(8):
        xin[r, 128:144, :] = rows16
    pack_rows(here, xin, xf)
    xs = swap_rows(wire, here, xin, xbuf)
    xbuf[here.row] = xin[here.row]

    wire.there(*q_load)
    wq_own[...] = dot(qf[...].astype(BF), qs[...], 1, 1).astype(BF)
    q_weights = weight_gather(wire, here, wq_own, wq)
    next(q_weights)
    wire.there(*o_load)
    wo_own[...] = dot(of[...].astype(BF), os[...], 1, 1).astype(BF)
    o_weights = weight_gather(wire, here, wo_own, wo)
    lane = lax.broadcasted_iota(jnp.int32, (128, 256), 1)
    for c in range(4):
        first = 512 * c + 128 * here.y
        place = positions[:, pl.ds(pl.multiple_of(first, 128), 128)]
        place = jnp.where(here.zl == 0, place[0:1], place[1:2])
        token = first + lax.broadcasted_iota(jnp.int32, (1, 128), 1)
        table[2 * c : 2 * c + 1, :] = jnp.concatenate([token - place] * 2, axis=1)
        table[2 * c + 1 : 2 * c + 2, :] = jnp.concatenate([token] * 2, axis=1)
        column = jnp.broadcast_to(place.astype(F32), (128, 128)).T[:, 0:1]
        angles = column * frequency[0:1]
        at = pl.ds(128 * c, 128)
        cosine[at, :] = jnp.where(lane < 2 * HS, jnp.cos(angles), 0.0)
        sine[at, :] = jnp.where(lane < 2 * HS, jnp.sin(angles), 0.0)
    wire.there(c_load)
    pack_rows(here, cin, cf)
    cbuf[here.row] = cin[here.row]

    wire.arrive(*xs)
    x = widened(xbuf, 0, 128)
    xtok[...] = x
    g = widened(xbuf, 128, 16).astype(F32)
    g = g[0:2] + g[2:4]
    gtok[...] = g
    h1_all[here.x] = normed(x.astype(F32), g[0:1])
    h1_flow = share(wire, here, h1_all)
    next(h1_flow)
    next(q_weights)
    wire.there(*f_load)
    win[:, 0:1024] = gf[0].astype(BF)
    win[:, 1024:2048] = gf[1].astype(BF)
    win[:, 2048:3072] = df[...].astype(BF)
    wire.stay(win, win_out)
    side_by_side(h1_flow, q_weights)
    next(o_weights)
    cs = swap_rows(wire, here, cin, cbuf)

    @pl.loop(0, 3)
    def _(n):
        qkv[:, columns(n)] = dot(tokens_of(h1_all), wq[:, columns(n)])

    for c in range(4):
        at = pl.ds(128 * c, 128)
        turn = cosine[at], sine[at]
        key = turned(qkv[at, 384:640], *turn)
        value = jnp.where(lane < 64, 0.0, qkv[at, 512:768])
        kv = packed_pair(key, value).astype(BF)
        kv_own[c] = kv
        kv_all[key_block(c, here.y)] = kv

    keys = ring_gather(
        wire,
        here.y,
        here.at(dy=1),
        here.at(dy=-1),
        lambda h: [kv_own.at[2 * h], kv_own.at[2 * h + 1]],
        lambda i, h: [kv_all.at[key_block(2 * h + n, i)] for n in range(2)],
    )
    next(keys)
    for c in range(4):
        at = pl.ds(128 * c, 128)
        turn = cosine[at], sine[at]
        q[at, 0:256] = turned(qkv[at, 0:256], *turn).astype(BF)
        second = pltpu.roll(qkv[at, 128:384], 192, 1)
        q[at, 256:512] = turned(second, *turn).astype(BF)
    next(o_weights)
    wire.arrive(*cs)
    c_value = widened(cbuf, 0, 128)
    ctok[...] = c_value
    c_all[here.x] = c_value
    side_by_side(keys, o_weights, share(wire, here, c_all))
    attend(here, q, kv_all, table, heads, log_total)
    back_to_width(heads, slice(None), wo, slice(None), part)
    wire.settle()
    for held, out in (
        (h1_all, h1_out), (c_all, c_out), (wq, wq_out), (wo, wo_out), (kv_all, kv_out)
    ):
        wire.stay(held, out)
    wire.finish()


def shape(dtype, *sizes):
    return jax.ShapeDtypeStruct(sizes, dtype)


def signals(*counts):
    return [pltpu.SemaphoreType.DMA((n,)) for n in counts]


def settings(number):
    return pltpu.CompilerParams(
        collective_id=number, has_side_effects=True, vmem_limit_bytes=60 << 20
    )


def enter(*operands):
    return pl.pallas_call(
        enter_kernel,
        out_shape=[
            shape(BF, 4, 128, D),
            shape(BF, 8, 128, D),
            shape(BF, D, 768),
            shape(BF, D, 512),
            shape(BF, 8, 128, D),
            shape(BF, 16, 128, 384),
            shape(BF, 192, 3072),
            shape(BF, 512, 512),
            shape(BF, 512, 512),
            shape(F32, 8, 256),
            shape(F32, 512, 256),
            shape(F32, 512, 256),
            shape(BF, 128, D),
            shape(BF, 128, D),
            shape(F32, 2, D),
            shape(jnp.int32, 8, 256),
        ],
        in_specs=[ANY] * 6 + [VM] * 3 + [ANY] * 2,
        out_specs=[VM] + [ANY] * 6 + [VM] * 9,
        scratch_shapes=[
            pltpu.VMEM((2, 192, 512), F32),
            pltpu.VMEM((2, 192, 512), F32),
            pltpu.VMEM((192, 768), F32),
            pltpu.VMEM((192, 384), F32),
            pltpu.VMEM((2, 192, 1024), F32),
            pltpu.VMEM((192, 1024), F32),
            pltpu.VMEM((768, 768), BF),
            pltpu.VMEM((512, 384), BF),
            pltpu.VMEM((8, 144, 256), BF),
            pltpu.VMEM((8, 128, 256), BF),
            pltpu.VMEM((192, 768), BF),
            pltpu.VMEM((192, 512), BF),
            pltpu.VMEM((192, 3072), BF),
            pltpu.VMEM((8, 144, 256), BF),
            pltpu.VMEM((8, 128, 256), BF),
            pltpu.VMEM((8, 128, D), BF),
            pltpu.VMEM((8, 128, D), BF),
            pltpu.VMEM((D, 768), BF),
            pltpu.VMEM((D, 512), BF),
            pltpu.VMEM((4, 128, 384), BF),
            pltpu.VMEM((16, 128, 384), BF),
            pltpu.VMEM((512, 768), F32),
            pltpu.VMEM((8, 256), F32),
        ]
        + signals(160, 160, 24),
        compiler_params=settings(1),
        name="enter",
    )(*operands)


def feed_kernel(width, cut, *refs):
    part, xtok, gtok, ctok, win, c_in = refs[:6]
    after, gain, rise, f_part, d_out = refs[6:11]
    sums = refs[11:15]
    far, near, far2, near2, middle, summed, h2_all, c_all, w_all, units, others, part2 = refs[15:27]
    main, rest, d_all = refs[27:30]
    scratch, (send, recv, local) = refs[30:-3], refs[-3:]
    here = Place()
    wire = Wire(send, recv, local)
    greet(ring_partners(here) + plane_partners(here) + [here.pair()])
    c_copy = wire.stay(c_in, c_all)

    def forward():
        yield from x_sum(wire, here, part, far, near, rise)
        value = rise[...] + xtok[...].astype(F32)
        middle[...] = value
        h2_all[here.x] = normed(value, gtok[1:2])
        yield from share(wire, here, h2_all)

    side_by_side(forward(), weight_gather(wire, here, win, w_all))
    wire.settle()
    wire.there(c_copy)

    def unit_tiles(first):
        @pl.loop(0, 2)
        def _(n):
            j = first * 2 + n
            gate = dot(tokens_of(h2_all), w_all[:, columns(j)])
            up = dot(tokens_of(h2_all), w_all[:, columns(j + 4)])
            dact = dot(tokens_of(c_all), w_all[:, columns(j + 8)])
            sigmoid = 1.0 / (1.0 + jnp.exp(-gate))
            silu = gate * sigmoid
            units[:, columns(j)] = (dact * up * sigmoid * (1.0 + gate * (1.0 - sigmoid))).astype(BF)
            units[:, columns(j + 4)] = (dact * silu).astype(BF)
            units[:, columns(j + 8)] = (silu * up).astype(BF)

    unit_tiles(1 - here.core)
    swaps = [
        wire.copy(
            units.at[:, columns(1 - here.core + 2 * n, 512)],
            others.at[:, pl.ds(512 * n, 512)],
            here.pair(),
        )
        for n in range(3)
    ]
    unit_tiles(here.core)
    back_to_width(units, slice(0, 2048), w_all, slice(0, 2048), part2)

    def backward():
        yield from x_sum(wire, here, part2, far2, near2, summed)
        left, gain_terms = norm_back(middle[...], summed[...], gtok[1:2])
        gain[...] = jnp.broadcast_to(gain_terms, gain.shape)
        after[...] = left
        d_all[here.x] = (left + ctok[...].astype(F32)).astype(BF)
        yield from share(wire, here, d_all)

    chain = backward()
    next(chain)
    back_to_width(units, slice(2048, 3072), w_all, slice(2048, 3072), f_part)
    next(chain)
    wire.arrive(*swaps)
    for n, tokens in enumerate((h2_all, h2_all, c_all)):
        at = pl.ds(512 * n, 512)
        weight_grads(
            tokens, (units, columns(here.core + 2 * n, 512)), (others, at), main, rest, at
        )
    side_by_side(chain, *first_sums(wire, here, (main, rest), scratch, sums, width, cut))
    wire.settle()
    wire.stay(d_all, d_out)
    wire.finish()


def grad_arrays(width):
    return [pltpu.VMEM((4, 2, 2, high, width), BF) for high in HIGHS]


def feed(part, xtok, gtok, ctok, win, c_in):
    width, cut = 1536, 768
    return pl.pallas_call(
        functools.partial(feed_kernel, width, cut),
        out_shape=[
            shape(F32, 128, D),
            shape(F32, 8, D),
            shape(F32, 128, D),
            shape(BF, 4, 128, D),
            shape(BF, 8, 128, D),
        ]
        + [shape(BF, *sizes) for sizes in half_sums(width, cut)],
        in_specs=[VM, VM, VM, VM, ANY, ANY],
        out_specs=[VM] * 4 + [ANY] + [VM] * 4,
        scratch_shapes=x_sum_scratch()
        + x_sum_scratch()
        + [
            pltpu.VMEM((128, D), F32),
            pltpu.VMEM((128, D), F32),
            pltpu.VMEM((8, 128, D), BF),
            pltpu.VMEM((8, 128, D), BF),
            pltpu.VMEM((D, 3072), BF),
            pltpu.VMEM((512, 3072), BF),
            pltpu.VMEM((512, 1536), BF),
            pltpu.VMEM((4, 128, D), BF),
        ]
        + grad_arrays(width)
        + [pltpu.VMEM((8, 128, D), BF)]
        + first_scratch(width, cut)
        + signals(144, 144, 8),
        compiler_params=settings(2),
        name="feed",
    )(part, xtok, gtok, ctok, win, c_in)


FEED = (1536, 768)
ATTN = (640, 256)


def leave_kernel(*refs):
    f_part, rise, xtok, after, gtok, gain, q, heads, log_total, table, cosine, sine = refs[:12]
    f_sums = refs[12:16]
    d_in, wq_in, wo_in, kv_in, h1_in = refs[16:21]
    o_all, s_all, gout, fout, gains_out = refs[21:26]
    d_all, wq, wo, kv_all, h1_all, dout, dq, total, dkv, kfar, knear, dkv_own, dqkv = refs[26:39]
    heads_in, dqkv_in, part, far, near, far2, near2, summed, osend, ssend = refs[39:49]
    gsend, grow, gcol, gdp, main, rest = refs[49:55]
    scratch, (send, recv, local) = refs[55:-3], refs[-3:]
    a_first, scratch = scratch[:8], scratch[8:]
    a_sums, scratch = scratch[:4], scratch[4:]
    a_second, f_second = scratch[:9], scratch[9:]
    here = Place()
    wire = Wire(send, recv, local)
    d_copy, wo_copy = wire.stay(d_in, d_all), wire.stay(wo_in, wo)
    kv_copy, wq_copy, h1_copy = wire.stay(kv_in, kv_all), wire.stay(wq_in, wq), wire.stay(h1_in, h1_all)
    greet(
        [here.in_row(s) for s in range(1, 8)]
        + ring_partners(here)
        + [here.at(dz=1), here.at(dz=-1), here.at(dx=2)]
        + [here.in_dp(s) for s in range(1, 4)]
    )
    f_flows = second_sums(wire, here, f_sums, f_second, *FEED)
    for flow in f_flows:
        next(flow)
    branch_sum = x_sum(wire, here, f_part, far, near, summed)
    next(branch_sum)
    heads_swap = wire.copy(heads.at[:, columns(1 - here.core)], heads_in, here.pair())
    wire.there(d_copy, wo_copy)

    @pl.loop(0, 2)
    def _(n):
        dout[:, columns(n)] = dot(tokens_of(d_all), wo[:, columns(n)]).astype(BF)

    for flow in f_flows:
        next(flow)
    next(branch_sum)
    wire.there(kv_copy)
    attend_back(here, q, kv_all, table, log_total, dout, dq, total)
    dkv[...] = total[...].astype(BF)
    side_by_side(*f_flows)
    f_share = grad_share(wire, here, f_second[-1], fout, FEED[0])
    next(f_share)
    pick = lambda h, i: [dkv.at[key_block(2 * h + n, i)] for n in range(2)]
    keys = ring_sum(
        wire,
        here.y,
        here.at(dy=1),
        here.at(dy=-1),
        lambda i, h: pick(h, i),
        lambda h: [kfar.at[h, n] for n in range(2)],
        lambda s, h: [knear.at[s, h, n] for n in range(2)],
        lambda h: [dkv_own.at[pl.ds(128 * (2 * h + n), 128)] for n in range(2)],
    )
    next(keys)
    side_by_side(branch_sum, f_share)
    narrowed(osend, (summed[...] + rise[...]).astype(BF))
    for c in range(4):
        at = pl.ds(128 * c, 128)
        turn = cosine[at], -sine[at]
        second = turned(dq[at, 256:512], *turn)
        both = packed_pair(turned(dq[at, 0:256], *turn), pltpu.roll(second, 64, 1))
        dqkv[at, 0:384] = both.astype(BF)
    next(keys)
    wire.arrive(heads_swap)
    weight_grads(
        d_all, (heads, columns(here.core)), (heads_in, slice(None)), main, rest, slice(384, 640)
    )
    side_by_side(keys)
    lane = lax.broadcasted_iota(jnp.int32, (128, 256), 1)
    for c in range(4):
        at = pl.ds(128 * c, 128)
        key = turned(dkv_own[at, 0:256], cosine[at], -sine[at])
        value = jnp.where(lane < 64, 0.0, dkv_own[at, 128:384])
        dqkv[at, 384:768] = packed_pair(key, value).astype(BF)
    dqkv_swap = wire.copy(dqkv.at[:, columns(1 - here.core, 384)], dqkv_in, here.pair())
    wire.there(wq_copy)
    back_to_width(dqkv, slice(None), wq, slice(None), part)

    def chain():
        yield from x_sum(wire, here, part, far2, near2, summed)
        left, gain_terms = norm_back(xtok[...].astype(F32), summed[...], gtok[0:1])
        gains = jnp.concatenate([gain_terms, gain[0:1], jnp.zeros((6, D), F32)], axis=0)
        narrowed(gsend, gains)
        g = swap_rows(wire, here, gsend, grow)
        narrowed(ssend, (left + after[...]).astype(BF))
        wire.stay(ssend.at[here.row], s_all.at[here.row])
        swap_rows(wire, here, ssend, s_all)
        yield
        wire.arrive(*g)
        grow[here.row] = gsend[here.row]
        total = grow[0]
        for n in range(1, 8):
            total = total + grow[n]
        gcol[here.x] = total
        g = [wire.copy(gcol.at[here.x], gcol.at[here.x], here.at(dx=s)) for s in range(1, 4)]
        yield
        wire.arrive(*g)
        gdp[here.dp] = ((gcol[0] + gcol[1]) + gcol[2]) + gcol[3]
        g = [wire.copy(gdp.at[here.dp], gdp.at[here.dp], here.in_dp(s)) for s in range(1, 4)]
        yield
        wire.arrive(*g)
        gains_out[...] = ((gdp[0] + gdp[1]) + gdp[2]) + gdp[3]

    steps = chain()
    next(steps)
    wire.stay(osend.at[here.row], o_all.at[here.row])
    swap_rows(wire, here, osend, o_all)
    wire.there(h1_copy)
    wire.arrive(dqkv_swap)
    weight_grads(
        h1_all, (dqkv, columns(here.core, 384)), (dqkv_in, slice(None)), main, rest, slice(0, 384)
    )
    first = first_sums(wire, here, (main, rest), a_first, a_sums, *ATTN)

    def sums():
        yield
        side_by_side(*first)
        second = second_sums(wire, here, a_sums, a_second, *ATTN)
        for flow in second:
            next(flow)
        yield
        for flow in second:
            next(flow)
        yield
        side_by_side(*second)
        yield from grad_share(wire, here, a_second[-1], gout, ATTN[0])

    for flow in first:
        next(flow)
    for flow in first:
        next(flow)
    side_by_side(steps, sums())
    wire.finish()


def leave(*operands):
    return pl.pallas_call(
        leave_kernel,
        out_shape=[
            shape(BF, 8, 128, 256),
            shape(BF, 8, 128, 256),
            shape(BF, 2, 96, 2 * ATTN[0]),
            shape(BF, 2, 96, 2 * FEED[0]),
            shape(F32, 8, 256),
        ],
        in_specs=[VM] * 16 + [ANY] * 5,
        out_specs=[ANY] * 4 + [VM],
        scratch_shapes=[
            pltpu.VMEM((8, 128, D), BF),
            pltpu.VMEM((D, 768), BF),
            pltpu.VMEM((D, 512), BF),
            pltpu.VMEM((16, 128, 384), BF),
            pltpu.VMEM((8, 128, D), BF),
            pltpu.VMEM((512, 512), BF),
            pltpu.VMEM((512, 512), F32),
            pltpu.VMEM((16, 128, 384), F32),
            pltpu.VMEM((16, 128, 384), BF),
            pltpu.VMEM((2, 2, 128, 384), BF),
            pltpu.VMEM((2, 2, 2, 128, 384), BF),
            pltpu.VMEM((512, 384), F32),
            pltpu.VMEM((512, 768), BF),
            pltpu.VMEM((512, 256), BF),
            pltpu.VMEM((512, 384), BF),
            pltpu.VMEM((4, 128, D), BF),
        ]
        + x_sum_scratch()
        + x_sum_scratch()
        + [
            pltpu.VMEM((128, D), F32),
            pltpu.VMEM((8, 128, 256), BF),
            pltpu.VMEM((8, 128, 256), BF),
            pltpu.VMEM((8, 8, 256), F32),
            pltpu.VMEM((8, 8, 256), F32),
            pltpu.VMEM((4, 8, 256), F32),
            pltpu.VMEM((4, 8, 256), F32),
        ]
        + grad_arrays(ATTN[0])
        + first_scratch(*ATTN)
        + [pltpu.VMEM(sizes, BF) for sizes in half_sums(*ATTN)]
        + second_scratch(*ATTN)
        + second_scratch(*FEED)
        + signals(160, 160, 12),
        compiler_params=settings(3),
        name="leave",
    )(*operands)


def step_rates():
    return (2.0 / D**0.5, 2.0 / max(HQ * HS // 64, 1) ** 0.5, 2.0 / D**0.5, 2.0 / FF**0.5, 0.4)


def adamw(state, at, gradient, step_rate, decay_rate):
    weight, first, second = state
    moment_one = beta_first * first[at] + (1.0 - beta_first) * gradient
    moment_two = beta_second * second[at] + (1.0 - beta_second) * gradient * gradient
    first[at] = moment_one
    second[at] = moment_two
    corrected = (moment_one * (1.0 / (1.0 - beta_first**STEP))) / (
        jnp.sqrt(moment_two * (1.0 / (1.0 - beta_second**STEP))) + adam_epsilon
    )
    old = weight[at]
    weight[at] = old - step_rate * (corrected + decay_rate * old)


def update_kernel(*refs):
    stream, cotangent, o_in, s_in, g_in, f_in, qkv_at, out_at = refs[:8]
    qkv, out, gate_up, down, gains = (refs[8 + 3 * n : 11 + 3 * n] for n in range(5))
    gains_tile = refs[23]
    o_out, s_out = refs[24:26]
    results = [refs[26 + 3 * n : 29 + 3 * n] for n in range(5)]
    xf, cf, ot, st, gb, fb, qs, os = refs[41:49]
    qkv_s, out_s, gate_s, down_s = (refs[49 + 3 * n : 52 + 3 * n] for n in range(4))
    local = refs[61]
    here = Place()
    wire = Wire(None, None, local)
    rate_qkv, rate_out, rate_gate_up, rate_down, rate_gains = step_rates()

    f_load = [wire.stay(f_in, fb)]
    for a, b in zip(gate_up, gate_s):
        f_load += [wire.stay(a.at[:, j], b.at[j]) for j in range(2)]
    d_load = [wire.stay(a, b) for a, b in zip(down, down_s)]
    x_load = [wire.stay(a, b) for a, b in ((stream, xf), (o_in, ot), (cotangent, cf), (s_in, st))]
    a_load = [wire.stay(a, b) for a, b in ((g_in, gb), (qkv_at, qs), (out_at, os))]
    a_load += [wire.stay(a, b) for a, b in zip(qkv + out, qkv_s + out_s)]

    def feed_part(states, first):
        @pl.loop(0, 4)
        def _(n):
            zh, k = lax.div(n, 2), lax.rem(n, 2)
            for start, size, begin in ((0, 64, 64 * zh), (64, 32, 128 + 32 * zh)):
                at = pl.ds(pl.multiple_of(begin, 32), size), columns(k, 512)
                for a, (state, rate) in enumerate(states):
                    lanes = pl.ds(pl.multiple_of(1536 * k + 512 * (first + a), 512), 512)
                    gradient = fb[zh, start : start + size, lanes].astype(F32)
                    adamw(state, at, gradient, rate, weight_decay)

    wire.there(*f_load)
    feed_part([([b.at[j] for b in gate_s], rate_gate_up) for j in range(2)], 0)
    for a, b in zip(results[2], gate_s):
        for j in range(2):
            wire.stay(b.at[j], a.at[:, j])
    wire.there(*d_load)
    feed_part([(down_s, rate_down)], 2)
    for a, b in zip(results[3], down_s):
        wire.stay(b, a)

    wire.there(*x_load)
    for held, tiles, result in ((xf, ot, o_out), (cf, st, s_out)):
        for y in range(4):
            for zl in range(2):
                tile = tiles[2 * y + zl].astype(F32).T
                rest = jnp.where(here.zl == 0, tile[128:192], tile[192:256])
                at = pl.ds(128 * y, 128)
                held[zl, 0:128, at] = held[zl, 0:128, at] + tile[0:128]
                held[zl, 128:192, at] = held[zl, 128:192, at] + rest
        wire.stay(held, result)

    wire.there(*a_load)

    def own_block(start, size):
        lanes = [pl.ds(ATTN[0] * k + start, size) for k in range(2)]
        parts = [(0, slice(0, 64)), (1, slice(0, 64)), (0, slice(64, 96)), (1, slice(64, 96))]
        return jnp.concatenate(
            [jnp.concatenate([gb[zh, at, l] for zh, at in parts], axis=0) for l in lanes], axis=1
        )

    gradient = dot(own_block(0, 384), qs[...])
    adamw(qkv_s, (slice(None), slice(None)), gradient, rate_qkv, weight_decay)
    gradient = dot(own_block(384, 256), os[...])
    adamw(out_s, (slice(None), slice(None)), gradient, rate_out, weight_decay)
    for a, b in zip(results[0] + results[1], qkv_s + out_s):
        wire.stay(b, a)

    tile = gains_tile[...]
    rest = own_half(here, tile[:, 128:])
    for old, new in zip(gains, results[4]):
        new[...] = old[...]
    adamw(results[4], (slice(None), slice(0, 128)), tile[0:2, 0:128], rate_gains, 0.0)
    adamw(results[4], (slice(None), slice(128, 192)), rest[0:2, 0:64], rate_gains, 0.0)
    wire.finish()


def update(*operands):
    sizes = [(192, 768)] * 3 + [(192, 384)] * 3 + [(192, 2, 1024)] * 3 + [(192, 1024)] * 3
    held = [(192, 768)] * 3 + [(192, 384)] * 3 + [(2, 192, 1024)] * 3 + [(192, 1024)] * 3
    return pl.pallas_call(
        update_kernel,
        out_shape=[shape(F32, 2, 192, 512)] * 2
        + [shape(F32, *size) for size in sizes]
        + [shape(F32, 2, 192)] * 3,
        in_specs=[ANY] * 20 + [VM] * 4,
        out_specs=[ANY] * 14 + [VM] * 3,
        scratch_shapes=[
            pltpu.VMEM((2, 192, 512), F32),
            pltpu.VMEM((2, 192, 512), F32),
            pltpu.VMEM((8, 128, 256), BF),
            pltpu.VMEM((8, 128, 256), BF),
            pltpu.VMEM((2, 96, 2 * ATTN[0]), BF),
            pltpu.VMEM((2, 96, 2 * FEED[0]), BF),
            pltpu.VMEM((768, 768), BF),
            pltpu.VMEM((512, 384), BF),
        ]
        + [pltpu.VMEM(size, F32) for size in held]
        + signals(64),
        compiler_params=pltpu.CompilerParams(vmem_limit_bytes=60 << 20),
        name="update",
    )(*operands)


def body(
    stream,
    cotangent,
    segments,
    positions,
    qkv_weight,
    qkv_first,
    qkv_second,
    out_weight,
    out_first,
    out_second,
    gate_up_weight,
    gate_up_first,
    gate_up_second,
    down_weight,
    down_first,
    down_second,
    gains,
    gains_first,
    gains_second,
):
    frequency = rope_theta ** (-2.0 * (jnp.arange(256) % (HS // 2)).astype(F32) / HS)
    frequency = jnp.broadcast_to(frequency, (8, 256))
    qkv_at, out_at = qkv_order(), out_order()
    stream_turned, cotangent_turned = stream.transpose(1, 2, 0), cotangent.transpose(1, 2, 0)
    (
        part, h1_all, wq, wo, c_all, kv_all, second_weights,
        q, heads, log_total, cosine, sine, xtok, ctok, gtok, table,
    ) = enter(
        stream_turned, cotangent_turned, qkv_weight, out_weight.T, gate_up_weight, down_weight.T,
        gains, positions, frequency, qkv_at, out_at,
    )
    after, gain_two, rise, f_part, d_all, *sums = feed(
        part, xtok, gtok, ctok, second_weights, c_all
    )
    o_tiles, s_tiles, attn_grads, feed_grads, gains_tile = leave(
        f_part, rise, xtok, after, gtok, gain_two, q, heads, log_total, table, cosine, sine,
        *sums, d_all, wq, wo, kv_all, h1_all,
    )
    made = update(
        stream_turned, cotangent_turned, o_tiles, s_tiles, attn_grads, feed_grads, qkv_at, out_at,
        qkv_weight, qkv_first, qkv_second,
        out_weight.T, out_first.T, out_second.T,
        gate_up_weight, gate_up_first, gate_up_second,
        down_weight.T, down_first.T, down_second.T,
        gains, gains_first, gains_second,
        gains_tile,
    )
    output, stream_grad = made[0].transpose(2, 0, 1), made[1].transpose(2, 0, 1)
    states = [made[2 + 3 * n : 5 + 3 * n] for n in range(5)]
    for n in (1, 3):
        states[n] = [a.T for a in states[n]]
    return (output, stream_grad, *(a for w, m, v in states for a in (m, v, w)))


def solution(mesh):
    tokens = P("col", "dp", "row")
    table = P("dp", None)
    wide, tall, pairs, both = P("row", "col"), P("col", "row"), P("row", None, "col"), P(None, "row")
    weights = (wide,) * 3 + (tall,) * 3 + (pairs,) * 3 + (tall,) * 3 + (both,) * 3
    return jax.shard_map(
        body,
        mesh=mesh,
        in_specs=(tokens, tokens, table, table, *weights),
        out_specs=(tokens, tokens, *weights),
        check_vma=False,
    )
```

```python
import functools

import jax
import jax.numpy as jnp
import numpy as np
from jax import lax
from jax.experimental import pallas as pl
from jax.experimental.pallas import tpu as pltpu
from jax.sharding import PartitionSpec as P

D = 1536
FF = 4096
HQ = 16
KVH = 8
HS = 96
STEP = 10
LEN = 2048
WINDOW = 1024

norm_epsilon = 1e-05
rope_theta = 100000.0
beta_first = 0.9
beta_second = 0.95
adam_epsilon = 1e-08
weight_decay = 0.1
score_scale = HS**-0.5

MESH = pl.DeviceIdType.MESH
BF = jnp.bfloat16
F32 = jnp.float32
VM = pl.BlockSpec(memory_space=pltpu.VMEM)
ANY = pl.BlockSpec(memory_space=pl.ANY)


def selection(source, count):
    chosen = np.zeros((count, len(source)), np.float32)
    chosen[source, np.arange(len(source))] = 1.0
    return jnp.asarray(chosen, BF)


def qkv_order():
    b = np.arange(768)
    return selection(b % 384 // HS * 192 + b // 384 * HS + b % HS, 768)


def out_order():
    b = np.arange(384)
    return selection(b % 192 // HS * 256 + 64 + b // 192 * HS + b % HS, 512)


class Place:
    def __init__(self):
        self.dp = lax.axis_index("dp")
        self.row = lax.axis_index("row")
        self.x = lax.axis_index("col")
        self.zh = lax.div(self.dp, 2)
        self.core = lax.rem(self.dp, 2)
        self.y = lax.div(self.row, 2)
        self.zl = lax.rem(self.row, 2)
        self.z = self.zh * 2 + self.zl

    def at(self, dx=0, dy=0, dz=0, dcore=0):
        x = lax.rem(self.x + (dx + 4), 4)
        y = lax.rem(self.y + (dy + 4), 4)
        z = lax.rem(self.z + (dz + 4), 4)
        core = lax.rem(self.core + dcore, 2)
        return (lax.div(z, 2) * 2 + core, y * 2 + lax.rem(z, 2), x)

    def pair(self):
        return self.at(dcore=1)

    def in_row(self, step):
        return (self.dp, lax.rem(self.row + step, 8), self.x)

    def in_dp(self, step):
        return (lax.rem(self.dp + step, 4), self.row, self.x)


def greet(devices):
    barrier = pltpu.get_barrier_semaphore()
    for device in devices:
        pl.semaphore_signal(barrier, inc=1, device_id=device, device_id_type=MESH)
    pl.semaphore_wait(barrier, len(devices))


class Wire:
    def __init__(self, send, recv, local=None):
        self.send, self.recv, self.local = send, recv, local
        self.sent, self.open, self.near, self.stays = [], {}, [], 0

    def copy(self, src, dst, device):
        n = len(self.sent)
        made = pltpu.make_async_remote_copy(
            src_ref=src,
            dst_ref=dst,
            send_sem=self.send.at[n],
            recv_sem=self.recv.at[n],
            device_id=device,
            device_id_type=MESH,
        )
        made.start()
        self.sent.append(made)
        self.open[n] = made
        return n

    def arrive(self, *numbers):
        for n in numbers:
            self.open.pop(n).wait_recv()

    def stay(self, src, dst):
        made = pltpu.make_async_copy(src, dst, self.local.at[self.stays])
        self.stays += 1
        made.start()
        self.near.append(made)
        return made

    def there(self, *stays):
        for made in stays:
            self.near = [other for other in self.near if other is not made]
            made.wait()

    def settle(self):
        self.arrive(*list(self.open))

    def finish(self):
        self.settle()
        for made in self.sent:
            made.wait_send()
        self.there(*list(self.near))


def around(me):
    return lax.rem(me + 3, 4), lax.rem(me + 1, 4), lax.rem(me + 2, 4)


def ring_gather(wire, me, right, left, own, slot):
    l, r, o = around(me)

    def send(src, dst, device):
        return [wire.copy(a, b, device) for a, b in zip(src, dst)]

    def pass_on(numbers, refs, device):
        passed = []
        for n, ref in zip(numbers, refs):
            wire.arrive(n)
            passed.append(wire.copy(ref, ref, device))
        return passed

    first = send(own(0), slot(me, 0), right), send(own(1), slot(me, 1), left)
    second = send(own(1), slot(me, 1), right), send(own(0), slot(me, 0), left)
    yield
    far = pass_on(first[0], slot(l, 0), right) + pass_on(first[1], slot(r, 1), left)
    yield
    wire.arrive(*second[0], *second[1])
    yield
    wire.arrive(*far)


def leading(ref):
    found = [()]
    for size in ref.shape[:-2]:
        found = [index + (n,) for index in found for n in range(size)]
    return found


def add_parts(out, refs):
    for index in leading(out):
        at = index + (slice(None), slice(None))
        total = refs[0][at].astype(F32)
        for ref in refs[1:]:
            total = total + ref[at].astype(F32)
        out[at] = total.astype(out.dtype)


def ring_sum(wire, me, right, left, part, far, near, out):
    l, r, o = around(me)

    def send(srcs, dsts, device):
        return [wire.copy(a, b, device) for a, b in zip(srcs, dsts)]

    far0 = send(part(o, 0), far(0), right)
    far1 = send(part(o, 1), far(1), left)
    to_right = send(part(r, 1), near(0, 1), right)
    to_left = send(part(l, 0), near(1, 0), left)
    yield
    for n, a, b, c in zip(far0, far(0), part(r, 0), near(0, 0)):
        wire.arrive(n)
        add_parts(a, [a, b])
        to_right.append(wire.copy(a, c, right))
    for n, a, b, c in zip(far1, far(1), part(l, 1), near(1, 1)):
        wire.arrive(n)
        add_parts(a, [a, b])
        to_left.append(wire.copy(a, c, left))
    yield
    wire.arrive(*to_right, *to_left)
    for h in range(2):
        for a, b, c, total in zip(part(me, h), near(0, h), near(1, h), out(h)):
            add_parts(total, [a, b, c])


def side_by_side(*flows):
    flows = list(flows)
    while flows:
        for flow in list(flows):
            try:
                next(flow)
            except StopIteration:
                flows.remove(flow)


def rows(ref, start, size, multiple):
    return ref.at[pl.ds(pl.multiple_of(start, multiple), size)]


def weight_gather(wire, here, own, whole):
    core, zl = here.core, here.zl
    right, left = here.at(dy=1), here.at(dy=-1)
    up, down = here.at(dz=1), here.at(dz=-1)
    l, r, o = around(here.y)

    def mine(j):
        start = (core * 64, core * 64 + 32, 128 + core * 32, 144 + core * 32)[j]
        return rows(own, start, (32, 32, 16, 16)[j], 16)

    def piece(y, j, lo):
        block = y * 2 + lo
        main, rest = block * 128 + core * 64, 1024 + block * 64 + core * 32
        start = (main, main + 32, rest, rest + 16)[j]
        return rows(whole, start, (32, 32, 16, 16)[j], 16)

    def to_pair(y, lo):
        block = y * 2 + lo
        for view in (
            rows(whole, block * 128 + core * 64, 64, 64),
            rows(whole, 1024 + block * 64 + core * 32, 32, 32),
        ):
            paired.append(wire.copy(view, view, here.pair()))

    paired = []

    def over(y, js, device, src=None):
        return [wire.copy((src or (lambda j: piece(y, j, zl)))(j), piece(y, j, zl), device) for j in js]

    y = here.y
    kept = (
        wire.stay(own.at[pl.ds(0, 128)], rows(whole, here.row * 128, 128, 128)),
        wire.stay(own.at[pl.ds(128, 64)], rows(whole, 1024 + here.row * 64, 64, 64)),
    )
    r_first, l_first = over(y, (0, 2), right, mine), over(y, (1, 3), left, mine)
    r_next, l_next = over(y, (1, 3), right, mine), over(y, (0, 2), left, mine)
    z_own = over(y, (0, 2), up, mine) + over(y, (1, 3), down, mine)
    yield
    wire.arrive(*r_first)
    far = over(l, (0, 2), right)
    wire.arrive(*l_first)
    far += over(r, (1, 3), left)
    z_l = over(l, (0, 2), up)
    z_r = over(r, (1, 3), down)
    yield
    wire.arrive(*r_next)
    z_l += over(l, (1, 3), down)
    to_pair(l, zl)
    wire.arrive(*l_next)
    z_r += over(r, (0, 2), up)
    to_pair(r, zl)
    yield
    wire.arrive(*far)
    z_o = over(o, (0, 2), up) + over(o, (1, 3), down)
    to_pair(o, zl)
    yield
    for block, numbers in ((y, z_own), (l, z_l), (r, z_r), (o, z_o)):
        wire.arrive(*numbers)
        to_pair(block, 1 - zl)
        yield
    wire.arrive(*paired)
    wire.there(*kept)


def token_pieces(half):
    return [pl.ds(64 * half + n, 32) for n in (0, 32)]


def share(wire, here, out):
    half = lambda i, h: [out.at[i, at] for at in token_pieces(h)]
    return ring_gather(
        wire, here.x, here.at(dx=1), here.at(dx=-1), lambda h: half(here.x, h), half
    )


def to_pair(wire, here, out):
    return wire.copy(out.at[pl.ds(0, 4)], out.at[pl.ds(4, 4)], here.pair())


def x_sum(wire, here, part, far, near, out):
    at = token_pieces
    return ring_sum(
        wire,
        here.x,
        here.at(dx=1),
        here.at(dx=-1),
        lambda i, h: [part.at[i, n] for n in at(h)],
        lambda h: [far.at[n] for n in at(h)],
        lambda s, h: [near.at[s, n] for n in at(h)],
        lambda h: [out.at[n] for n in at(h)],
    )


def x_sum_scratch():
    return [pltpu.VMEM((128, D), BF), pltpu.VMEM((2, 128, D), BF)]


HIGHS = (64, 32)


def order_columns(width, cut, order):
    return (0, cut) if order == 0 else (cut, width - cut)


def first_scratch(width, cut):
    shapes = []
    for order in range(2):
        size = order_columns(width, cut, order)[1]
        for high in HIGHS:
            shapes += [
                pltpu.VMEM((2, 2, high, size), BF),
                pltpu.VMEM((2, 2, 2, high, size), BF),
            ]
    return shapes


def half_sums(width, cut):
    return [
        (2, 2, high, order_columns(width, cut, order)[1]) for order in range(2) for high in HIGHS
    ]


def second_scratch(width, cut):
    shapes = []
    for order in range(2):
        size = order_columns(width, cut, order)[1]
        for high in HIGHS:
            shapes += [
                pltpu.VMEM((2, high // 2, size), BF),
                pltpu.VMEM((2, 2, high // 2, size), BF),
            ]
    return shapes + [pltpu.VMEM((96, width), BF)]


def rings(here):
    y_ring = (here.y, here.at(dy=1), here.at(dy=-1))
    z_ring = (here.z, here.at(dz=1), here.at(dz=-1))
    return y_ring, z_ring


def first_sums(wire, here, grads, scratch, sums, width, cut):
    def flow(order):
        at = pl.ds(*order_columns(width, cut, order))
        buffers, out = scratch[4 * order : 4 * order + 4], sums[2 * order : 2 * order + 2]

        def of_z(ref, i, h):
            return ref.at[pl.ds(2 * h, 2), lax.rem(i, 2), lax.div(i, 2), :, at]

        def of_y(ref, i, h):
            return ref.at[i, h, :, :, at]

        pick = of_z if order == 0 else of_y
        return ring_sum(
            wire,
            *rings(here)[1 - order],
            lambda i, h: [pick(g, i, h) for g in grads],
            lambda h: [b.at[h] for b in buffers[0::2]],
            lambda s, h: [b.at[s, h] for b in buffers[1::2]],
            lambda h: [b.at[h] for b in out],
        )

    return flow(0), flow(1)


def second_sums(wire, here, sums, scratch, width, cut):
    fin = scratch[-1]

    def flow(order):
        at = pl.ds(*order_columns(width, cut, order))
        buffers, terms = scratch[4 * order : 4 * order + 4], sums[2 * order : 2 * order + 2]

        def part(i, h):
            high, low = lax.div(i, 2), lax.rem(i, 2)
            lead = (high, low) if order == 0 else (low, high)
            return [
                b.at[lead[0], lead[1], pl.ds(tall // 2 * h, tall // 2)]
                for b, tall in zip(terms, HIGHS)
            ]

        return ring_sum(
            wire,
            *rings(here)[order],
            part,
            lambda h: [b.at[h] for b in buffers[0::2]],
            lambda s, h: [b.at[s, h] for b in buffers[1::2]],
            lambda h: [
                fin.at[pl.ds(start + tall // 2 * h, tall // 2), at]
                for start, tall in zip((0, 64), HIGHS)
            ],
        )

    return flow(0), flow(1)


def grad_share(wire, here, fin, out, width):
    columns = pl.ds(pl.multiple_of(here.core * width, 128), width)
    mine = out.at[here.zh, :, columns]
    other = out.at[1 - here.zh, :, columns]
    wire.stay(fin, mine)
    wire.copy(fin, mine, here.pair())
    n = wire.copy(fin, mine, here.at(dz=2))
    yield
    wire.arrive(n)
    wire.copy(other, other, here.pair())


def swap_rows(wire, here, src, dst):
    return [
        wire.copy(src.at[lax.rem(here.row + s, 8)], dst.at[here.row], here.in_row(s))
        for s in range(1, 8)
    ]


def low_lanes(rows):
    return lax.broadcasted_iota(jnp.int32, (rows, 128), 1) < 64


def widened(ref):
    main = [ref[r, 0:128, :] for r in range(8)]
    rest = []
    for j in range(4):
        even, odd = ref[2 * j, 128:192, :].astype(F32), ref[2 * j + 1, 128:192, :].astype(F32)
        top = jnp.where(low_lanes(64), even, odd)
        bottom = pltpu.roll(jnp.where(low_lanes(64), odd, even), 64, 1)
        rest.append(jnp.concatenate([top, bottom], axis=0).astype(BF))
    return jnp.concatenate(main + rest, axis=1)


def widened_rows(ref, start, size):
    main = [ref[r, start : start + size, :] for r in range(8)]
    after = slice(start + size, start + 2 * size)
    rest = [ref[2 * j, after, :] + ref[2 * j + 1, after, :] for j in range(4)]
    return jnp.concatenate(main + rest, axis=1)


def narrowed(out, value):
    for r in range(8):
        out[r, 0:128, :] = value[:, 128 * r : 128 * r + 128].astype(BF)
        j = 1024 + 128 * (r // 2)
        top, bottom = value[0:64, j : j + 128], value[64:128, j : j + 128]
        if r % 2 == 0:
            rest = jnp.where(low_lanes(64), top, pltpu.roll(bottom, 64, 1))
        else:
            rest = jnp.where(low_lanes(64), pltpu.roll(top, 64, 1), bottom)
        out[r, 128:192, :] = rest.astype(BF)


def narrowed_rows(out, value):
    for r in range(8):
        out[r, :, 0:128] = value[:, 128 * r : 128 * r + 128]
        j = 1024 + 128 * (r // 2)
        out[r, :, 128:256] = value[:, j : j + 128]


def ring_partners(here):
    return [here.at(dx=1), here.at(dx=-1)]


def plane_partners(here):
    return [here.at(dy=1), here.at(dy=-1), here.at(dz=1), here.at(dz=-1)]


def dot(a, b, left=1, right=0):
    return lax.dot_general(a, b, (((left,), (right,)), ((), ())), preferred_element_type=F32)


def turned(values, cosine, sine):
    lane = lax.broadcasted_iota(jnp.int32, values.shape, 1)
    front = lax.rem(lane, HS) < HS // 2
    ahead, back = pltpu.roll(values, 256 - HS // 2, 1), pltpu.roll(values, HS // 2, 1)
    return values * cosine + jnp.where(front, -ahead, back) * sine


def packed_pair(a, b):
    return jnp.concatenate([a[:, :128], a[:, 128:] + b[:, :128], b[:, 128:]], axis=1)


def windows(y):
    return ((0, 4), (0, 8), (1 + y, 8), (5 + y, 8))


def allowed_keys(table, c, start, count):
    key = start * 128 + lax.broadcasted_iota(jnp.int32, (count * 128, 256), 0)
    return (key >= table[2 * c : 2 * c + 1]) & (key <= table[2 * c + 1 : 2 * c + 2])


def both_heads(ref, at):
    return jnp.concatenate([ref[at, 0:256], ref[at, 256:512]], axis=0)


def attend(here, q, kv, table, heads, log_total):
    lane = lax.broadcasted_iota(jnp.int32, (256, 256), 1)
    for c, (start, count) in enumerate(windows(here.y)):
        at = pl.ds(128 * c, 128)
        allowed = allowed_keys(table, c, start, count)
        q_both = both_heads(q, at)
        k = kv[pl.ds(start, count), :, 0:256].reshape(count * 128, 256)
        v = kv[pl.ds(start, count), :, 128:384].reshape(count * 128, 256)
        made = []
        for g in range(2):
            n = 2 * c + g
            q_one = jnp.where((lane >= HS) == (g == 1), q_both, jnp.zeros_like(q_both))
            scores = dot(k, q_one, 1, 1) * score_scale
            scores = jnp.where(allowed, scores, -1e30)
            top = jnp.max(scores, axis=0, keepdims=True)
            weights = jnp.exp(scores - top)
            total = jnp.sum(weights, axis=0, keepdims=True)
            shares = (weights * (1.0 / total)).astype(BF)
            made.append(dot(shares, v, 0, 0))
            log_total[n : n + 1] = top + jnp.log(total)
        out = jnp.where(lane < 64 + HS, made[0], made[1])
        out = jnp.where(lane < 64, 0.0, out).astype(BF)
        heads[at, 0:256] = out[:128]
        heads[at, 256:512] = out[128:]
        yield


def attend_back(here, q, kv, table, log_total, dout, dq, total):
    lane = lax.broadcasted_iota(jnp.int32, (256, 256), 1)
    total[...] = jnp.zeros_like(total)
    for c, (start, count) in reversed(list(enumerate(windows(here.y)))):
        at = pl.ds(128 * c, 128)
        blocks = pl.ds(start, count)
        allowed = allowed_keys(table, c, start, count)
        q_both, d_both = both_heads(q, at), both_heads(dout, at)
        k = kv[blocks, :, 0:256].reshape(count * 128, 256)
        v = kv[blocks, :, 128:384].reshape(count * 128, 256)
        made = []
        for g in range(2):
            n = 2 * c + g
            q_one = jnp.where((lane >= HS) == (g == 1), q_both, jnp.zeros_like(q_both))
            d_one = jnp.where((lane >= 64 + HS) == (g == 1), d_both, jnp.zeros_like(d_both))
            scores = dot(k, q_one, 1, 1) * score_scale
            shares = jnp.where(allowed, jnp.exp(scores - log_total[n : n + 1]), 0.0)
            dshares = dot(v, d_one, 1, 1)
            inner = jnp.sum(shares * dshares, axis=0, keepdims=True)
            dscores = (shares * (dshares - inner)).astype(BF)
            made.append(dot(dscores, k, 0, 0))
            dk = dot(dscores, q_one) * score_scale
            dv = dot(shares.astype(BF), d_one)
            total[blocks, :, 0:256] += dk.reshape(count, 128, 256)
            total[blocks, :, 128:384] += dv.reshape(count, 128, 256)
        out = jnp.where(lane < HS, made[0], made[1]) * score_scale
        dq[at, 0:256] = out[:128]
        dq[at, 256:512] = out[128:]
        yield


def tokens_of(ref, pair=0):
    return ref[4 * pair : 4 * pair + 4].reshape(512, D)


def columns(n, size=256):
    return pl.ds(pl.multiple_of(n * size, size), size)


def back_to_width(units, weights, out, token_at=slice(None)):
    @pl.loop(0, D // 256)
    def _(n):
        made = dot(units(), weights[columns(n), :], 1, 1)
        out[:, token_at, columns(n)] = made.astype(BF).reshape(4, made.shape[0] // 4, 256)


def weight_grads(tokens, own, pair, main, rest, at):
    def made(n):
        total = dot(tokens[0:4, :, columns(n)].reshape(512, 256), own(), 0, 0)
        return total + dot(tokens[4:8, :, columns(n)].reshape(512, 256), pair(), 0, 0)

    @pl.loop(0, 4)
    def _(n):
        value = made(n)
        main[n, :, :, :, at] = value.astype(BF).reshape(2, 2, 64, value.shape[1])

    @pl.loop(0, 2)
    def _(n):
        value = made(n + 4)
        rest[pl.ds(2 * n, 2), :, :, :, at] = value.astype(BF).reshape(2, 2, 2, 32, value.shape[1])


def norm_back(value, grad, gain):
    scale = lax.rsqrt(jnp.mean(value * value, axis=1, keepdims=True) + norm_epsilon)
    unit = value * scale
    scaled = grad * gain
    inner = jnp.mean(scaled * unit, axis=1, keepdims=True)
    return scale * (scaled - unit * inner), jnp.sum(grad * unit, axis=0, keepdims=True)


def normed(value, gain):
    scale = lax.rsqrt(jnp.mean(value * value, axis=1, keepdims=True) + norm_epsilon)
    return (value * scale * gain).astype(BF)


def key_block(c, y):
    return 4 * c + y


def pack_rows(here, out, values):
    for y in range(4):
        for zl in range(2):
            block = values[zl, :, 128 * y : 128 * y + 128]
            rest = block[128:]
            swapped = pltpu.roll(rest, 64, 1)
            first = jnp.where(here.zl == 0, rest, swapped)
            second = jnp.where(here.zl == 0, swapped, rest)
            out[2 * y + zl, 0:128, :] = block[:128].T.astype(BF)
            both = jnp.concatenate([first, second], axis=0).T
            out[2 * y + zl, 128:192, :] = both[0:64].astype(BF)


def own_half(here, rest):
    return jnp.where(here.zl == 0, rest, pltpu.roll(rest, 64, 1))


def enter_kernel(
    stream, cotangent, qkv_weight, out_weight, gate_up, down, gains, positions, frequency, qkv_at, out_at,
    h1_out, wq_out, wo_out, c_out, kv_out, down_out, w_both, rise, h2_own,
    q, heads, log_total, cosine, sine, xtok, ctok, gtok, table,
    xf, cf, qf, of, gf, df, qs, os, xin, cin, wq_own, wo_own, win,
    xbuf, cbuf, h1_all, c_all, wq, wo, part, far, near, kv_own, kv_all, qkv, gpad, send, recv, local,
):
    here = Place()
    wire = Wire(send, recv, local)
    x_load = wire.stay(stream, xf)
    q_load = wire.stay(qkv_weight, qf), wire.stay(qkv_at, qs)
    o_load = wire.stay(out_weight, of), wire.stay(out_at, os)
    c_load = wire.stay(cotangent, cf)
    f_load = [wire.stay(gate_up.at[:, j], gf.at[j]) for j in range(2)] + [wire.stay(down, df)]
    greet(
        [here.in_row(s) for s in range(1, 8)]
        + ring_partners(here)
        + [here.at(dz=1), here.at(dz=-1), here.pair()]
    )
    gpad[...] = jnp.zeros_like(gpad)
    gpad[0:2, 0:192] = gains[...]
    g = gpad[...]
    high = g.astype(BF).astype(F32)
    rows4 = jnp.concatenate([high[0:2], (g - high)[0:2]], axis=0)
    rest = rows4[:, 128:]
    rest = jnp.where(here.zl == 0, rest, pltpu.roll(rest, 64, 1))
    rows16 = jnp.concatenate([rows4[:, :128], rest, jnp.zeros((8, 128), F32)], axis=0).astype(BF)
    wire.there(x_load)
    for r in range(8):
        xin[r, 192:208, :] = rows16
    pack_rows(here, xin, xf)
    xs = swap_rows(wire, here, xin, xbuf)
    xbuf[here.row] = xin[here.row]

    wire.there(*q_load)
    wq_own[...] = dot(qf[...].astype(BF), qs[...], 1, 1).astype(BF)
    q_weights = weight_gather(wire, here, wq_own, wq)
    next(q_weights)
    wire.there(*o_load)
    wo_own[...] = dot(of[...].astype(BF), os[...], 1, 1).astype(BF)
    o_weights = weight_gather(wire, here, wo_own, wo)
    lane = lax.broadcasted_iota(jnp.int32, (128, 256), 1)
    for c in range(4):
        first = 512 * c + 128 * here.y
        place = positions[:, pl.ds(pl.multiple_of(first, 128), 128)]
        place = jnp.where(here.zl == 0, place[0:1], place[1:2])
        token = first + lax.broadcasted_iota(jnp.int32, (1, 128), 1)
        table[2 * c : 2 * c + 1, :] = jnp.concatenate([token - place] * 2, axis=1)
        table[2 * c + 1 : 2 * c + 2, :] = jnp.concatenate([token] * 2, axis=1)
        column = jnp.broadcast_to(place.astype(F32), (128, 128)).T[:, 0:1]
        angles = column * frequency[0:1]
        at = pl.ds(128 * c, 128)
        cosine[at, :] = jnp.where(lane < 2 * HS, jnp.cos(angles), 0.0)
        sine[at, :] = jnp.where(lane < 2 * HS, jnp.sin(angles), 0.0)
    wire.there(c_load)
    pack_rows(here, cin, cf)
    cbuf[here.row] = cin[here.row]

    wire.arrive(*xs)
    x = widened(xbuf)
    xtok[...] = x
    g = widened_rows(xbuf, 192, 4).astype(F32)
    g = g[0:2] + g[2:4]
    gtok[...] = g
    h1_all[here.x] = normed(x.astype(F32), g[0:1])
    h1_flow = share(wire, here, h1_all)
    next(h1_flow)
    next(q_weights)
    wire.there(*f_load)
    for k in range(2):
        for j in range(2):
            at = 1024 * k + 512 * j
            win[:, at : at + 512] = gf[j, :, 512 * k : 512 * k + 512].astype(BF)
    win[:, 2048:3072] = df[...].astype(BF)
    wire.stay(win.at[:, pl.ds(2048, 1024)], down_out)
    side_by_side(h1_flow, q_weights)
    wire.stay(wq, wq_out)
    wire.stay(h1_all, h1_out)
    next(o_weights)
    cs = swap_rows(wire, here, cin, cbuf)

    @pl.loop(0, 3)
    def _(n):
        qkv[:, columns(n)] = dot(tokens_of(h1_all), wq[:, columns(n)])

    for c in range(4):
        at = pl.ds(128 * c, 128)
        turn = cosine[at], sine[at]
        key = turned(qkv[at, 384:640], *turn)
        value = jnp.where(lane < 64, 0.0, qkv[at, 512:768])
        kv = packed_pair(key, value).astype(BF)
        kv_own[c] = kv
        kv_all[key_block(c, here.y)] = kv

    keys = ring_gather(
        wire,
        here.y,
        here.at(dy=1),
        here.at(dy=-1),
        lambda h: [kv_own.at[2 * h + n] for n in range(2)],
        lambda i, h: [kv_all.at[key_block(2 * h + n, i)] for n in range(2)],
    )
    next(keys)
    for c in range(4):
        at = pl.ds(128 * c, 128)
        turn = cosine[at], sine[at]
        q[at, 0:256] = turned(qkv[at, 0:256], *turn).astype(BF)
        second = pltpu.roll(qkv[at, 128:384], 192, 1)
        q[at, 256:512] = turned(second, *turn).astype(BF)
    next(o_weights)
    wire.arrive(*cs)
    c_value = widened(cbuf)
    ctok[...] = c_value
    c_all[here.x] = c_value
    side_by_side(keys, o_weights, share(wire, here, c_all))
    for held, out in ((c_all, c_out), (wo, wo_out), (kv_all, kv_out)):
        wire.stay(held, out)
    weights = weight_gather(wire, here, win.at[:, pl.ds(0, 2048)], w_both)
    next(weights)
    for _ in attend(here, q, kv_all, table, heads, log_total):
        pass
    back_to_width(lambda: heads[...], wo, part)
    chain = x_sum(wire, here, part, far, near, rise)
    next(chain)
    next(weights)
    next(weights)
    next(chain)
    next(weights)
    side_by_side(chain, weights)
    h2_own[...] = normed(rise[...] + xtok[...].astype(F32), gtok[1:2])
    wire.finish()


def shape(dtype, *sizes):
    return jax.ShapeDtypeStruct(sizes, dtype)


def signals(*counts):
    return [pltpu.SemaphoreType.DMA((n,)) for n in counts]


def settings(number):
    return pltpu.CompilerParams(
        collective_id=number, has_side_effects=True, vmem_limit_bytes=60 << 20
    )


def enter(*operands):
    return pl.pallas_call(
        enter_kernel,
        out_shape=[
            shape(BF, 4, 128, D),
            shape(BF, D, 768),
            shape(BF, D, 512),
            shape(BF, 4, 128, D),
            shape(BF, 16, 128, 384),
            shape(BF, 192, 1024),
            shape(BF, D, 2048),
            shape(F32, 128, D),
            shape(BF, 128, D),
            shape(BF, 512, 512),
            shape(BF, 512, 512),
            shape(F32, 8, 256),
            shape(F32, 512, 256),
            shape(F32, 512, 256),
            shape(BF, 128, D),
            shape(BF, 128, D),
            shape(F32, 2, D),
            shape(jnp.int32, 8, 256),
        ],
        in_specs=[ANY] * 6 + [VM] * 3 + [ANY] * 2,
        out_specs=[ANY] * 7 + [VM] * 11,
        scratch_shapes=[
            pltpu.VMEM((2, 192, 512), F32),
            pltpu.VMEM((2, 192, 512), F32),
            pltpu.VMEM((192, 768), F32),
            pltpu.VMEM((192, 384), F32),
            pltpu.VMEM((2, 192, 1024), F32),
            pltpu.VMEM((192, 1024), F32),
            pltpu.VMEM((768, 768), BF),
            pltpu.VMEM((512, 384), BF),
            pltpu.VMEM((8, 208, 128), BF),
            pltpu.VMEM((8, 192, 128), BF),
            pltpu.VMEM((192, 768), BF),
            pltpu.VMEM((192, 512), BF),
            pltpu.VMEM((192, 3072), BF),
            pltpu.VMEM((8, 208, 128), BF),
            pltpu.VMEM((8, 192, 128), BF),
            pltpu.VMEM((4, 128, D), BF),
            pltpu.VMEM((4, 128, D), BF),
            pltpu.VMEM((D, 768), BF),
            pltpu.VMEM((D, 512), BF),
            pltpu.VMEM((4, 128, D), BF),
        ]
        + x_sum_scratch()
        + [
            pltpu.VMEM((4, 128, 384), BF),
            pltpu.VMEM((16, 128, 384), BF),
            pltpu.VMEM((512, 768), F32),
            pltpu.VMEM((8, 256), F32),
        ]
        + signals(200, 200, 24),
        compiler_params=settings(1),
        name="enter",
    )(*operands)


BOTH = (1024, 512)
DOWN = (512, 256)


def feed_kernel(*refs):
    rise, h2_own, xtok, gtok, ctok, down_own, both_w, c_in = refs[:8]
    after_out, gain, f_out, d_out = refs[8:12]
    both_sums, down_sums = refs[12:16], refs[16:20]
    after, f_part, far, near, middle, summed, h2_all, c_all = refs[20:28]
    w_down, w_both, both, act, both_in, act_in, hidden, part2, d_all = refs[28:37]
    main, rest, down_main, down_rest = refs[37:41]
    both_first, down_first, (send, recv, local) = refs[41:49], refs[49:57], refs[57:]
    here = Place()
    wire = Wire(send, recv, local)
    greet(ring_partners(here) + plane_partners(here) + [here.pair()])
    h2_all[here.x] = h2_own[...]
    chain = share(wire, here, h2_all)
    next(chain)
    down = weight_gather(wire, here, down_own, w_down)
    next(down)
    loads = wire.stay(c_in, c_all.at[pl.ds(0, 4)]), wire.stay(both_w, w_both)
    middle[...] = rise[...] + xtok[...].astype(F32)
    next(chain)
    next(down)
    next(down)
    next(chain)
    next(down)
    side_by_side(chain)
    wire.there(*loads)
    paired = [to_pair(wire, here, h2_all)]

    @pl.loop(0, 8)
    def _(n):
        hidden[:, columns(n)] = dot(tokens_of(h2_all), w_both[:, columns(n)])

    side_by_side(down)

    def unit_tiles(half):
        @pl.loop(0, 2)
        def _(n):
            at, down_at = columns(half * 4 + n), columns(half * 2 + n)
            up_at = columns(half * 4 + n + 2)
            gate, up = hidden[:, at], hidden[:, up_at]
            grad = dot(tokens_of(c_all), w_down[:, down_at])
            sigmoid = 1.0 / (1.0 + jnp.exp(-gate))
            silu = gate * sigmoid
            both[:, at] = (grad * up * sigmoid * (1.0 + gate * (1.0 - sigmoid))).astype(BF)
            both[:, up_at] = (grad * silu).astype(BF)
            act[:, down_at] = (silu * up).astype(BF)

    other = 1 - here.core
    unit_tiles(other)
    paired.append(wire.copy(both.at[:, columns(other, 1024)], both_in, here.pair()))
    paired.append(wire.copy(act.at[:, columns(other, 512)], act_in, here.pair()))
    c_paired = to_pair(wire, here, c_all)
    unit_tiles(here.core)
    back_to_width(lambda: both[...], w_both, part2)

    def backward():
        yield from x_sum(wire, here, part2, far, near, summed)
        left, gain_terms = norm_back(middle[...], summed[...], gtok[1:2])
        gain[...] = jnp.broadcast_to(gain_terms, gain.shape)
        after[...] = left
        d_all[here.x] = (left + ctok[...].astype(F32)).astype(BF)
        wire.stay(after, after_out)
        yield from share(wire, here, d_all)

    chain = backward()
    next(chain)
    back_to_width(lambda: act[...], w_down, f_part)
    wire.stay(f_part, f_out)
    wire.arrive(*paired)
    next(chain)
    weight_grads(
        h2_all, lambda: both[:, columns(here.core, 1024)], lambda: both_in[...], main, rest, slice(None)
    )
    flows = first_sums(wire, here, (main, rest), both_first, both_sums, *BOTH)
    for flow in flows:
        next(flow)
    next(chain)
    wire.arrive(c_paired)
    weight_grads(
        c_all, lambda: act[:, columns(here.core, 512)], lambda: act_in[...], down_main, down_rest, slice(None)
    )
    flows += first_sums(wire, here, (down_main, down_rest), down_first, down_sums, *DOWN)
    next(chain)
    for flow in flows:
        next(flow)
    next(chain)
    side_by_side(chain)
    wire.stay(d_all, d_out)
    side_by_side(*flows)
    wire.finish()


def grad_shapes(width):
    return [(4, 2, 2, high, width) for high in HIGHS]


def grad_arrays(width):
    return [pltpu.VMEM(sizes, BF) for sizes in grad_shapes(width)]


def feed(*operands):
    return pl.pallas_call(
        feed_kernel,
        out_shape=[
            shape(F32, 128, D),
            shape(F32, 8, D),
            shape(BF, 4, 128, D),
            shape(BF, 4, 128, D),
        ]
        + [shape(BF, *sizes) for sizes in half_sums(*BOTH) + half_sums(*DOWN)],
        in_specs=[VM] * 5 + [ANY] * 3,
        out_specs=[ANY, VM] + [ANY] * 2 + [VM] * 8,
        scratch_shapes=[
            pltpu.VMEM((128, D), F32),
            pltpu.VMEM((4, 128, D), BF),
        ]
        + x_sum_scratch()
        + [
            pltpu.VMEM((128, D), F32),
            pltpu.VMEM((128, D), F32),
            pltpu.VMEM((8, 128, D), BF),
            pltpu.VMEM((8, 128, D), BF),
            pltpu.VMEM((D, 1024), BF),
            pltpu.VMEM((D, 2048), BF),
            pltpu.VMEM((512, 2048), BF),
            pltpu.VMEM((512, 1024), BF),
            pltpu.VMEM((512, 1024), BF),
            pltpu.VMEM((512, 512), BF),
            pltpu.VMEM((512, 2048), F32),
            pltpu.VMEM((4, 128, D), BF),
            pltpu.VMEM((4, 128, D), BF),
        ]
        + grad_arrays(BOTH[0])
        + grad_arrays(DOWN[0])
        + first_scratch(*BOTH)
        + first_scratch(*DOWN)
        + signals(200, 200, 16),
        compiler_params=settings(2),
        name="feed",
    )(*operands)


ATTN = (640, 256)


def leave_held():
    sizes = [(4, 128, D)]
    sizes += half_sums(*BOTH) + half_sums(*DOWN)
    sizes += [(4, 128, D), (D, 512), (512, 512), (16, 128, 384), (512, 512), (4, 128, D)]
    sizes += [(D, 768), (128, D)]
    return [(size, BF) for size in sizes] + [
        ((128, D), F32), ((128, D), F32), ((512, 256), F32), ((512, 256), F32)
    ]


def leave_kernel(*refs):
    gtok, gain, log_total, table = refs[:4]
    count = len(leave_held())
    held_in, refs = refs[4 : 4 + count], refs[4 + count :]
    o_all, s_all, gout, both_out, down_out, gains_out = refs[:6]
    held, refs = refs[6 : 6 + count], refs[6 + count :]
    f_part, both_sums, down_sums = held[0], held[1:5], held[5:9]
    d_all, wo, q, kv_all, heads, h1_all, wq, xtok, rise, after, cosine, sine = held[9:]
    dout, dq, total, dkv, kfar, knear, dkv_own, dqkv = refs[:8]
    heads_in, dqkv_in, part, far, near, far2, near2, summed, osend, ssend = refs[8:18]
    gsend, grow, gcol, gdp, main, rest = refs[18:24]
    scratch, (send, recv, local) = refs[24:-3], refs[-3:]
    a_first, a_sums, a_second = scratch[:8], scratch[8:12], scratch[12:21]
    both_second, down_second = scratch[21:30], scratch[30:39]
    here = Place()
    wire = Wire(send, recv, local)
    loads = []
    for src, dst in zip(held_in, held):
        dst = dst.at[pl.ds(0, 4)] if dst.shape != src.shape else dst
        loads.append(wire.stay(src, dst))
    greet(
        [here.in_row(s) for s in range(1, 8)]
        + ring_partners(here)
        + [here.at(dz=1), here.at(dz=-1), here.at(dx=2)]
        + [here.in_dp(s) for s in range(1, 4)]
    )
    wire.there(*loads[:9])
    branch_sum = x_sum(wire, here, f_part, far, near, summed)
    next(branch_sum)
    sums = second_sums(wire, here, both_sums, both_second, *BOTH)
    sums += second_sums(wire, here, down_sums, down_second, *DOWN)
    for flow in sums:
        next(flow)
    wire.there(*loads[9:14])

    @pl.loop(0, 2)
    def _(n):
        dout[:, columns(n)] = dot(tokens_of(d_all), wo[:, columns(n)]).astype(BF)

    heads_swap = wire.copy(heads.at[:, columns(1 - here.core)], heads_in, here.pair())
    d_paired = to_pair(wire, here, d_all)
    for flow in sums:
        next(flow)
    next(branch_sum)

    def key_sums(half):
        block = lambda h: 2 * half + h
        return ring_sum(
            wire,
            here.y,
            here.at(dy=1),
            here.at(dy=-1),
            lambda i, h: [dkv.at[key_block(block(h), i)]],
            lambda h: [kfar.at[half, h]],
            lambda s, h: [knear.at[half, s, h]],
            lambda h: [dkv_own.at[pl.ds(128 * block(h), 128)]],
        )

    attention = attend_back(here, q, kv_all, table, log_total, dout, dq, total)
    next(attention)
    next(attention)
    dkv[8:16] = total[8:16].astype(BF)
    late_keys = key_sums(1)
    next(late_keys)
    next(attention)
    next(late_keys)
    next(attention)
    dkv[0:8] = total[0:8].astype(BF)
    keys = key_sums(0)
    next(keys)
    wire.there(*loads[14:])
    side_by_side(*sums)
    both_share = grad_share(wire, here, both_second[-1], both_out, BOTH[0])
    down_share = grad_share(wire, here, down_second[-1], down_out, DOWN[0])
    next(both_share)
    next(down_share)
    h1_paired = to_pair(wire, here, h1_all)
    side_by_side(branch_sum)
    narrowed(osend, summed[...] + rise[...])
    for c in range(4):
        at = pl.ds(128 * c, 128)
        turn = cosine[at], -sine[at]
        second = turned(dq[at, 256:512], *turn)
        both = packed_pair(turned(dq[at, 0:256], *turn), pltpu.roll(second, 64, 1))
        dqkv[at, 0:384] = both.astype(BF)
    next(keys)
    wire.arrive(heads_swap, d_paired)
    weight_grads(
        d_all, lambda: heads[:, columns(here.core)], lambda: heads_in[...], main, rest, slice(384, 640)
    )
    lane = lax.broadcasted_iota(jnp.int32, (128, 256), 1)
    side_by_side(late_keys, keys)
    for c in range(4):
        at = pl.ds(128 * c, 128)
        key = turned(dkv_own[at, 0:256], cosine[at], -sine[at])
        value = jnp.where(lane < 64, 0.0, dkv_own[at, 128:384])
        dqkv[at, 384:768] = packed_pair(key, value).astype(BF)
    dqkv_swap = wire.copy(dqkv.at[:, columns(1 - here.core, 384)], dqkv_in, here.pair())
    back_to_width(lambda: dqkv[...], wq, part)

    def chain():
        yield from x_sum(wire, here, part, far2, near2, summed)
        left, gain_terms = norm_back(xtok[...].astype(F32), summed[...], gtok[0:1])
        gains = jnp.concatenate([gain_terms, gain[0:1], jnp.zeros((6, D), F32)], axis=0)
        narrowed_rows(gsend, gains)
        g = swap_rows(wire, here, gsend, grow)
        narrowed(ssend, left + after[...])
        wire.stay(ssend.at[here.row], s_all.at[here.row])
        swap_rows(wire, here, ssend, s_all)
        yield
        wire.arrive(*g)
        grow[here.row] = gsend[here.row]
        total = grow[0]
        for n in range(1, 8):
            total = total + grow[n]
        gcol[here.x] = total
        g = [wire.copy(gcol.at[here.x], gcol.at[here.x], here.at(dx=s)) for s in range(1, 4)]
        yield
        wire.arrive(*g)
        gdp[here.dp] = ((gcol[0] + gcol[1]) + gcol[2]) + gcol[3]
        g = [wire.copy(gdp.at[here.dp], gdp.at[here.dp], here.in_dp(s)) for s in range(1, 4)]
        yield
        wire.arrive(*g)
        gains_out[...] = ((gdp[0] + gdp[1]) + gdp[2]) + gdp[3]

    steps = chain()
    next(steps)
    side_by_side(both_share, down_share)
    wire.stay(osend.at[here.row], o_all.at[here.row])
    swap_rows(wire, here, osend, o_all)
    wire.arrive(dqkv_swap, h1_paired)
    weight_grads(
        h1_all, lambda: dqkv[:, columns(here.core, 384)], lambda: dqkv_in[...], main, rest, slice(0, 384)
    )
    first = first_sums(wire, here, (main, rest), a_first, a_sums, *ATTN)

    def sums():
        yield
        side_by_side(*first)
        second = second_sums(wire, here, a_sums, a_second, *ATTN)
        for flow in second:
            next(flow)
        yield
        for flow in second:
            next(flow)
        yield
        side_by_side(*second)
        yield from grad_share(wire, here, a_second[-1], gout, ATTN[0])

    for flow in first:
        next(flow)
    for flow in first:
        next(flow)
    side_by_side(steps, sums())
    wire.finish()


def leave(*operands):
    held = [pltpu.VMEM(size, kind) for size, kind in leave_held()]
    for n in (9, 14):
        held[n] = pltpu.VMEM((8, 128, D), BF)
    return pl.pallas_call(
        leave_kernel,
        out_shape=[
            shape(BF, 8, 192, 128),
            shape(BF, 8, 192, 128),
            shape(BF, 2, 96, 2 * ATTN[0]),
            shape(BF, 2, 96, 2 * BOTH[0]),
            shape(BF, 2, 96, 2 * DOWN[0]),
            shape(F32, 8, 256),
        ],
        in_specs=[VM] * 4 + [ANY] * len(held),
        out_specs=[ANY] * 5 + [VM],
        scratch_shapes=held
        + [
            pltpu.VMEM((512, 512), BF),
            pltpu.VMEM((512, 512), F32),
            pltpu.VMEM((16, 128, 384), F32),
            pltpu.VMEM((16, 128, 384), BF),
            pltpu.VMEM((2, 2, 128, 384), BF),
            pltpu.VMEM((2, 2, 2, 128, 384), BF),
            pltpu.VMEM((512, 384), F32),
            pltpu.VMEM((512, 768), BF),
            pltpu.VMEM((512, 256), BF),
            pltpu.VMEM((512, 384), BF),
            pltpu.VMEM((4, 128, D), BF),
        ]
        + x_sum_scratch()
        + x_sum_scratch()
        + [
            pltpu.VMEM((128, D), F32),
            pltpu.VMEM((8, 192, 128), BF),
            pltpu.VMEM((8, 192, 128), BF),
            pltpu.VMEM((8, 8, 256), F32),
            pltpu.VMEM((8, 8, 256), F32),
            pltpu.VMEM((4, 8, 256), F32),
            pltpu.VMEM((4, 8, 256), F32),
        ]
        + grad_arrays(ATTN[0])
        + first_scratch(*ATTN)
        + [pltpu.VMEM(sizes, BF) for sizes in half_sums(*ATTN)]
        + second_scratch(*ATTN)
        + second_scratch(*BOTH)
        + second_scratch(*DOWN)
        + signals(240, 240, 32),
        compiler_params=settings(3),
        name="leave",
    )(*operands)


def step_rates():
    return (2.0 / D**0.5, 2.0 / max(HQ * HS // 64, 1) ** 0.5, 2.0 / D**0.5, 2.0 / FF**0.5, 0.4)


def adamw(state, at, gradient, step_rate, decay_rate):
    weight, first, second = state
    moment_one = beta_first * first[at] + (1.0 - beta_first) * gradient
    moment_two = beta_second * second[at] + (1.0 - beta_second) * gradient * gradient
    first[at] = moment_one
    second[at] = moment_two
    corrected = (moment_one * (1.0 / (1.0 - beta_first**STEP))) / (
        jnp.sqrt(moment_two * (1.0 / (1.0 - beta_second**STEP))) + adam_epsilon
    )
    old = weight[at]
    weight[at] = old - step_rate * (corrected + decay_rate * old)


def update_kernel(*refs):
    stream, cotangent, o_in, s_in, g_in, both_in, down_in, qkv_at, out_at = refs[:9]
    qkv, out, gate_up, down, gains = (refs[9 + 3 * n : 12 + 3 * n] for n in range(5))
    gains_tile = refs[24]
    o_out, s_out = refs[25:27]
    results = [refs[27 + 3 * n : 30 + 3 * n] for n in range(5)]
    xf, cf, ot, st, gb, fb, db, qs, os = refs[42:51]
    qkv_s, out_s, gate_s, down_s = (refs[51 + 3 * n : 54 + 3 * n] for n in range(4))
    local = refs[63]
    here = Place()
    wire = Wire(None, None, local)
    rate_qkv, rate_out, rate_gate_up, rate_down, rate_gains = step_rates()

    f_load = [wire.stay(both_in, fb)]
    for a, b in zip(gate_up, gate_s):
        f_load += [wire.stay(a.at[:, j], b.at[j]) for j in range(2)]
    d_load = [wire.stay(down_in, db)] + [wire.stay(a, b) for a, b in zip(down, down_s)]
    x_load = [wire.stay(a, b) for a, b in ((stream, xf), (o_in, ot), (cotangent, cf), (s_in, st))]
    a_load = [wire.stay(a, b) for a, b in ((g_in, gb), (qkv_at, qs), (out_at, os))]
    a_load += [wire.stay(a, b) for a, b in zip(qkv + out, qkv_s + out_s)]

    def feed_part(states, grads):
        @pl.loop(0, 4)
        def _(n):
            zh, k = lax.div(n, 2), lax.rem(n, 2)
            for start, size, begin in ((0, 64, 64 * zh), (64, 32, 128 + 32 * zh)):
                at = pl.ds(pl.multiple_of(begin, 32), size), columns(k, 512)
                for a, (state, rate) in enumerate(states):
                    lanes = columns(len(states) * k + a, 512)
                    gradient = grads[zh, start : start + size, lanes].astype(F32)
                    adamw(state, at, gradient, rate, weight_decay)

    wire.there(*f_load)
    feed_part([([b.at[j] for b in gate_s], rate_gate_up) for j in range(2)], fb)
    for a, b in zip(results[2], gate_s):
        for j in range(2):
            wire.stay(b.at[j], a.at[:, j])
    wire.there(*d_load)
    feed_part([(down_s, rate_down)], db)
    for a, b in zip(results[3], down_s):
        wire.stay(b, a)

    wire.there(*x_load)
    for held, tiles, result in ((xf, ot, o_out), (cf, st, s_out)):
        for y in range(4):
            for zl in range(2):
                tile = tiles[2 * y + zl].astype(F32)
                rest = jnp.concatenate([tile[128:192]] * 2, axis=0).T
                rest = jnp.where(low_lanes(64), rest[0:64], rest[64:128])
                at = pl.ds(128 * y, 128)
                held[zl, 0:128, at] = held[zl, 0:128, at] + tile[0:128].T
                held[zl, 128:192, at] = held[zl, 128:192, at] + rest
        wire.stay(held, result)

    wire.there(*a_load)

    def own_block(start, size):
        lanes = [pl.ds(ATTN[0] * k + start, size) for k in range(2)]
        parts = [(0, slice(0, 64)), (1, slice(0, 64)), (0, slice(64, 96)), (1, slice(64, 96))]
        return jnp.concatenate(
            [jnp.concatenate([gb[zh, at, l] for zh, at in parts], axis=0) for l in lanes], axis=1
        )

    gradient = dot(own_block(0, 384), qs[...])
    adamw(qkv_s, (slice(None), slice(None)), gradient, rate_qkv, weight_decay)
    gradient = dot(own_block(384, 256), os[...])
    adamw(out_s, (slice(None), slice(None)), gradient, rate_out, weight_decay)
    for a, b in zip(results[0] + results[1], qkv_s + out_s):
        wire.stay(b, a)

    tile = gains_tile[...]
    rest = own_half(here, tile[:, 128:])
    for old, new in zip(gains, results[4]):
        new[...] = old[...]
    adamw(results[4], (slice(None), slice(0, 128)), tile[0:2, 0:128], rate_gains, 0.0)
    adamw(results[4], (slice(None), slice(128, 192)), rest[0:2, 0:64], rate_gains, 0.0)
    wire.finish()


def update(*operands):
    sizes = [(192, 768)] * 3 + [(192, 384)] * 3 + [(192, 2, 1024)] * 3 + [(192, 1024)] * 3
    held = [(192, 768)] * 3 + [(192, 384)] * 3 + [(2, 192, 1024)] * 3 + [(192, 1024)] * 3
    return pl.pallas_call(
        update_kernel,
        out_shape=[shape(F32, 2, 192, 512)] * 2
        + [shape(F32, *size) for size in sizes]
        + [shape(F32, 2, 192)] * 3,
        in_specs=[ANY] * 21 + [VM] * 4,
        out_specs=[ANY] * 14 + [VM] * 3,
        scratch_shapes=[
            pltpu.VMEM((2, 192, 512), F32),
            pltpu.VMEM((2, 192, 512), F32),
            pltpu.VMEM((8, 192, 128), BF),
            pltpu.VMEM((8, 192, 128), BF),
            pltpu.VMEM((2, 96, 2 * ATTN[0]), BF),
            pltpu.VMEM((2, 96, 2 * BOTH[0]), BF),
            pltpu.VMEM((2, 96, 2 * DOWN[0]), BF),
            pltpu.VMEM((768, 768), BF),
            pltpu.VMEM((512, 384), BF),
        ]
        + [pltpu.VMEM(size, F32) for size in held]
        + signals(64),
        compiler_params=pltpu.CompilerParams(vmem_limit_bytes=60 << 20),
        name="update",
    )(*operands)


def body(
    stream,
    cotangent,
    segments,
    positions,
    qkv_weight,
    qkv_first,
    qkv_second,
    out_weight,
    out_first,
    out_second,
    gate_up_weight,
    gate_up_first,
    gate_up_second,
    down_weight,
    down_first,
    down_second,
    gains,
    gains_first,
    gains_second,
):
    frequency = rope_theta ** (-2.0 * (jnp.arange(256) % (HS // 2)).astype(F32) / HS)
    frequency = jnp.broadcast_to(frequency, (8, 256))
    qkv_at, out_at = qkv_order(), out_order()
    stream_turned, cotangent_turned = stream.transpose(1, 2, 0), cotangent.transpose(1, 2, 0)
    (
        h1_all, wq, wo, c_all, kv_all, down_own, w_both, rise, h2_own,
        q, heads, log_total, cosine, sine, xtok, ctok, gtok, table,
    ) = enter(
        stream_turned, cotangent_turned, qkv_weight, out_weight.T, gate_up_weight, down_weight.T,
        gains, positions, frequency, qkv_at, out_at,
    )
    after, gain_two, f_part, d_all, *sums = feed(
        rise, h2_own, xtok, gtok, ctok, down_own, w_both, c_all
    )
    o_tiles, s_tiles, attn_grads, both_grads, down_grads, gains_tile = leave(
        gtok, gain_two, log_total, table,
        f_part, *sums, d_all, wo, q, kv_all, heads, h1_all, wq, xtok, rise, after, cosine, sine,
    )
    made = update(
        stream_turned, cotangent_turned, o_tiles, s_tiles, attn_grads, both_grads, down_grads, qkv_at, out_at,
        qkv_weight, qkv_first, qkv_second,
        out_weight.T, out_first.T, out_second.T,
        gate_up_weight, gate_up_first, gate_up_second,
        down_weight.T, down_first.T, down_second.T,
        gains, gains_first, gains_second,
        gains_tile,
    )
    output, stream_grad = made[0].transpose(2, 0, 1), made[1].transpose(2, 0, 1)
    states = [made[2 + 3 * n : 5 + 3 * n] for n in range(5)]
    for n in (1, 3):
        states[n] = [a.T for a in states[n]]
    return (output, stream_grad, *(a for w, m, v in states for a in (m, v, w)))


def solution(mesh):
    tokens = P("col", "dp", "row")
    table = P("dp", None)
    wide, tall, pairs, both = P("row", "col"), P("col", "row"), P("row", None, "col"), P(None, "row")
    weights = (wide,) * 3 + (tall,) * 3 + (pairs,) * 3 + (tall,) * 3 + (both,) * 3
    return jax.shard_map(
        body,
        mesh=mesh,
        in_specs=(tokens, tokens, table, table, *weights),
        out_specs=(tokens, tokens, *weights),
        check_vma=False,
    )
```

```python
import functools

import jax
import jax.numpy as jnp
import numpy as np
from jax import lax
from jax.experimental import pallas as pl
from jax.experimental.pallas import tpu as pltpu
from jax.sharding import PartitionSpec as P

D = 1536
FF = 4096
HQ = 16
KVH = 8
HS = 96
STEP = 10
LEN = 2048
WINDOW = 1024

norm_epsilon = 1e-05
rope_theta = 100000.0
beta_first = 0.9
beta_second = 0.95
adam_epsilon = 1e-08
weight_decay = 0.1
score_scale = HS**-0.5

MESH = pl.DeviceIdType.MESH
BF = jnp.bfloat16
F32 = jnp.float32
VM = pl.BlockSpec(memory_space=pltpu.VMEM)
ANY = pl.BlockSpec(memory_space=pl.ANY)


def selection(source, count):
    chosen = np.zeros((count, len(source)), np.float32)
    chosen[source, np.arange(len(source))] = 1.0
    return jnp.asarray(chosen, BF)


def qkv_order():
    b = np.arange(768)
    return selection(b % 384 // HS * 192 + b // 384 * HS + b % HS, 768)


def out_order():
    b = np.arange(384)
    return selection(b % 192 // HS * 256 + 64 + b // 192 * HS + b % HS, 512)


class Place:
    def __init__(self):
        self.dp = lax.axis_index("dp")
        self.row = lax.axis_index("row")
        self.x = lax.axis_index("col")
        self.zh = lax.div(self.dp, 2)
        self.core = lax.rem(self.dp, 2)
        self.y = lax.div(self.row, 2)
        self.zl = lax.rem(self.row, 2)
        self.z = self.zh * 2 + self.zl

    def at(self, dx=0, dy=0, dz=0, dcore=0):
        x = lax.rem(self.x + (dx + 4), 4)
        y = lax.rem(self.y + (dy + 4), 4)
        z = lax.rem(self.z + (dz + 4), 4)
        core = lax.rem(self.core + dcore, 2)
        return (lax.div(z, 2) * 2 + core, y * 2 + lax.rem(z, 2), x)

    def pair(self):
        return self.at(dcore=1)

    def in_row(self, step):
        return (self.dp, lax.rem(self.row + step, 8), self.x)

    def in_dp(self, step):
        return (lax.rem(self.dp + step, 4), self.row, self.x)


def greet(devices):
    barrier = pltpu.get_barrier_semaphore()
    for device in devices:
        pl.semaphore_signal(barrier, inc=1, device_id=device, device_id_type=MESH)
    pl.semaphore_wait(barrier, len(devices))


class Wire:
    def __init__(self, send, recv, local=None):
        self.send, self.recv, self.local = send, recv, local
        self.sent, self.open, self.near, self.stays = [], {}, [], 0

    def copy(self, src, dst, device):
        n = len(self.sent)
        made = pltpu.make_async_remote_copy(
            src_ref=src,
            dst_ref=dst,
            send_sem=self.send.at[n],
            recv_sem=self.recv.at[n],
            device_id=device,
            device_id_type=MESH,
        )
        made.start()
        self.sent.append(made)
        self.open[n] = made
        return n

    def arrive(self, *numbers):
        for n in numbers:
            self.open.pop(n).wait_recv()

    def stay(self, src, dst):
        made = pltpu.make_async_copy(src, dst, self.local.at[self.stays])
        self.stays += 1
        made.start()
        self.near.append(made)
        return made

    def there(self, *stays):
        for made in stays:
            self.near = [other for other in self.near if other is not made]
            made.wait()

    def settle(self):
        self.arrive(*list(self.open))

    def finish(self):
        self.settle()
        for made in self.sent:
            made.wait_send()
        self.there(*list(self.near))


def around(me):
    return lax.rem(me + 3, 4), lax.rem(me + 1, 4), lax.rem(me + 2, 4)


def ring_gather(wire, me, right, left, own, slot):
    l, r, o = around(me)

    def send(src, dst, device):
        return [wire.copy(a, b, device) for a, b in zip(src, dst)]

    def pass_on(numbers, refs, device):
        passed = []
        for n, ref in zip(numbers, refs):
            wire.arrive(n)
            passed.append(wire.copy(ref, ref, device))
        return passed

    first = send(own(0), slot(me, 0), right), send(own(1), slot(me, 1), left)
    second = send(own(1), slot(me, 1), right), send(own(0), slot(me, 0), left)
    yield
    far = pass_on(first[0], slot(l, 0), right) + pass_on(first[1], slot(r, 1), left)
    yield
    wire.arrive(*second[0], *second[1])
    yield
    wire.arrive(*far)


def leading(ref):
    found = [()]
    for size in ref.shape[:-2]:
        found = [index + (n,) for index in found for n in range(size)]
    return found


def add_parts(out, refs):
    for index in leading(out):
        at = index + (slice(None), slice(None))
        total = refs[0][at].astype(F32)
        for ref in refs[1:]:
            total = total + ref[at].astype(F32)
        out[at] = total.astype(out.dtype)


def ring_sum(wire, me, right, left, part, far, near, out):
    l, r, o = around(me)

    def send(srcs, dsts, device):
        return [wire.copy(a, b, device) for a, b in zip(srcs, dsts)]

    far0 = send(part(o, 0), far(0), right)
    far1 = send(part(o, 1), far(1), left)
    to_right = send(part(r, 1), near(0, 1), right)
    to_left = send(part(l, 0), near(1, 0), left)
    yield
    for n, a, b, c in zip(far0, far(0), part(r, 0), near(0, 0)):
        wire.arrive(n)
        add_parts(a, [a, b])
        to_right.append(wire.copy(a, c, right))
    for n, a, b, c in zip(far1, far(1), part(l, 1), near(1, 1)):
        wire.arrive(n)
        add_parts(a, [a, b])
        to_left.append(wire.copy(a, c, left))
    yield
    wire.arrive(*to_right, *to_left)
    for h in range(2):
        for a, b, c, total in zip(part(me, h), near(0, h), near(1, h), out(h)):
            add_parts(total, [a, b, c])


def side_by_side(*flows):
    flows = list(flows)
    while flows:
        for flow in list(flows):
            try:
                next(flow)
            except StopIteration:
                flows.remove(flow)


def rows(ref, start, size, multiple):
    return ref.at[pl.ds(pl.multiple_of(start, multiple), size)]


def weight_gather(wire, here, own, whole, z_first=False):
    core, zl = here.core, here.zl
    right, left = here.at(dy=1), here.at(dy=-1)
    up, down = here.at(dz=1), here.at(dz=-1)
    l, r, o = around(here.y)

    def mine(j):
        start = (core * 64, core * 64 + 32, 128 + core * 32, 144 + core * 32)[j]
        return rows(own, start, (32, 32, 16, 16)[j], 16)

    def piece(y, j, lo):
        block = y * 2 + lo
        main, rest = block * 128 + core * 64, 1024 + block * 64 + core * 32
        start = (main, main + 32, rest, rest + 16)[j]
        return rows(whole, start, (32, 32, 16, 16)[j], 16)

    def to_pair(y, lo):
        block = y * 2 + lo
        for view in (
            rows(whole, block * 128 + core * 64, 64, 64),
            rows(whole, 1024 + block * 64 + core * 32, 32, 32),
        ):
            paired.append(wire.copy(view, view, here.pair()))

    paired = []

    def over(y, js, device, src=None):
        return [wire.copy((src or (lambda j: piece(y, j, zl)))(j), piece(y, j, zl), device) for j in js]

    y = here.y
    kept = (
        wire.stay(own.at[pl.ds(0, 128)], rows(whole, here.row * 128, 128, 128)),
        wire.stay(own.at[pl.ds(128, 64)], rows(whole, 1024 + here.row * 64, 64, 64)),
    )
    z_own = lambda: over(y, (0, 2), up, mine) + over(y, (1, 3), down, mine)
    if z_first:
        z_y = z_own()
        yield
    r_first, l_first = over(y, (0, 2), right, mine), over(y, (1, 3), left, mine)
    r_next, l_next = over(y, (1, 3), right, mine), over(y, (0, 2), left, mine)
    if not z_first:
        z_y = z_own()
    yield
    wire.arrive(*r_first)
    far = over(l, (0, 2), right)
    wire.arrive(*l_first)
    far += over(r, (1, 3), left)
    z_l = over(l, (0, 2), up)
    z_r = over(r, (1, 3), down)
    yield
    wire.arrive(*r_next)
    z_l += over(l, (1, 3), down)
    to_pair(l, zl)
    wire.arrive(*l_next)
    z_r += over(r, (0, 2), up)
    to_pair(r, zl)
    yield
    wire.arrive(*far)
    z_o = over(o, (0, 2), up) + over(o, (1, 3), down)
    to_pair(o, zl)
    yield
    for block, numbers in ((y, z_y), (l, z_l), (r, z_r), (o, z_o)):
        wire.arrive(*numbers)
        to_pair(block, 1 - zl)
        yield
    wire.arrive(*paired)
    wire.there(*kept)


def token_pieces(half):
    return [pl.ds(64 * half + n, 16) for n in range(0, 64, 16)]


def share(wire, here, out):
    half = lambda i, h: [out.at[i, at] for at in token_pieces(h)]
    return ring_gather(
        wire, here.x, here.at(dx=1), here.at(dx=-1), lambda h: half(here.x, h), half
    )


def to_pair(wire, here, out):
    return wire.copy(out.at[pl.ds(0, 4)], out.at[pl.ds(4, 4)], here.pair())


def x_sum(wire, here, part, far, near, out):
    at = token_pieces
    return ring_sum(
        wire,
        here.x,
        here.at(dx=1),
        here.at(dx=-1),
        lambda i, h: [part.at[i, n] for n in at(h)],
        lambda h: [far.at[n] for n in at(h)],
        lambda s, h: [near.at[s, n] for n in at(h)],
        lambda h: [out.at[n] for n in at(h)],
    )


def x_sum_scratch():
    return [pltpu.VMEM((128, D), BF), pltpu.VMEM((2, 128, D), BF)]


HIGHS = (64, 32)


def order_columns(width, cut, order):
    return (0, cut) if order == 0 else (cut, width - cut)


def first_scratch(width, cut):
    shapes = []
    for order in range(2):
        size = order_columns(width, cut, order)[1]
        for high in HIGHS:
            shapes += [
                pltpu.VMEM((2, 2, high, size), BF),
                pltpu.VMEM((2, 2, 2, high, size), BF),
            ]
    return shapes


def half_sums(width, cut):
    return [
        (2, 2, high, order_columns(width, cut, order)[1]) for order in range(2) for high in HIGHS
    ]


def second_scratch(width, cut):
    shapes = []
    for order in range(2):
        size = order_columns(width, cut, order)[1]
        for high in HIGHS:
            shapes += [
                pltpu.VMEM((2, high // 2, size), BF),
                pltpu.VMEM((2, 2, high // 2, size), BF),
            ]
    return shapes + [pltpu.VMEM((96, width), BF)]


def rings(here):
    y_ring = (here.y, here.at(dy=1), here.at(dy=-1))
    z_ring = (here.z, here.at(dz=1), here.at(dz=-1))
    return y_ring, z_ring


def first_sums(wire, here, grads, scratch, sums, width, cut):
    def flow(order):
        at = pl.ds(*order_columns(width, cut, order))
        buffers, out = scratch[4 * order : 4 * order + 4], sums[2 * order : 2 * order + 2]

        def of_z(ref, i, h):
            return ref.at[pl.ds(2 * h, 2), lax.rem(i, 2), lax.div(i, 2), :, at]

        def of_y(ref, i, h):
            return ref.at[i, h, :, :, at]

        pick = of_z if order == 0 else of_y
        return ring_sum(
            wire,
            *rings(here)[1 - order],
            lambda i, h: [pick(g, i, h) for g in grads],
            lambda h: [b.at[h] for b in buffers[0::2]],
            lambda s, h: [b.at[s, h] for b in buffers[1::2]],
            lambda h: [b.at[h] for b in out],
        )

    return flow(0), flow(1)


def second_sums(wire, here, sums, scratch, width, cut):
    fin = scratch[-1]

    def flow(order):
        at = pl.ds(*order_columns(width, cut, order))
        buffers, terms = scratch[4 * order : 4 * order + 4], sums[2 * order : 2 * order + 2]

        def part(i, h):
            high, low = lax.div(i, 2), lax.rem(i, 2)
            lead = (high, low) if order == 0 else (low, high)
            return [
                b.at[lead[0], lead[1], pl.ds(tall // 2 * h, tall // 2)]
                for b, tall in zip(terms, HIGHS)
            ]

        return ring_sum(
            wire,
            *rings(here)[order],
            part,
            lambda h: [b.at[h] for b in buffers[0::2]],
            lambda s, h: [b.at[s, h] for b in buffers[1::2]],
            lambda h: [
                fin.at[pl.ds(start + tall // 2 * h, tall // 2), at]
                for start, tall in zip((0, 64), HIGHS)
            ],
        )

    return flow(0), flow(1)


def grad_share(wire, here, fin, out, width):
    columns = pl.ds(pl.multiple_of(here.core * width, 128), width)
    mine = out.at[here.zh, :, columns]
    other = out.at[1 - here.zh, :, columns]
    wire.stay(fin, mine)
    wire.copy(fin, mine, here.pair())
    n = wire.copy(fin, mine, here.at(dz=2))
    yield
    wire.arrive(n)
    wire.copy(other, other, here.pair())


def swap_rows(wire, here, src, dst):
    return [
        wire.copy(src.at[lax.rem(here.row + s, 8)], dst.at[here.row], here.in_row(s))
        for s in range(1, 8)
    ]


def low_lanes(rows):
    return lax.broadcasted_iota(jnp.int32, (rows, 128), 1) < 64


def widened(ref):
    main = [ref[r, 0:128, :] for r in range(8)]
    rest = []
    for j in range(4):
        even, odd = ref[2 * j, 128:192, :].astype(F32), ref[2 * j + 1, 128:192, :].astype(F32)
        top = jnp.where(low_lanes(64), even, odd)
        bottom = pltpu.roll(jnp.where(low_lanes(64), odd, even), 64, 1)
        rest.append(jnp.concatenate([top, bottom], axis=0).astype(BF))
    return jnp.concatenate(main + rest, axis=1)


def widened_rows(ref, start, size):
    main = [ref[r, start : start + size, :] for r in range(8)]
    after = slice(start + size, start + 2 * size)
    rest = [ref[2 * j, after, :] + ref[2 * j + 1, after, :] for j in range(4)]
    return jnp.concatenate(main + rest, axis=1)


def narrowed(out, value):
    for r in range(8):
        out[r, 0:128, :] = value[:, 128 * r : 128 * r + 128].astype(BF)
        j = 1024 + 128 * (r // 2)
        top, bottom = value[0:64, j : j + 128], value[64:128, j : j + 128]
        if r % 2 == 0:
            rest = jnp.where(low_lanes(64), top, pltpu.roll(bottom, 64, 1))
        else:
            rest = jnp.where(low_lanes(64), pltpu.roll(top, 64, 1), bottom)
        out[r, 128:192, :] = rest.astype(BF)


def narrowed_rows(out, value):
    for r in range(8):
        out[r, :, 0:128] = value[:, 128 * r : 128 * r + 128]
        j = 1024 + 128 * (r // 2)
        out[r, :, 128:256] = value[:, j : j + 128]


def ring_partners(here):
    return [here.at(dx=1), here.at(dx=-1)]


def plane_partners(here):
    return [here.at(dy=1), here.at(dy=-1), here.at(dz=1), here.at(dz=-1)]


def dot(a, b, left=1, right=0):
    return lax.dot_general(a, b, (((left,), (right,)), ((), ())), preferred_element_type=F32)


def turned(values, cosine, sine):
    lane = lax.broadcasted_iota(jnp.int32, values.shape, 1)
    front = lax.rem(lane, HS) < HS // 2
    ahead, back = pltpu.roll(values, 256 - HS // 2, 1), pltpu.roll(values, HS // 2, 1)
    return values * cosine + jnp.where(front, -ahead, back) * sine


def packed_pair(a, b):
    return jnp.concatenate([a[:, :128], a[:, 128:] + b[:, :128], b[:, 128:]], axis=1)


def windows(y):
    return ((0, 4), (0, 8), (1 + y, 8), (5 + y, 8))


def allowed_keys(table, c, start, count):
    key = start * 128 + lax.broadcasted_iota(jnp.int32, (count * 128, 256), 0)
    return (key >= table[2 * c : 2 * c + 1]) & (key <= table[2 * c + 1 : 2 * c + 2])


def both_heads(ref, at):
    return jnp.concatenate([ref[at, 0:256], ref[at, 256:512]], axis=0)


def attend(here, q, kv, table, heads, log_total):
    lane = lax.broadcasted_iota(jnp.int32, (256, 256), 1)
    for c, (start, count) in enumerate(windows(here.y)):
        at = pl.ds(128 * c, 128)
        allowed = allowed_keys(table, c, start, count)
        q_both = both_heads(q, at)
        k = kv[pl.ds(start, count), :, 0:256].reshape(count * 128, 256)
        v = kv[pl.ds(start, count), :, 128:384].reshape(count * 128, 256)
        made = []
        for g in range(2):
            n = 2 * c + g
            q_one = jnp.where((lane >= HS) == (g == 1), q_both, jnp.zeros_like(q_both))
            scores = dot(k, q_one, 1, 1) * score_scale
            scores = jnp.where(allowed, scores, -1e30)
            top = jnp.max(scores, axis=0, keepdims=True)
            weights = jnp.exp(scores - top)
            total = jnp.sum(weights, axis=0, keepdims=True)
            shares = (weights * (1.0 / total)).astype(BF)
            made.append(dot(shares, v, 0, 0))
            log_total[n : n + 1] = top + jnp.log(total)
        out = jnp.where(lane < 64 + HS, made[0], made[1])
        out = jnp.where(lane < 64, 0.0, out).astype(BF)
        heads[at, 0:256] = out[:128]
        heads[at, 256:512] = out[128:]
        yield


def attend_back(here, q, kv, table, log_total, dout, dq, total):
    lane = lax.broadcasted_iota(jnp.int32, (256, 256), 1)
    total[...] = jnp.zeros_like(total)
    for c, (start, count) in reversed(list(enumerate(windows(here.y)))):
        at = pl.ds(128 * c, 128)
        blocks = pl.ds(start, count)
        allowed = allowed_keys(table, c, start, count)
        q_both, d_both = both_heads(q, at), both_heads(dout, at)
        k = kv[blocks, :, 0:256].reshape(count * 128, 256)
        v = kv[blocks, :, 128:384].reshape(count * 128, 256)
        made = []
        for g in range(2):
            n = 2 * c + g
            q_one = jnp.where((lane >= HS) == (g == 1), q_both, jnp.zeros_like(q_both))
            d_one = jnp.where((lane >= 64 + HS) == (g == 1), d_both, jnp.zeros_like(d_both))
            scores = dot(k, q_one, 1, 1) * score_scale
            shares = jnp.where(allowed, jnp.exp(scores - log_total[n : n + 1]), 0.0)
            dshares = dot(v, d_one, 1, 1)
            inner = jnp.sum(shares * dshares, axis=0, keepdims=True)
            dscores = (shares * (dshares - inner)).astype(BF)
            made.append(dot(dscores, k, 0, 0))
            dk = dot(dscores, q_one) * score_scale
            dv = dot(shares.astype(BF), d_one)
            total[blocks, :, 0:256] += dk.reshape(count, 128, 256)
            total[blocks, :, 128:384] += dv.reshape(count, 128, 256)
        out = jnp.where(lane < HS, made[0], made[1]) * score_scale
        dq[at, 0:256] = out[:128]
        dq[at, 256:512] = out[128:]
        yield


def tokens_of(ref, pair=0):
    return ref[4 * pair : 4 * pair + 4].reshape(512, D)


def columns(n, size=256):
    return pl.ds(pl.multiple_of(n * size, size), size)


def back_to_width(units, weights, out, token_at=slice(None)):
    @pl.loop(0, D // 256)
    def _(n):
        made = dot(units(), weights[columns(n), :], 1, 1)
        out[:, token_at, columns(n)] = made.astype(BF).reshape(4, made.shape[0] // 4, 256)


def weight_grads(tokens, own, pair, main, rest, at):
    def made(n):
        total = dot(tokens[0:4, :, columns(n)].reshape(512, 256), own(), 0, 0)
        return total + dot(tokens[4:8, :, columns(n)].reshape(512, 256), pair(), 0, 0)

    @pl.loop(0, 4)
    def _(n):
        value = made(n)
        main[n, :, :, :, at] = value.astype(BF).reshape(2, 2, 64, value.shape[1])

    @pl.loop(0, 2)
    def _(n):
        value = made(n + 4)
        rest[pl.ds(2 * n, 2), :, :, :, at] = value.astype(BF).reshape(2, 2, 2, 32, value.shape[1])


def norm_back(value, grad, gain):
    scale = lax.rsqrt(jnp.mean(value * value, axis=1, keepdims=True) + norm_epsilon)
    unit = value * scale
    scaled = grad * gain
    inner = jnp.mean(scaled * unit, axis=1, keepdims=True)
    return scale * (scaled - unit * inner), jnp.sum(grad * unit, axis=0, keepdims=True)


def normed(value, gain):
    scale = lax.rsqrt(jnp.mean(value * value, axis=1, keepdims=True) + norm_epsilon)
    return (value * scale * gain).astype(BF)


def key_block(c, y):
    return 4 * c + y


def pack_rows(here, out, values):
    for y in range(4):
        for zl in range(2):
            block = values[zl, :, 128 * y : 128 * y + 128]
            rest = block[128:]
            swapped = pltpu.roll(rest, 64, 1)
            first = jnp.where(here.zl == 0, rest, swapped)
            second = jnp.where(here.zl == 0, swapped, rest)
            out[2 * y + zl, 0:128, :] = block[:128].T.astype(BF)
            both = jnp.concatenate([first, second], axis=0).T
            out[2 * y + zl, 128:192, :] = both[0:64].astype(BF)


def own_half(here, rest):
    return jnp.where(here.zl == 0, rest, pltpu.roll(rest, 64, 1))


def enter_kernel(
    stream, cotangent, qkv_weight, out_weight, gate_up, down, gains, positions, frequency, qkv_at, out_at,
    h1_out, wq_out, wo_out, c_out, kv_out, down_out, w_both,
    q_out, heads_out, cosine_out, sine_out, xtok_out, ctok_out,
    rise, h2_own, log_total, gtok, table,
    q, heads, cosine, sine, xtok, ctok,
    xf, cf, qf, of, gf, df, qs, os, xin, cin, wq_own, wo_own, win,
    xbuf, cbuf, h1_all, c_all, wq, wo, part, far, near, kv_own, kv_all, qkv, gpad, send, recv, local,
):
    here = Place()
    wire = Wire(send, recv, local)
    x_load = wire.stay(stream, xf)
    greet(
        [here.in_row(s) for s in range(1, 8)]
        + ring_partners(here)
        + [here.at(dz=1), here.at(dz=-1), here.pair()]
    )
    gpad[...] = jnp.zeros_like(gpad)
    gpad[0:2, 0:192] = gains[...]
    g = gpad[...]
    high = g.astype(BF).astype(F32)
    rows4 = jnp.concatenate([high[0:2], (g - high)[0:2]], axis=0)
    rest = rows4[:, 128:]
    rest = jnp.where(here.zl == 0, rest, pltpu.roll(rest, 64, 1))
    rows16 = jnp.concatenate([rows4[:, :128], rest, jnp.zeros((8, 128), F32)], axis=0).astype(BF)
    wire.there(x_load)
    q_load = wire.stay(qkv_weight, qf), wire.stay(qkv_at, qs)
    for r in range(8):
        xin[r, 192:208, :] = rows16
    pack_rows(here, xin, xf)
    xs = swap_rows(wire, here, xin, xbuf)
    xbuf[here.row] = xin[here.row]
    o_load = wire.stay(out_weight, of), wire.stay(out_at, os)
    c_load = wire.stay(cotangent, cf)
    f_load = [wire.stay(gate_up.at[:, j], gf.at[j]) for j in range(2)] + [wire.stay(down, df)]

    wire.there(*q_load)
    wq_own[...] = dot(qf[...].astype(BF), qs[...], 1, 1).astype(BF)
    q_weights = weight_gather(wire, here, wq_own, wq)
    next(q_weights)
    wire.there(*o_load)
    wo_own[...] = dot(of[...].astype(BF), os[...], 1, 1).astype(BF)
    o_weights = weight_gather(wire, here, wo_own, wo)
    lane = lax.broadcasted_iota(jnp.int32, (128, 256), 1)
    for c in range(4):
        first = 512 * c + 128 * here.y
        place = positions[:, pl.ds(pl.multiple_of(first, 128), 128)]
        place = jnp.where(here.zl == 0, place[0:1], place[1:2])
        token = first + lax.broadcasted_iota(jnp.int32, (1, 128), 1)
        table[2 * c : 2 * c + 1, :] = jnp.concatenate([token - place] * 2, axis=1)
        table[2 * c + 1 : 2 * c + 2, :] = jnp.concatenate([token] * 2, axis=1)
        column = jnp.broadcast_to(place.astype(F32), (128, 128)).T[:, 0:1]
        angles = column * frequency[0:1]
        at = pl.ds(128 * c, 128)
        cosine[at, :] = jnp.where(lane < 2 * HS, jnp.cos(angles), 0.0)
        sine[at, :] = jnp.where(lane < 2 * HS, jnp.sin(angles), 0.0)
    wire.stay(cosine, cosine_out)
    wire.stay(sine, sine_out)
    wire.there(c_load)
    pack_rows(here, cin, cf)
    cbuf[here.row] = cin[here.row]

    wire.arrive(*xs)
    x = widened(xbuf)
    xtok[...] = x
    wire.stay(xtok, xtok_out)
    g = widened_rows(xbuf, 192, 4).astype(F32)
    g = g[0:2] + g[2:4]
    gtok[...] = g
    h1_all[here.x] = normed(x.astype(F32), g[0:1])
    h1_flow = share(wire, here, h1_all)
    next(h1_flow)
    next(q_weights)
    wire.there(*f_load)
    for k in range(2):
        for j in range(2):
            at = 1024 * k + 512 * j
            win[:, at : at + 512] = gf[j, :, 512 * k : 512 * k + 512].astype(BF)
    win[:, 2048:3072] = df[...].astype(BF)
    wire.stay(win.at[:, pl.ds(2048, 1024)], down_out)
    side_by_side(h1_flow, q_weights)
    wire.stay(wq, wq_out)
    wire.stay(h1_all, h1_out)
    next(o_weights)
    cs = swap_rows(wire, here, cin, cbuf)

    @pl.loop(0, 3)
    def _(n):
        qkv[:, columns(n)] = dot(tokens_of(h1_all), wq[:, columns(n)])

    for c in range(4):
        at = pl.ds(128 * c, 128)
        turn = cosine[at], sine[at]
        key = turned(qkv[at, 384:640], *turn)
        value = jnp.where(lane < 64, 0.0, qkv[at, 512:768])
        kv = packed_pair(key, value).astype(BF)
        kv_own[c] = kv
        kv_all[key_block(c, here.y)] = kv

    keys = ring_gather(
        wire,
        here.y,
        here.at(dy=1),
        here.at(dy=-1),
        lambda h: [kv_own.at[2 * h + n] for n in range(2)],
        lambda i, h: [kv_all.at[key_block(2 * h + n, i)] for n in range(2)],
    )
    next(keys)
    for c in range(4):
        at = pl.ds(128 * c, 128)
        turn = cosine[at], sine[at]
        q[at, 0:256] = turned(qkv[at, 0:256], *turn).astype(BF)
        second = pltpu.roll(qkv[at, 128:384], 192, 1)
        q[at, 256:512] = turned(second, *turn).astype(BF)
    next(o_weights)
    next(keys)
    wire.arrive(*cs)
    c_value = widened(cbuf)
    ctok[...] = c_value
    wire.stay(ctok, ctok_out)
    c_all[here.x] = c_value
    c_flow = share(wire, here, c_all)
    next(c_flow)
    weights = weight_gather(wire, here, win.at[:, pl.ds(0, 2048)], w_both, True)
    next(weights)
    next(o_weights)
    side_by_side(keys)
    next(weights)
    for c, _ in enumerate(attend(here, q, kv_all, table, heads, log_total)):
        next(o_weights, None)
        next(o_weights, None)
        if c % 2 == 0:
            next(c_flow)
    side_by_side(o_weights, c_flow)
    for held, out in ((c_all, c_out), (wo, wo_out), (kv_all, kv_out), (q, q_out)):
        wire.stay(held, out)
    wire.stay(heads, heads_out)
    back_to_width(lambda: heads[...], wo, part)
    chain = x_sum(wire, here, part, far, near, rise)
    next(chain)
    next(weights)
    next(weights)
    next(chain)
    next(weights)
    side_by_side(chain, weights)
    h2_own[...] = normed(rise[...] + xtok[...].astype(F32), gtok[1:2])
    wire.finish()


def shape(dtype, *sizes):
    return jax.ShapeDtypeStruct(sizes, dtype)


def signals(*counts):
    return [pltpu.SemaphoreType.DMA((n,)) for n in counts]


def settings(number):
    return pltpu.CompilerParams(
        collective_id=number, has_side_effects=True, vmem_limit_bytes=60 << 20
    )


def enter(*operands):
    return pl.pallas_call(
        enter_kernel,
        out_shape=[
            shape(BF, 4, 128, D),
            shape(BF, D, 768),
            shape(BF, D, 512),
            shape(BF, 4, 128, D),
            shape(BF, 16, 128, 384),
            shape(BF, 192, 1024),
            shape(BF, D, 2048),
            shape(BF, 512, 512),
            shape(BF, 512, 512),
            shape(F32, 512, 256),
            shape(F32, 512, 256),
            shape(BF, 128, D),
            shape(BF, 128, D),
            shape(F32, 128, D),
            shape(BF, 128, D),
            shape(F32, 8, 256),
            shape(F32, 2, D),
            shape(jnp.int32, 8, 256),
        ],
        in_specs=[ANY] * 6 + [VM] * 3 + [ANY] * 2,
        out_specs=[ANY] * 13 + [VM] * 5,
        scratch_shapes=[
            pltpu.VMEM((512, 512), BF),
            pltpu.VMEM((512, 512), BF),
            pltpu.VMEM((512, 256), F32),
            pltpu.VMEM((512, 256), F32),
            pltpu.VMEM((128, D), BF),
            pltpu.VMEM((128, D), BF),
            pltpu.VMEM((2, 192, 512), F32),
            pltpu.VMEM((2, 192, 512), F32),
            pltpu.VMEM((192, 768), F32),
            pltpu.VMEM((192, 384), F32),
            pltpu.VMEM((2, 192, 1024), F32),
            pltpu.VMEM((192, 1024), F32),
            pltpu.VMEM((768, 768), BF),
            pltpu.VMEM((512, 384), BF),
            pltpu.VMEM((8, 208, 128), BF),
            pltpu.VMEM((8, 192, 128), BF),
            pltpu.VMEM((192, 768), BF),
            pltpu.VMEM((192, 512), BF),
            pltpu.VMEM((192, 3072), BF),
            pltpu.VMEM((8, 208, 128), BF),
            pltpu.VMEM((8, 192, 128), BF),
            pltpu.VMEM((4, 128, D), BF),
            pltpu.VMEM((4, 128, D), BF),
            pltpu.VMEM((D, 768), BF),
            pltpu.VMEM((D, 512), BF),
            pltpu.VMEM((4, 128, D), BF),
        ]
        + x_sum_scratch()
        + [
            pltpu.VMEM((4, 128, 384), BF),
            pltpu.VMEM((16, 128, 384), BF),
            pltpu.VMEM((512, 768), F32),
            pltpu.VMEM((8, 256), F32),
        ]
        + signals(256, 256, 32),
        compiler_params=settings(1),
        name="enter",
    )(*operands)


BOTH = (1024, 512)
DOWN = (512, 256)


def feed_kernel(*refs):
    h2_own, gtok, rise_in, xtok_in, ctok_in, down_own, both_w, c_in = refs[:8]
    after_out, gain, f_out, d_out = refs[8:12]
    both_sums, down_sums = refs[12:16], refs[16:20]
    after, f_part, far, near, middle, summed, h2_all, c_all = refs[20:28]
    w_down, w_both, both, act, both_in, act_in, hidden, part2, d_all = refs[28:37]
    main, rest, down_main, down_rest = refs[37:41]
    rise, xtok, ctok = refs[41:44]
    both_first, down_first, (send, recv, local) = refs[44:52], refs[52:60], refs[60:]
    here = Place()
    wire = Wire(send, recv, local)
    greet(ring_partners(here) + plane_partners(here) + [here.pair()])
    h2_all[here.x] = h2_own[...]
    chain = share(wire, here, h2_all)
    next(chain)
    down = weight_gather(wire, here, down_own, w_down)
    next(down)
    loads = [wire.stay(a, b) for a, b in ((rise_in, rise), (xtok_in, xtok), (ctok_in, ctok))]
    loads += [wire.stay(c_in, c_all.at[pl.ds(0, 4)]), wire.stay(both_w, w_both)]
    next(chain)
    next(down)
    next(down)
    next(chain)
    next(down)
    side_by_side(chain)
    wire.there(*loads)
    middle[...] = rise[...] + xtok[...].astype(F32)
    paired = [to_pair(wire, here, h2_all)]

    @pl.loop(0, 8)
    def _(n):
        hidden[:, columns(n)] = dot(tokens_of(h2_all), w_both[:, columns(n)])

    side_by_side(down)

    def unit_tiles(half):
        @pl.loop(0, 2)
        def _(n):
            at, down_at = columns(half * 4 + n), columns(half * 2 + n)
            up_at = columns(half * 4 + n + 2)
            gate, up = hidden[:, at], hidden[:, up_at]
            grad = dot(tokens_of(c_all), w_down[:, down_at])
            sigmoid = 1.0 / (1.0 + jnp.exp(-gate))
            silu = gate * sigmoid
            both[:, at] = (grad * up * sigmoid * (1.0 + gate * (1.0 - sigmoid))).astype(BF)
            both[:, up_at] = (grad * silu).astype(BF)
            act[:, down_at] = (silu * up).astype(BF)

    other = 1 - here.core
    unit_tiles(other)
    paired.append(wire.copy(both.at[:, columns(other, 1024)], both_in, here.pair()))
    act_swap = wire.copy(act.at[:, columns(other, 512)], act_in, here.pair())
    c_paired = to_pair(wire, here, c_all)
    unit_tiles(here.core)
    back_to_width(lambda: both[...], w_both, part2)

    def backward():
        yield from x_sum(wire, here, part2, far, near, summed)
        left, gain_terms = norm_back(middle[...], summed[...], gtok[1:2])
        gain[...] = jnp.broadcast_to(gain_terms, gain.shape)
        after[...] = left
        d_all[here.x] = (left + ctok[...].astype(F32)).astype(BF)
        wire.stay(after, after_out)
        yield from share(wire, here, d_all)

    chain = backward()
    next(chain)
    back_to_width(lambda: act[...], w_down, f_part)
    wire.stay(f_part, f_out)
    wire.arrive(c_paired, act_swap)
    weight_grads(
        c_all, lambda: act[:, columns(here.core, 512)], lambda: act_in[...], down_main, down_rest, slice(None)
    )
    flows = first_sums(wire, here, (down_main, down_rest), down_first, down_sums, *DOWN)
    for flow in flows:
        next(flow)
    next(chain)
    wire.arrive(*paired)
    weight_grads(
        h2_all, lambda: both[:, columns(here.core, 1024)], lambda: both_in[...], main, rest, slice(None)
    )
    both_flows = first_sums(wire, here, (main, rest), both_first, both_sums, *BOTH)
    for flow in both_flows + flows:
        next(flow)
    next(chain)
    next(chain)
    for flow in both_flows:
        next(flow)
    next(chain)
    side_by_side(chain)
    wire.stay(d_all, d_out)
    side_by_side(*flows, *both_flows)
    wire.finish()


def grad_shapes(width):
    return [(4, 2, 2, high, width) for high in HIGHS]


def grad_arrays(width):
    return [pltpu.VMEM(sizes, BF) for sizes in grad_shapes(width)]


def feed(*operands):
    return pl.pallas_call(
        feed_kernel,
        out_shape=[
            shape(F32, 128, D),
            shape(F32, 8, D),
            shape(BF, 4, 128, D),
            shape(BF, 4, 128, D),
        ]
        + [shape(BF, *sizes) for sizes in half_sums(*BOTH) + half_sums(*DOWN)],
        in_specs=[VM] * 2 + [ANY] * 6,
        out_specs=[ANY, VM] + [ANY] * 2 + [VM] * 8,
        scratch_shapes=[
            pltpu.VMEM((128, D), F32),
            pltpu.VMEM((4, 128, D), BF),
        ]
        + x_sum_scratch()
        + [
            pltpu.VMEM((128, D), F32),
            pltpu.VMEM((128, D), F32),
            pltpu.VMEM((8, 128, D), BF),
            pltpu.VMEM((8, 128, D), BF),
            pltpu.VMEM((D, 1024), BF),
            pltpu.VMEM((D, 2048), BF),
            pltpu.VMEM((512, 2048), BF),
            pltpu.VMEM((512, 1024), BF),
            pltpu.VMEM((512, 1024), BF),
            pltpu.VMEM((512, 512), BF),
            pltpu.VMEM((512, 2048), F32),
            pltpu.VMEM((4, 128, D), BF),
            pltpu.VMEM((4, 128, D), BF),
        ]
        + grad_arrays(BOTH[0])
        + grad_arrays(DOWN[0])
        + [pltpu.VMEM((128, D), F32), pltpu.VMEM((128, D), BF), pltpu.VMEM((128, D), BF)]
        + first_scratch(*BOTH)
        + first_scratch(*DOWN)
        + signals(200, 200, 16),
        compiler_params=settings(2),
        name="feed",
    )(*operands)


ATTN = (640, 256)


def leave_held():
    sizes = [(4, 128, D)]
    sizes += half_sums(*BOTH) + half_sums(*DOWN)
    sizes += [(4, 128, D), (D, 512), (512, 512), (16, 128, 384), (512, 512), (4, 128, D)]
    sizes += [(D, 768), (128, D)]
    return [(size, BF) for size in sizes] + [
        ((128, D), F32), ((128, D), F32), ((512, 256), F32), ((512, 256), F32)
    ]


def leave_kernel(*refs):
    gtok, gain, log_total, table = refs[:4]
    count = len(leave_held())
    held_in, refs = refs[4 : 4 + count], refs[4 + count :]
    o_all, s_all, gout, both_out, down_out, gains_out = refs[:6]
    held, refs = refs[6 : 6 + count], refs[6 + count :]
    f_part, both_sums, down_sums = held[0], held[1:5], held[5:9]
    d_all, wo, q, kv_all, heads, h1_all, wq, xtok, rise, after, cosine, sine = held[9:]
    dout, dq, total, dkv, kfar, knear, dkv_own, dqkv = refs[:8]
    heads_in, dqkv_in, part, far, near, far2, near2, summed, osend, ssend = refs[8:18]
    gsend, grow, gcol, gdp, main, rest = refs[18:24]
    scratch, (send, recv, local) = refs[24:-3], refs[-3:]
    a_first, a_sums, a_second = scratch[:8], scratch[8:12], scratch[12:21]
    both_second, down_second = scratch[21:30], scratch[30:39]
    here = Place()
    wire = Wire(send, recv, local)
    def load(first, last):
        made = []
        for src, dst in zip(held_in[first:last], held[first:last]):
            dst = dst.at[pl.ds(0, 4)] if dst.shape != src.shape else dst
            made.append(wire.stay(src, dst))
        return made

    attention_loads = load(9, 14)
    greet(
        [here.in_row(s) for s in range(1, 8)]
        + ring_partners(here)
        + [here.at(dz=1), here.at(dz=-1), here.at(dx=2)]
        + [here.in_dp(s) for s in range(1, 4)]
    )
    wire.there(*attention_loads)
    sums_loads = load(0, 9)

    @pl.loop(0, 2)
    def _(n):
        dout[:, columns(n)] = dot(tokens_of(d_all), wo[:, columns(n)]).astype(BF)

    heads_swap = wire.copy(heads.at[:, columns(1 - here.core)], heads_in, here.pair())
    wire.there(*sums_loads)
    branch_sum = x_sum(wire, here, f_part, far, near, summed)
    next(branch_sum)
    sums = second_sums(wire, here, both_sums, both_second, *BOTH)
    sums += second_sums(wire, here, down_sums, down_second, *DOWN)
    for flow in sums:
        next(flow)
    d_paired = to_pair(wire, here, d_all)
    late_loads = load(14, count)

    def key_sums(half):
        block = lambda h: 2 * half + h
        return ring_sum(
            wire,
            here.y,
            here.at(dy=1),
            here.at(dy=-1),
            lambda i, h: [dkv.at[key_block(block(h), i)]],
            lambda h: [kfar.at[half, h]],
            lambda s, h: [knear.at[half, s, h]],
            lambda h: [dkv_own.at[pl.ds(128 * block(h), 128)]],
        )

    attention = attend_back(here, q, kv_all, table, log_total, dout, dq, total)
    next(attention)
    for flow in sums:
        next(flow)
    next(attention)
    next(branch_sum)
    dkv[8:16] = total[8:16].astype(BF)
    late_keys = key_sums(1)
    next(late_keys)
    next(attention)
    next(late_keys)
    next(attention)
    dkv[0:8] = total[0:8].astype(BF)
    keys = key_sums(0)
    next(keys)
    wire.there(*late_loads)
    side_by_side(*sums)
    both_share = grad_share(wire, here, both_second[-1], both_out, BOTH[0])
    down_share = grad_share(wire, here, down_second[-1], down_out, DOWN[0])
    next(both_share)
    next(down_share)
    h1_paired = to_pair(wire, here, h1_all)
    side_by_side(branch_sum)
    narrowed(osend, summed[...] + rise[...])
    for c in range(4):
        at = pl.ds(128 * c, 128)
        turn = cosine[at], -sine[at]
        second = turned(dq[at, 256:512], *turn)
        both = packed_pair(turned(dq[at, 0:256], *turn), pltpu.roll(second, 64, 1))
        dqkv[at, 0:384] = both.astype(BF)
    next(keys)
    wire.arrive(heads_swap, d_paired)
    weight_grads(
        d_all, lambda: heads[:, columns(here.core)], lambda: heads_in[...], main, rest, slice(384, 640)
    )
    lane = lax.broadcasted_iota(jnp.int32, (128, 256), 1)
    side_by_side(late_keys, keys)
    for c in range(4):
        at = pl.ds(128 * c, 128)
        key = turned(dkv_own[at, 0:256], cosine[at], -sine[at])
        value = jnp.where(lane < 64, 0.0, dkv_own[at, 128:384])
        dqkv[at, 384:768] = packed_pair(key, value).astype(BF)
    dqkv_swap = wire.copy(dqkv.at[:, columns(1 - here.core, 384)], dqkv_in, here.pair())
    back_to_width(lambda: dqkv[...], wq, part)

    def chain():
        yield from x_sum(wire, here, part, far2, near2, summed)
        left, gain_terms = norm_back(xtok[...].astype(F32), summed[...], gtok[0:1])
        gains = jnp.concatenate([gain_terms, gain[0:1], jnp.zeros((6, D), F32)], axis=0)
        narrowed_rows(gsend, gains)
        g = swap_rows(wire, here, gsend, grow)
        narrowed(ssend, left + after[...])
        wire.stay(ssend.at[here.row], s_all.at[here.row])
        swap_rows(wire, here, ssend, s_all)
        yield
        wire.arrive(*g)
        grow[here.row] = gsend[here.row]
        total = grow[0]
        for n in range(1, 8):
            total = total + grow[n]
        gcol[here.x] = total
        g = [wire.copy(gcol.at[here.x], gcol.at[here.x], here.at(dx=s)) for s in range(1, 4)]
        yield
        wire.arrive(*g)
        gdp[here.dp] = ((gcol[0] + gcol[1]) + gcol[2]) + gcol[3]
        g = [wire.copy(gdp.at[here.dp], gdp.at[here.dp], here.in_dp(s)) for s in range(1, 4)]
        yield
        wire.arrive(*g)
        gains_out[...] = ((gdp[0] + gdp[1]) + gdp[2]) + gdp[3]

    steps = chain()
    next(steps)
    side_by_side(both_share, down_share)
    wire.stay(osend.at[here.row], o_all.at[here.row])
    swap_rows(wire, here, osend, o_all)
    wire.arrive(dqkv_swap, h1_paired)
    weight_grads(
        h1_all, lambda: dqkv[:, columns(here.core, 384)], lambda: dqkv_in[...], main, rest, slice(0, 384)
    )
    first = first_sums(wire, here, (main, rest), a_first, a_sums, *ATTN)

    def sums():
        yield
        side_by_side(*first)
        second = second_sums(wire, here, a_sums, a_second, *ATTN)
        for flow in second:
            next(flow)
        yield
        for flow in second:
            next(flow)
        yield
        side_by_side(*second)
        yield from grad_share(wire, here, a_second[-1], gout, ATTN[0])

    for flow in first:
        next(flow)
    next(steps)
    for flow in first:
        next(flow)
    side_by_side(steps, sums())
    wire.finish()


def leave(*operands):
    held = [pltpu.VMEM(size, kind) for size, kind in leave_held()]
    for n in (9, 14):
        held[n] = pltpu.VMEM((8, 128, D), BF)
    return pl.pallas_call(
        leave_kernel,
        out_shape=[
            shape(BF, 8, 192, 128),
            shape(BF, 8, 192, 128),
            shape(BF, 2, 96, 2 * ATTN[0]),
            shape(BF, 2, 96, 2 * BOTH[0]),
            shape(BF, 2, 96, 2 * DOWN[0]),
            shape(F32, 8, 256),
        ],
        in_specs=[VM] * 4 + [ANY] * len(held),
        out_specs=[ANY] * 5 + [VM],
        scratch_shapes=held
        + [
            pltpu.VMEM((512, 512), BF),
            pltpu.VMEM((512, 512), F32),
            pltpu.VMEM((16, 128, 384), F32),
            pltpu.VMEM((16, 128, 384), BF),
            pltpu.VMEM((2, 2, 128, 384), BF),
            pltpu.VMEM((2, 2, 2, 128, 384), BF),
            pltpu.VMEM((512, 384), F32),
            pltpu.VMEM((512, 768), BF),
            pltpu.VMEM((512, 256), BF),
            pltpu.VMEM((512, 384), BF),
            pltpu.VMEM((4, 128, D), BF),
        ]
        + x_sum_scratch()
        + x_sum_scratch()
        + [
            pltpu.VMEM((128, D), F32),
            pltpu.VMEM((8, 192, 128), BF),
            pltpu.VMEM((8, 192, 128), BF),
            pltpu.VMEM((8, 8, 256), F32),
            pltpu.VMEM((8, 8, 256), F32),
            pltpu.VMEM((4, 8, 256), F32),
            pltpu.VMEM((4, 8, 256), F32),
        ]
        + grad_arrays(ATTN[0])
        + first_scratch(*ATTN)
        + [pltpu.VMEM(sizes, BF) for sizes in half_sums(*ATTN)]
        + second_scratch(*ATTN)
        + second_scratch(*BOTH)
        + second_scratch(*DOWN)
        + signals(240, 240, 32),
        compiler_params=settings(3),
        name="leave",
    )(*operands)


def step_rates():
    return (2.0 / D**0.5, 2.0 / max(HQ * HS // 64, 1) ** 0.5, 2.0 / D**0.5, 2.0 / FF**0.5, 0.4)


def adamw(state, at, gradient, step_rate, decay_rate):
    weight, first, second = state
    moment_one = beta_first * first[at] + (1.0 - beta_first) * gradient
    moment_two = beta_second * second[at] + (1.0 - beta_second) * gradient * gradient
    first[at] = moment_one
    second[at] = moment_two
    corrected = (moment_one * (1.0 / (1.0 - beta_first**STEP))) / (
        jnp.sqrt(moment_two * (1.0 / (1.0 - beta_second**STEP))) + adam_epsilon
    )
    old = weight[at]
    weight[at] = old - step_rate * (corrected + decay_rate * old)


def update_kernel(*refs):
    stream, cotangent, o_in, s_in, g_in, both_in, down_in, qkv_at, out_at = refs[:9]
    qkv, out, gate_up, down, gains = (refs[9 + 3 * n : 12 + 3 * n] for n in range(5))
    gains_tile = refs[24]
    o_out, s_out = refs[25:27]
    results = [refs[27 + 3 * n : 30 + 3 * n] for n in range(5)]
    xf, cf, ot, st, gb, fb, db, qs, os = refs[42:51]
    qkv_s, out_s, gate_s, down_s = (refs[51 + 3 * n : 54 + 3 * n] for n in range(4))
    local = refs[63]
    here = Place()
    wire = Wire(None, None, local)
    rate_qkv, rate_out, rate_gate_up, rate_down, rate_gains = step_rates()

    f_load = [wire.stay(both_in, fb)]
    for a, b in zip(gate_up, gate_s):
        f_load += [wire.stay(a.at[:, j], b.at[j]) for j in range(2)]
    d_load = [wire.stay(down_in, db)] + [wire.stay(a, b) for a, b in zip(down, down_s)]
    x_load = [wire.stay(a, b) for a, b in ((stream, xf), (o_in, ot), (cotangent, cf), (s_in, st))]
    a_load = [wire.stay(a, b) for a, b in ((g_in, gb), (qkv_at, qs), (out_at, os))]
    a_load += [wire.stay(a, b) for a, b in zip(qkv + out, qkv_s + out_s)]

    def feed_part(states, grads):
        @pl.loop(0, 4)
        def _(n):
            zh, k = lax.div(n, 2), lax.rem(n, 2)
            for start, size, begin in ((0, 64, 64 * zh), (64, 32, 128 + 32 * zh)):
                at = pl.ds(pl.multiple_of(begin, 32), size), columns(k, 512)
                for a, (state, rate) in enumerate(states):
                    lanes = columns(len(states) * k + a, 512)
                    gradient = grads[zh, start : start + size, lanes].astype(F32)
                    adamw(state, at, gradient, rate, weight_decay)

    wire.there(*f_load)
    feed_part([([b.at[j] for b in gate_s], rate_gate_up) for j in range(2)], fb)
    for a, b in zip(results[2], gate_s):
        for j in range(2):
            wire.stay(b.at[j], a.at[:, j])
    wire.there(*d_load)
    feed_part([(down_s, rate_down)], db)
    for a, b in zip(results[3], down_s):
        wire.stay(b, a)

    wire.there(*x_load)
    for held, tiles, result in ((xf, ot, o_out), (cf, st, s_out)):
        for y in range(4):
            for zl in range(2):
                tile = tiles[2 * y + zl].astype(F32)
                rest = jnp.concatenate([tile[128:192]] * 2, axis=0).T
                rest = jnp.where(low_lanes(64), rest[0:64], rest[64:128])
                at = pl.ds(128 * y, 128)
                held[zl, 0:128, at] = held[zl, 0:128, at] + tile[0:128].T
                held[zl, 128:192, at] = held[zl, 128:192, at] + rest
        wire.stay(held, result)

    wire.there(*a_load)

    def own_block(start, size):
        lanes = [pl.ds(ATTN[0] * k + start, size) for k in range(2)]
        parts = [(0, slice(0, 64)), (1, slice(0, 64)), (0, slice(64, 96)), (1, slice(64, 96))]
        return jnp.concatenate(
            [jnp.concatenate([gb[zh, at, l] for zh, at in parts], axis=0) for l in lanes], axis=1
        )

    gradient = dot(own_block(0, 384), qs[...])
    adamw(qkv_s, (slice(None), slice(None)), gradient, rate_qkv, weight_decay)
    gradient = dot(own_block(384, 256), os[...])
    adamw(out_s, (slice(None), slice(None)), gradient, rate_out, weight_decay)
    for a, b in zip(results[0] + results[1], qkv_s + out_s):
        wire.stay(b, a)

    tile = gains_tile[...]
    rest = own_half(here, tile[:, 128:])
    for old, new in zip(gains, results[4]):
        new[...] = old[...]
    adamw(results[4], (slice(None), slice(0, 128)), tile[0:2, 0:128], rate_gains, 0.0)
    adamw(results[4], (slice(None), slice(128, 192)), rest[0:2, 0:64], rate_gains, 0.0)
    wire.finish()


def update(*operands):
    sizes = [(192, 768)] * 3 + [(192, 384)] * 3 + [(192, 2, 1024)] * 3 + [(192, 1024)] * 3
    held = [(192, 768)] * 3 + [(192, 384)] * 3 + [(2, 192, 1024)] * 3 + [(192, 1024)] * 3
    return pl.pallas_call(
        update_kernel,
        out_shape=[shape(F32, 2, 192, 512)] * 2
        + [shape(F32, *size) for size in sizes]
        + [shape(F32, 2, 192)] * 3,
        in_specs=[ANY] * 21 + [VM] * 4,
        out_specs=[ANY] * 14 + [VM] * 3,
        scratch_shapes=[
            pltpu.VMEM((2, 192, 512), F32),
            pltpu.VMEM((2, 192, 512), F32),
            pltpu.VMEM((8, 192, 128), BF),
            pltpu.VMEM((8, 192, 128), BF),
            pltpu.VMEM((2, 96, 2 * ATTN[0]), BF),
            pltpu.VMEM((2, 96, 2 * BOTH[0]), BF),
            pltpu.VMEM((2, 96, 2 * DOWN[0]), BF),
            pltpu.VMEM((768, 768), BF),
            pltpu.VMEM((512, 384), BF),
        ]
        + [pltpu.VMEM(size, F32) for size in held]
        + signals(64),
        compiler_params=pltpu.CompilerParams(vmem_limit_bytes=60 << 20),
        name="update",
    )(*operands)


def body(
    stream,
    cotangent,
    segments,
    positions,
    qkv_weight,
    qkv_first,
    qkv_second,
    out_weight,
    out_first,
    out_second,
    gate_up_weight,
    gate_up_first,
    gate_up_second,
    down_weight,
    down_first,
    down_second,
    gains,
    gains_first,
    gains_second,
):
    frequency = rope_theta ** (-2.0 * (jnp.arange(256) % (HS // 2)).astype(F32) / HS)
    frequency = jnp.broadcast_to(frequency, (8, 256))
    qkv_at, out_at = qkv_order(), out_order()
    stream_turned, cotangent_turned = stream.transpose(1, 2, 0), cotangent.transpose(1, 2, 0)
    (
        h1_all, wq, wo, c_all, kv_all, down_own, w_both,
        q, heads, cosine, sine, xtok, ctok, rise, h2_own, log_total, gtok, table,
    ) = enter(
        stream_turned, cotangent_turned, qkv_weight, out_weight.T, gate_up_weight, down_weight.T,
        gains, positions, frequency, qkv_at, out_at,
    )
    after, gain_two, f_part, d_all, *sums = feed(
        h2_own, gtok, rise, xtok, ctok, down_own, w_both, c_all
    )
    o_tiles, s_tiles, attn_grads, both_grads, down_grads, gains_tile = leave(
        gtok, gain_two, log_total, table,
        f_part, *sums, d_all, wo, q, kv_all, heads, h1_all, wq, xtok, rise, after, cosine, sine,
    )
    made = update(
        stream_turned, cotangent_turned, o_tiles, s_tiles, attn_grads, both_grads, down_grads, qkv_at, out_at,
        qkv_weight, qkv_first, qkv_second,
        out_weight.T, out_first.T, out_second.T,
        gate_up_weight, gate_up_first, gate_up_second,
        down_weight.T, down_first.T, down_second.T,
        gains, gains_first, gains_second,
        gains_tile,
    )
    output, stream_grad = made[0].transpose(2, 0, 1), made[1].transpose(2, 0, 1)
    states = [made[2 + 3 * n : 5 + 3 * n] for n in range(5)]
    for n in (1, 3):
        states[n] = [a.T for a in states[n]]
    return (output, stream_grad, *(a for w, m, v in states for a in (m, v, w)))


def solution(mesh):
    tokens = P("col", "dp", "row")
    table = P("dp", None)
    wide, tall, pairs, both = P("row", "col"), P("col", "row"), P("row", None, "col"), P(None, "row")
    weights = (wide,) * 3 + (tall,) * 3 + (pairs,) * 3 + (tall,) * 3 + (both,) * 3
    return jax.shard_map(
        body,
        mesh=mesh,
        in_specs=(tokens, tokens, table, table, *weights),
        out_specs=(tokens, tokens, *weights),
        check_vma=False,
    )
```

```python
import functools

import jax
import jax.numpy as jnp
import numpy as np
from jax import lax
from jax.experimental import pallas as pl
from jax.experimental.pallas import tpu as pltpu
from jax.sharding import PartitionSpec as P

D = 1536
FF = 4096
HQ = 16
KVH = 8
HS = 96
STEP = 10
LEN = 2048
WINDOW = 1024

norm_epsilon = 1e-05
rope_theta = 100000.0
beta_first = 0.9
beta_second = 0.95
adam_epsilon = 1e-08
weight_decay = 0.1
score_scale = HS**-0.5

MESH = pl.DeviceIdType.MESH
BF = jnp.bfloat16
F32 = jnp.float32
VM = pl.BlockSpec(memory_space=pltpu.VMEM)
ANY = pl.BlockSpec(memory_space=pl.ANY)


def selection(source, count):
    chosen = np.zeros((count, len(source)), np.float32)
    chosen[source, np.arange(len(source))] = 1.0
    return jnp.asarray(chosen, BF)


def qkv_order():
    b = np.arange(768)
    return selection(b % 384 // HS * 192 + b // 384 * HS + b % HS, 768)


def out_order():
    b = np.arange(384)
    return selection(b % 192 // HS * 256 + 64 + b // 192 * HS + b % HS, 512)


class Place:
    def __init__(self):
        self.dp = lax.axis_index("dp")
        self.row = lax.axis_index("row")
        self.x = lax.axis_index("col")
        self.zh = lax.div(self.dp, 2)
        self.core = lax.rem(self.dp, 2)
        self.y = lax.div(self.row, 2)
        self.zl = lax.rem(self.row, 2)
        self.z = self.zh * 2 + self.zl

    def at(self, dx=0, dy=0, dz=0, dcore=0):
        x = lax.rem(self.x + (dx + 4), 4)
        y = lax.rem(self.y + (dy + 4), 4)
        z = lax.rem(self.z + (dz + 4), 4)
        core = lax.rem(self.core + dcore, 2)
        return (lax.div(z, 2) * 2 + core, y * 2 + lax.rem(z, 2), x)

    def pair(self):
        return self.at(dcore=1)

    def in_row(self, step):
        return (self.dp, lax.rem(self.row + step, 8), self.x)

    def in_dp(self, step):
        return (lax.rem(self.dp + step, 4), self.row, self.x)


def greet(devices):
    barrier = pltpu.get_barrier_semaphore()
    for device in devices:
        pl.semaphore_signal(barrier, inc=1, device_id=device, device_id_type=MESH)
    pl.semaphore_wait(barrier, len(devices))


class Wire:
    def __init__(self, send, recv, local=None):
        self.send, self.recv, self.local = send, recv, local
        self.sent, self.open, self.near, self.stays = [], {}, [], 0

    def copy(self, src, dst, device):
        n = len(self.sent)
        made = pltpu.make_async_remote_copy(
            src_ref=src,
            dst_ref=dst,
            send_sem=self.send.at[n],
            recv_sem=self.recv.at[n],
            device_id=device,
            device_id_type=MESH,
        )
        made.start()
        self.sent.append(made)
        self.open[n] = made
        return n

    def arrive(self, *numbers):
        for n in numbers:
            self.open.pop(n).wait_recv()

    def stay(self, src, dst):
        made = pltpu.make_async_copy(src, dst, self.local.at[self.stays])
        self.stays += 1
        made.start()
        self.near.append(made)
        return made

    def there(self, *stays):
        for made in stays:
            self.near = [other for other in self.near if other is not made]
            made.wait()

    def settle(self):
        self.arrive(*list(self.open))

    def finish(self):
        self.settle()
        for made in self.sent:
            made.wait_send()
        self.there(*list(self.near))


def around(me):
    return lax.rem(me + 3, 4), lax.rem(me + 1, 4), lax.rem(me + 2, 4)


def ring_gather(wire, me, right, left, own, slot):
    l, r, o = around(me)

    def send(src, dst, device):
        return [wire.copy(a, b, device) for a, b in zip(src, dst)]

    def pass_on(numbers, refs, device):
        passed = []
        for n, ref in zip(numbers, refs):
            wire.arrive(n)
            passed.append(wire.copy(ref, ref, device))
        return passed

    first = send(own(0), slot(me, 0), right), send(own(1), slot(me, 1), left)
    second = send(own(1), slot(me, 1), right), send(own(0), slot(me, 0), left)
    yield
    far = pass_on(first[0], slot(l, 0), right) + pass_on(first[1], slot(r, 1), left)
    yield
    wire.arrive(*second[0], *second[1])
    yield
    wire.arrive(*far)


def leading(ref):
    found = [()]
    for size in ref.shape[:-2]:
        found = [index + (n,) for index in found for n in range(size)]
    return found


def add_parts(out, refs):
    for index in leading(out):
        at = index + (slice(None), slice(None))
        total = refs[0][at].astype(F32)
        for ref in refs[1:]:
            total = total + ref[at].astype(F32)
        out[at] = total.astype(out.dtype)


def ring_sum(wire, me, right, left, part, far, near, out):
    l, r, o = around(me)

    def send(srcs, dsts, device):
        return [wire.copy(a, b, device) for a, b in zip(srcs, dsts)]

    far0 = send(part(o, 0), far(0), right)
    far1 = send(part(o, 1), far(1), left)
    to_right = send(part(r, 1), near(0, 1), right)
    to_left = send(part(l, 0), near(1, 0), left)
    yield
    for n, a, b, c in zip(far0, far(0), part(r, 0), near(0, 0)):
        wire.arrive(n)
        add_parts(a, [a, b])
        to_right.append(wire.copy(a, c, right))
    for n, a, b, c in zip(far1, far(1), part(l, 1), near(1, 1)):
        wire.arrive(n)
        add_parts(a, [a, b])
        to_left.append(wire.copy(a, c, left))
    yield
    wire.arrive(*to_right, *to_left)
    for h in range(2):
        for a, b, c, total in zip(part(me, h), near(0, h), near(1, h), out(h)):
            add_parts(total, [a, b, c])


def side_by_side(*flows):
    flows = list(flows)
    while flows:
        for flow in list(flows):
            try:
                next(flow)
            except StopIteration:
                flows.remove(flow)


def rows(ref, start, size, multiple):
    return ref.at[pl.ds(pl.multiple_of(start, multiple), size)]


def weight_gather(wire, here, own, whole, z_first=False):
    core, zl = here.core, here.zl
    right, left = here.at(dy=1), here.at(dy=-1)
    up, down = here.at(dz=1), here.at(dz=-1)
    l, r, o = around(here.y)

    def mine(j):
        start = (core * 64, core * 64 + 32, 128 + core * 32, 144 + core * 32)[j]
        return rows(own, start, (32, 32, 16, 16)[j], 16)

    def piece(y, j, lo):
        block = y * 2 + lo
        main, rest = block * 128 + core * 64, 1024 + block * 64 + core * 32
        start = (main, main + 32, rest, rest + 16)[j]
        return rows(whole, start, (32, 32, 16, 16)[j], 16)

    def to_pair(y, lo):
        block = y * 2 + lo
        for view in (
            rows(whole, block * 128 + core * 64, 64, 64),
            rows(whole, 1024 + block * 64 + core * 32, 32, 32),
        ):
            paired.append(wire.copy(view, view, here.pair()))

    paired = []

    def over(y, js, device, src=None):
        return [wire.copy((src or (lambda j: piece(y, j, zl)))(j), piece(y, j, zl), device) for j in js]

    y = here.y
    kept = (
        wire.stay(own.at[pl.ds(0, 128)], rows(whole, here.row * 128, 128, 128)),
        wire.stay(own.at[pl.ds(128, 64)], rows(whole, 1024 + here.row * 64, 64, 64)),
    )
    z_own = lambda: over(y, (0, 2), up, mine) + over(y, (1, 3), down, mine)
    if z_first:
        z_y = z_own()
        yield
    r_first, l_first = over(y, (0, 2), right, mine), over(y, (1, 3), left, mine)
    r_next, l_next = over(y, (1, 3), right, mine), over(y, (0, 2), left, mine)
    if not z_first:
        z_y = z_own()
    yield
    wire.arrive(*r_first)
    far = over(l, (0, 2), right)
    wire.arrive(*l_first)
    far += over(r, (1, 3), left)
    z_l = over(l, (0, 2), up)
    z_r = over(r, (1, 3), down)
    yield
    wire.arrive(*r_next)
    z_l += over(l, (1, 3), down)
    to_pair(l, zl)
    wire.arrive(*l_next)
    z_r += over(r, (0, 2), up)
    to_pair(r, zl)
    yield
    wire.arrive(*far)
    z_o = over(o, (0, 2), up) + over(o, (1, 3), down)
    to_pair(o, zl)
    yield
    for block, numbers in ((y, z_y), (l, z_l), (r, z_r), (o, z_o)):
        wire.arrive(*numbers)
        to_pair(block, 1 - zl)
        yield
    wire.arrive(*paired)
    wire.there(*kept)


def token_pieces(half):
    return [pl.ds(64 * half + n, 16) for n in range(0, 64, 16)]


def share(wire, here, out):
    half = lambda i, h: [out.at[i, at] for at in token_pieces(h)]
    return ring_gather(
        wire, here.x, here.at(dx=1), here.at(dx=-1), lambda h: half(here.x, h), half
    )


def to_pair(wire, here, out):
    return wire.copy(out.at[pl.ds(0, 4)], out.at[pl.ds(4, 4)], here.pair())


def x_sum(wire, here, part, far, near, out):
    at = token_pieces
    return ring_sum(
        wire,
        here.x,
        here.at(dx=1),
        here.at(dx=-1),
        lambda i, h: [part.at[i, n] for n in at(h)],
        lambda h: [far.at[n] for n in at(h)],
        lambda s, h: [near.at[s, n] for n in at(h)],
        lambda h: [out.at[n] for n in at(h)],
    )


def x_sum_scratch():
    return [pltpu.VMEM((128, D), BF), pltpu.VMEM((2, 128, D), BF)]


HIGHS = (64, 32)


def order_columns(width, cut, order):
    return (0, cut) if order == 0 else (cut, width - cut)


def first_scratch(width, cut):
    shapes = []
    for order in range(2):
        size = order_columns(width, cut, order)[1]
        for high in HIGHS:
            shapes += [
                pltpu.VMEM((2, 2, high, size), BF),
                pltpu.VMEM((2, 2, 2, high, size), BF),
            ]
    return shapes


def half_sums(width, cut):
    return [
        (2, 2, high, order_columns(width, cut, order)[1]) for order in range(2) for high in HIGHS
    ]


def second_scratch(width, cut):
    shapes = []
    for order in range(2):
        size = order_columns(width, cut, order)[1]
        for high in HIGHS:
            shapes += [
                pltpu.VMEM((2, high // 2, size), BF),
                pltpu.VMEM((2, 2, high // 2, size), BF),
            ]
    return shapes + [pltpu.VMEM((96, width), BF)]


def rings(here):
    y_ring = (here.y, here.at(dy=1), here.at(dy=-1))
    z_ring = (here.z, here.at(dz=1), here.at(dz=-1))
    return y_ring, z_ring


def first_sums(wire, here, grads, scratch, sums, width, cut):
    def flow(order):
        at = pl.ds(*order_columns(width, cut, order))
        buffers, out = scratch[4 * order : 4 * order + 4], sums[2 * order : 2 * order + 2]

        def of_z(ref, i, h):
            return ref.at[pl.ds(2 * h, 2), lax.rem(i, 2), lax.div(i, 2), :, at]

        def of_y(ref, i, h):
            return ref.at[i, h, :, :, at]

        pick = of_z if order == 0 else of_y
        return ring_sum(
            wire,
            *rings(here)[1 - order],
            lambda i, h: [pick(g, i, h) for g in grads],
            lambda h: [b.at[h] for b in buffers[0::2]],
            lambda s, h: [b.at[s, h] for b in buffers[1::2]],
            lambda h: [b.at[h] for b in out],
        )

    return flow(0), flow(1)


def second_sums(wire, here, sums, scratch, width, cut):
    fin = scratch[-1]

    def flow(order):
        at = pl.ds(*order_columns(width, cut, order))
        buffers, terms = scratch[4 * order : 4 * order + 4], sums[2 * order : 2 * order + 2]

        def part(i, h):
            high, low = lax.div(i, 2), lax.rem(i, 2)
            lead = (high, low) if order == 0 else (low, high)
            return [
                b.at[lead[0], lead[1], pl.ds(tall // 2 * h, tall // 2)]
                for b, tall in zip(terms, HIGHS)
            ]

        return ring_sum(
            wire,
            *rings(here)[order],
            part,
            lambda h: [b.at[h] for b in buffers[0::2]],
            lambda s, h: [b.at[s, h] for b in buffers[1::2]],
            lambda h: [
                fin.at[pl.ds(start + tall // 2 * h, tall // 2), at]
                for start, tall in zip((0, 64), HIGHS)
            ],
        )

    return flow(0), flow(1)


def grad_share(wire, here, fin, out, width):
    columns = pl.ds(pl.multiple_of(here.core * width, 128), width)
    mine = out.at[here.zh, :, columns]
    other = out.at[1 - here.zh, :, columns]
    wire.stay(fin, mine)
    wire.copy(fin, mine, here.pair())
    n = wire.copy(fin, mine, here.at(dz=2))
    yield
    wire.arrive(n)
    wire.copy(other, other, here.pair())


def swap_rows(wire, here, src, dst):
    return [
        wire.copy(src.at[lax.rem(here.row + s, 8)], dst.at[here.row], here.in_row(s))
        for s in range(1, 8)
    ]


def low_lanes(rows):
    return lax.broadcasted_iota(jnp.int32, (rows, 128), 1) < 64


def widened(ref):
    main = [ref[r, 0:128, :] for r in range(8)]
    rest = []
    for j in range(4):
        even, odd = ref[2 * j, 128:192, :].astype(F32), ref[2 * j + 1, 128:192, :].astype(F32)
        top = jnp.where(low_lanes(64), even, odd)
        bottom = pltpu.roll(jnp.where(low_lanes(64), odd, even), 64, 1)
        rest.append(jnp.concatenate([top, bottom], axis=0).astype(BF))
    return jnp.concatenate(main + rest, axis=1)


def widened_rows(ref, start, size):
    main = [ref[r, start : start + size, :] for r in range(8)]
    after = slice(start + size, start + 2 * size)
    rest = [ref[2 * j, after, :] + ref[2 * j + 1, after, :] for j in range(4)]
    return jnp.concatenate(main + rest, axis=1)


def narrowed(out, value):
    for r in range(8):
        out[r, 0:128, :] = value[:, 128 * r : 128 * r + 128].astype(BF)
        j = 1024 + 128 * (r // 2)
        top, bottom = value[0:64, j : j + 128], value[64:128, j : j + 128]
        if r % 2 == 0:
            rest = jnp.where(low_lanes(64), top, pltpu.roll(bottom, 64, 1))
        else:
            rest = jnp.where(low_lanes(64), pltpu.roll(top, 64, 1), bottom)
        out[r, 128:192, :] = rest.astype(BF)


def narrowed_rows(out, value):
    for r in range(8):
        out[r, :, 0:128] = value[:, 128 * r : 128 * r + 128]
        j = 1024 + 128 * (r // 2)
        out[r, :, 128:256] = value[:, j : j + 128]


def ring_partners(here):
    return [here.at(dx=1), here.at(dx=-1)]


def plane_partners(here):
    return [here.at(dy=1), here.at(dy=-1), here.at(dz=1), here.at(dz=-1)]


def dot(a, b, left=1, right=0):
    return lax.dot_general(a, b, (((left,), (right,)), ((), ())), preferred_element_type=F32)


def turned(values, cosine, sine):
    lane = lax.broadcasted_iota(jnp.int32, values.shape, 1)
    front = lax.rem(lane, HS) < HS // 2
    ahead, back = pltpu.roll(values, 256 - HS // 2, 1), pltpu.roll(values, HS // 2, 1)
    return values * cosine + jnp.where(front, -ahead, back) * sine


def packed_pair(a, b):
    return jnp.concatenate([a[:, :128], a[:, 128:] + b[:, :128], b[:, 128:]], axis=1)


def windows(y):
    return ((0, 4), (0, 8), (1 + y, 8), (5 + y, 8))


def allowed_keys(table, c, start, count):
    key = start * 128 + lax.broadcasted_iota(jnp.int32, (count * 128, 256), 0)
    return (key >= table[2 * c : 2 * c + 1]) & (key <= table[2 * c + 1 : 2 * c + 2])


def both_heads(ref, at):
    return jnp.concatenate([ref[at, 0:256], ref[at, 256:512]], axis=0)


def attend(here, q, kv, table, heads, log_total):
    lane = lax.broadcasted_iota(jnp.int32, (256, 256), 1)
    for c, (start, count) in enumerate(windows(here.y)):
        at = pl.ds(128 * c, 128)
        allowed = allowed_keys(table, c, start, count)
        q_both = both_heads(q, at)
        k = kv[pl.ds(start, count), :, 0:256].reshape(count * 128, 256)
        v = kv[pl.ds(start, count), :, 128:384].reshape(count * 128, 256)
        made = []
        for g in range(2):
            n = 2 * c + g
            q_one = jnp.where((lane >= HS) == (g == 1), q_both, jnp.zeros_like(q_both))
            scores = dot(k, q_one, 1, 1) * score_scale
            scores = jnp.where(allowed, scores, -1e30)
            top = jnp.max(scores, axis=0, keepdims=True)
            weights = jnp.exp(scores - top)
            total = jnp.sum(weights, axis=0, keepdims=True)
            shares = (weights * (1.0 / total)).astype(BF)
            made.append(dot(shares, v, 0, 0))
            log_total[n : n + 1] = top + jnp.log(total)
        out = jnp.where(lane < 64 + HS, made[0], made[1])
        out = jnp.where(lane < 64, 0.0, out).astype(BF)
        heads[at, 0:256] = out[:128]
        heads[at, 256:512] = out[128:]
        yield


def attend_back(here, q, kv, table, log_total, dout, dq, total):
    lane = lax.broadcasted_iota(jnp.int32, (256, 256), 1)
    total[...] = jnp.zeros_like(total)
    for c, (start, count) in reversed(list(enumerate(windows(here.y)))):
        at = pl.ds(128 * c, 128)
        blocks = pl.ds(start, count)
        allowed = allowed_keys(table, c, start, count)
        q_both, d_both = both_heads(q, at), both_heads(dout, at)
        k = kv[blocks, :, 0:256].reshape(count * 128, 256)
        v = kv[blocks, :, 128:384].reshape(count * 128, 256)
        made = []
        for g in range(2):
            n = 2 * c + g
            q_one = jnp.where((lane >= HS) == (g == 1), q_both, jnp.zeros_like(q_both))
            d_one = jnp.where((lane >= 64 + HS) == (g == 1), d_both, jnp.zeros_like(d_both))
            scores = dot(k, q_one, 1, 1) * score_scale
            shares = jnp.where(allowed, jnp.exp(scores - log_total[n : n + 1]), 0.0)
            dshares = dot(v, d_one, 1, 1)
            inner = jnp.sum(shares * dshares, axis=0, keepdims=True)
            dscores = (shares * (dshares - inner)).astype(BF)
            made.append(dot(dscores, k, 0, 0))
            dk = dot(dscores, q_one) * score_scale
            dv = dot(shares.astype(BF), d_one)
            total[blocks, :, 0:256] += dk.reshape(count, 128, 256)
            total[blocks, :, 128:384] += dv.reshape(count, 128, 256)
        out = jnp.where(lane < HS, made[0], made[1]) * score_scale
        dq[at, 0:256] = out[:128]
        dq[at, 256:512] = out[128:]
        yield


def tokens_of(ref, pair=0):
    return ref[4 * pair : 4 * pair + 4].reshape(512, D)


def columns(n, size=256):
    return pl.ds(pl.multiple_of(n * size, size), size)


def back_to_width(units, weights, out, token_at=slice(None)):
    @pl.loop(0, D // 256)
    def _(n):
        made = dot(units(), weights[columns(n), :], 1, 1)
        out[:, token_at, columns(n)] = made.astype(BF).reshape(4, made.shape[0] // 4, 256)


def weight_grads(tokens, own, pair, main, rest, at):
    def made(n):
        total = dot(tokens[0:4, :, columns(n)].reshape(512, 256), own(), 0, 0)
        return total + dot(tokens[4:8, :, columns(n)].reshape(512, 256), pair(), 0, 0)

    @pl.loop(0, 4)
    def _(n):
        value = made(n)
        main[n, :, :, :, at] = value.astype(BF).reshape(2, 2, 64, value.shape[1])

    @pl.loop(0, 2)
    def _(n):
        value = made(n + 4)
        rest[pl.ds(2 * n, 2), :, :, :, at] = value.astype(BF).reshape(2, 2, 2, 32, value.shape[1])


def norm_back(value, grad, gain):
    scale = lax.rsqrt(jnp.mean(value * value, axis=1, keepdims=True) + norm_epsilon)
    unit = value * scale
    scaled = grad * gain
    inner = jnp.mean(scaled * unit, axis=1, keepdims=True)
    return scale * (scaled - unit * inner), jnp.sum(grad * unit, axis=0, keepdims=True)


def normed(value, gain):
    scale = lax.rsqrt(jnp.mean(value * value, axis=1, keepdims=True) + norm_epsilon)
    return (value * scale * gain).astype(BF)


def key_block(c, y):
    return 4 * c + y


def pack_rows(here, out, values):
    for y in range(4):
        for zl in range(2):
            block = values[zl, :, 128 * y : 128 * y + 128]
            rest = block[128:]
            swapped = pltpu.roll(rest, 64, 1)
            first = jnp.where(here.zl == 0, rest, swapped)
            second = jnp.where(here.zl == 0, swapped, rest)
            out[2 * y + zl, 0:128, :] = block[:128].T.astype(BF)
            both = jnp.concatenate([first, second], axis=0).T
            out[2 * y + zl, 128:192, :] = both[0:64].astype(BF)


def own_half(here, rest):
    return jnp.where(here.zl == 0, rest, pltpu.roll(rest, 64, 1))


def enter_kernel(
    stream, cotangent, qkv_weight, out_weight, gate_up, down, gains, positions, frequency, qkv_at, out_at,
    h1_out, wq_out, wo_out, c_out, kv_out, down_out, w_both,
    q_out, heads_out, cosine_out, sine_out, xtok_out, ctok_out,
    rise, h2_own, log_total, gtok, table,
    q, heads, cosine, sine, xtok, ctok,
    xf, cf, qf, of, gf, df, qs, os, xin, cin, wq_own, wo_own, win,
    xbuf, cbuf, h1_all, c_all, wq, wo, part, far, near, kv_own, kv_all, qkv, gpad, send, recv, local,
):
    here = Place()
    wire = Wire(send, recv, local)
    x_load = wire.stay(stream, xf)
    greet(
        [here.in_row(s) for s in range(1, 8)]
        + ring_partners(here)
        + [here.at(dz=1), here.at(dz=-1), here.pair()]
    )
    gpad[...] = jnp.zeros_like(gpad)
    gpad[0:2, 0:192] = gains[...]
    g = gpad[...]
    high = g.astype(BF).astype(F32)
    rows4 = jnp.concatenate([high[0:2], (g - high)[0:2]], axis=0)
    rest = rows4[:, 128:]
    rest = jnp.where(here.zl == 0, rest, pltpu.roll(rest, 64, 1))
    rows16 = jnp.concatenate([rows4[:, :128], rest, jnp.zeros((8, 128), F32)], axis=0).astype(BF)
    wire.there(x_load)
    q_load = wire.stay(qkv_weight, qf), wire.stay(qkv_at, qs)
    for r in range(8):
        xin[r, 192:208, :] = rows16
    pack_rows(here, xin, xf)
    xs = swap_rows(wire, here, xin, xbuf)
    xbuf[here.row] = xin[here.row]
    o_load = wire.stay(out_weight, of), wire.stay(out_at, os)
    c_load = wire.stay(cotangent, cf)
    f_load = [wire.stay(gate_up.at[:, j], gf.at[j]) for j in range(2)] + [wire.stay(down, df)]

    wire.there(*q_load)
    wq_own[...] = dot(qf[...].astype(BF), qs[...], 1, 1).astype(BF)
    q_weights = weight_gather(wire, here, wq_own, wq)
    next(q_weights)
    wire.there(*o_load)
    wo_own[...] = dot(of[...].astype(BF), os[...], 1, 1).astype(BF)
    o_weights = weight_gather(wire, here, wo_own, wo)
    lane = lax.broadcasted_iota(jnp.int32, (128, 256), 1)
    for c in range(4):
        first = 512 * c + 128 * here.y
        place = positions[:, pl.ds(pl.multiple_of(first, 128), 128)]
        place = jnp.where(here.zl == 0, place[0:1], place[1:2])
        token = first + lax.broadcasted_iota(jnp.int32, (1, 128), 1)
        table[2 * c : 2 * c + 1, :] = jnp.concatenate([token - place] * 2, axis=1)
        table[2 * c + 1 : 2 * c + 2, :] = jnp.concatenate([token] * 2, axis=1)
        column = jnp.broadcast_to(place.astype(F32), (128, 128)).T[:, 0:1]
        angles = column * frequency[0:1]
        at = pl.ds(128 * c, 128)
        cosine[at, :] = jnp.where(lane < 2 * HS, jnp.cos(angles), 0.0)
        sine[at, :] = jnp.where(lane < 2 * HS, jnp.sin(angles), 0.0)
    wire.stay(cosine, cosine_out)
    wire.stay(sine, sine_out)
    wire.there(c_load)
    pack_rows(here, cin, cf)
    cbuf[here.row] = cin[here.row]

    next(q_weights)
    wire.arrive(*xs)
    x = widened(xbuf)
    xtok[...] = x
    wire.stay(xtok, xtok_out)
    g = widened_rows(xbuf, 192, 4).astype(F32)
    g = g[0:2] + g[2:4]
    gtok[...] = g
    h1_all[here.x] = normed(x.astype(F32), g[0:1])
    h1_flow = share(wire, here, h1_all)
    next(h1_flow)
    next(q_weights)
    wire.there(*f_load)
    for k in range(2):
        for j in range(2):
            at = 1024 * k + 512 * j
            win[:, at : at + 512] = gf[j, :, 512 * k : 512 * k + 512].astype(BF)
    win[:, 2048:3072] = df[...].astype(BF)
    wire.stay(win.at[:, pl.ds(2048, 1024)], down_out)
    next(q_weights)
    next(o_weights)
    cs = swap_rows(wire, here, cin, cbuf)
    next(h1_flow)
    for _ in range(4):
        next(q_weights)
    next(h1_flow)
    next(o_weights)
    side_by_side(h1_flow, q_weights)
    wire.stay(wq, wq_out)
    wire.stay(h1_all, h1_out)
    wire.arrive(*cs)
    c_value = widened(cbuf)
    ctok[...] = c_value
    wire.stay(ctok, ctok_out)
    c_all[here.x] = c_value
    c_flow = share(wire, here, c_all)
    next(c_flow)
    next(o_weights)

    @pl.loop(0, 3)
    def _(n):
        qkv[:, columns(n)] = dot(tokens_of(h1_all), wq[:, columns(n)])

    for c in range(4):
        at = pl.ds(128 * c, 128)
        turn = cosine[at], sine[at]
        key = turned(qkv[at, 384:640], *turn)
        value = jnp.where(lane < 64, 0.0, qkv[at, 512:768])
        kv = packed_pair(key, value).astype(BF)
        kv_own[c] = kv
        kv_all[key_block(c, here.y)] = kv

    keys = ring_gather(
        wire,
        here.y,
        here.at(dy=1),
        here.at(dy=-1),
        lambda h: [kv_own.at[2 * h + n] for n in range(2)],
        lambda i, h: [kv_all.at[key_block(2 * h + n, i)] for n in range(2)],
    )
    next(keys)
    for c in range(4):
        at = pl.ds(128 * c, 128)
        turn = cosine[at], sine[at]
        q[at, 0:256] = turned(qkv[at, 0:256], *turn).astype(BF)
        second = pltpu.roll(qkv[at, 128:384], 192, 1)
        q[at, 256:512] = turned(second, *turn).astype(BF)
    next(o_weights)
    next(c_flow)
    next(keys)
    for _ in range(4):
        next(o_weights)
    weights = weight_gather(wire, here, win.at[:, pl.ds(0, 2048)], w_both, True)
    next(weights)
    next(c_flow)
    side_by_side(keys, c_flow)
    next(weights)
    for _ in attend(here, q, kv_all, table, heads, log_total):
        pass
    side_by_side(o_weights)
    for held, out in ((c_all, c_out), (wo, wo_out), (kv_all, kv_out), (q, q_out)):
        wire.stay(held, out)
    wire.stay(heads, heads_out)
    back_to_width(lambda: heads[...], wo, part)
    chain = x_sum(wire, here, part, far, near, rise)
    next(chain)
    next(weights)
    next(weights)
    next(chain)
    next(weights)
    side_by_side(chain, weights)
    h2_own[...] = normed(rise[...] + xtok[...].astype(F32), gtok[1:2])
    wire.finish()


def shape(dtype, *sizes):
    return jax.ShapeDtypeStruct(sizes, dtype)


def signals(*counts):
    return [pltpu.SemaphoreType.DMA((n,)) for n in counts]


def settings(number):
    return pltpu.CompilerParams(
        collective_id=number, has_side_effects=True, vmem_limit_bytes=60 << 20
    )


def enter(*operands):
    return pl.pallas_call(
        enter_kernel,
        out_shape=[
            shape(BF, 4, 128, D),
            shape(BF, D, 768),
            shape(BF, D, 512),
            shape(BF, 4, 128, D),
            shape(BF, 16, 128, 384),
            shape(BF, 192, 1024),
            shape(BF, D, 2048),
            shape(BF, 512, 512),
            shape(BF, 512, 512),
            shape(F32, 512, 256),
            shape(F32, 512, 256),
            shape(BF, 128, D),
            shape(BF, 128, D),
            shape(F32, 128, D),
            shape(BF, 128, D),
            shape(F32, 8, 256),
            shape(F32, 2, D),
            shape(jnp.int32, 8, 256),
        ],
        in_specs=[ANY] * 6 + [VM] * 3 + [ANY] * 2,
        out_specs=[ANY] * 13 + [VM] * 5,
        scratch_shapes=[
            pltpu.VMEM((512, 512), BF),
            pltpu.VMEM((512, 512), BF),
            pltpu.VMEM((512, 256), F32),
            pltpu.VMEM((512, 256), F32),
            pltpu.VMEM((128, D), BF),
            pltpu.VMEM((128, D), BF),
            pltpu.VMEM((2, 192, 512), F32),
            pltpu.VMEM((2, 192, 512), F32),
            pltpu.VMEM((192, 768), F32),
            pltpu.VMEM((192, 384), F32),
            pltpu.VMEM((2, 192, 1024), F32),
            pltpu.VMEM((192, 1024), F32),
            pltpu.VMEM((768, 768), BF),
            pltpu.VMEM((512, 384), BF),
            pltpu.VMEM((8, 208, 128), BF),
            pltpu.VMEM((8, 192, 128), BF),
            pltpu.VMEM((192, 768), BF),
            pltpu.VMEM((192, 512), BF),
            pltpu.VMEM((192, 3072), BF),
            pltpu.VMEM((8, 208, 128), BF),
            pltpu.VMEM((8, 192, 128), BF),
            pltpu.VMEM((4, 128, D), BF),
            pltpu.VMEM((4, 128, D), BF),
            pltpu.VMEM((D, 768), BF),
            pltpu.VMEM((D, 512), BF),
            pltpu.VMEM((4, 128, D), BF),
        ]
        + x_sum_scratch()
        + [
            pltpu.VMEM((4, 128, 384), BF),
            pltpu.VMEM((16, 128, 384), BF),
            pltpu.VMEM((512, 768), F32),
            pltpu.VMEM((8, 256), F32),
        ]
        + signals(256, 256, 32),
        compiler_params=settings(1),
        name="enter",
    )(*operands)


BOTH = (1024, 512)
DOWN = (512, 256)


def feed_kernel(*refs):
    h2_own, gtok, rise_in, xtok_in, ctok_in, down_own, both_w, c_in = refs[:8]
    after_out, gain, f_out, d_out = refs[8:12]
    both_sums, down_sums = refs[12:16], refs[16:20]
    after, f_part, far, near, middle, summed, h2_all, c_all = refs[20:28]
    w_down, w_both, both, act, both_in, act_in, hidden, part2, d_all = refs[28:37]
    main, rest, down_main, down_rest = refs[37:41]
    rise, xtok, ctok = refs[41:44]
    both_first, down_first, (send, recv, local) = refs[44:52], refs[52:60], refs[60:]
    here = Place()
    wire = Wire(send, recv, local)
    greet(ring_partners(here) + plane_partners(here) + [here.pair()])
    h2_all[here.x] = h2_own[...]
    chain = share(wire, here, h2_all)
    next(chain)
    down = weight_gather(wire, here, down_own, w_down)
    next(down)
    loads = [wire.stay(a, b) for a, b in ((rise_in, rise), (xtok_in, xtok), (ctok_in, ctok))]
    loads += [wire.stay(c_in, c_all.at[pl.ds(0, 4)]), wire.stay(both_w, w_both)]
    next(chain)
    next(down)
    next(down)
    wire.there(loads[3])
    c_paired = to_pair(wire, here, c_all)
    next(down)
    next(chain)
    for _ in range(4):
        next(down)
    side_by_side(chain)
    wire.there(*loads[:3], loads[4])
    middle[...] = rise[...] + xtok[...].astype(F32)
    paired = [to_pair(wire, here, h2_all)]

    @pl.loop(0, 8)
    def _(n):
        hidden[:, columns(n)] = dot(tokens_of(h2_all), w_both[:, columns(n)])

    side_by_side(down)

    def unit_tiles(half):
        @pl.loop(0, 2)
        def _(n):
            at, down_at = columns(half * 4 + n), columns(half * 2 + n)
            up_at = columns(half * 4 + n + 2)
            gate, up = hidden[:, at], hidden[:, up_at]
            grad = dot(tokens_of(c_all), w_down[:, down_at])
            sigmoid = 1.0 / (1.0 + jnp.exp(-gate))
            silu = gate * sigmoid
            both[:, at] = (grad * up * sigmoid * (1.0 + gate * (1.0 - sigmoid))).astype(BF)
            both[:, up_at] = (grad * silu).astype(BF)
            act[:, down_at] = (silu * up).astype(BF)

    other = 1 - here.core
    unit_tiles(other)
    paired.append(wire.copy(both.at[:, columns(other, 1024)], both_in, here.pair()))
    act_swap = wire.copy(act.at[:, columns(other, 512)], act_in, here.pair())
    unit_tiles(here.core)
    back_to_width(lambda: both[...], w_both, part2)

    def backward():
        yield from x_sum(wire, here, part2, far, near, summed)
        left, gain_terms = norm_back(middle[...], summed[...], gtok[1:2])
        gain[...] = jnp.broadcast_to(gain_terms, gain.shape)
        after[...] = left
        d_all[here.x] = (left + ctok[...].astype(F32)).astype(BF)
        wire.stay(after, after_out)
        yield from share(wire, here, d_all)

    chain = backward()
    next(chain)
    wire.arrive(c_paired, act_swap)
    weight_grads(
        c_all, lambda: act[:, columns(here.core, 512)], lambda: act_in[...], down_main, down_rest, slice(None)
    )
    flows = first_sums(wire, here, (down_main, down_rest), down_first, down_sums, *DOWN)
    for flow in flows:
        next(flow)
    wire.arrive(*paired)
    weight_grads(
        h2_all, lambda: both[:, columns(here.core, 1024)], lambda: both_in[...], main, rest, slice(None)
    )
    both_flows = first_sums(wire, here, (main, rest), both_first, both_sums, *BOTH)
    for flow in both_flows:
        next(flow)
    next(chain)
    back_to_width(lambda: act[...], w_down, f_part)
    wire.stay(f_part, f_out)
    for flow in flows:
        next(flow)
    next(chain)
    for flow in both_flows:
        next(flow)
    next(chain)
    next(chain)
    side_by_side(chain)
    wire.stay(d_all, d_out)
    side_by_side(*flows, *both_flows)
    wire.finish()


def grad_shapes(width):
    return [(4, 2, 2, high, width) for high in HIGHS]


def grad_arrays(width):
    return [pltpu.VMEM(sizes, BF) for sizes in grad_shapes(width)]


def feed(*operands):
    return pl.pallas_call(
        feed_kernel,
        out_shape=[
            shape(F32, 128, D),
            shape(F32, 8, D),
            shape(BF, 4, 128, D),
            shape(BF, 4, 128, D),
        ]
        + [shape(BF, *sizes) for sizes in half_sums(*BOTH) + half_sums(*DOWN)],
        in_specs=[VM] * 2 + [ANY] * 6,
        out_specs=[ANY, VM] + [ANY] * 2 + [VM] * 8,
        scratch_shapes=[
            pltpu.VMEM((128, D), F32),
            pltpu.VMEM((4, 128, D), BF),
        ]
        + x_sum_scratch()
        + [
            pltpu.VMEM((128, D), F32),
            pltpu.VMEM((128, D), F32),
            pltpu.VMEM((8, 128, D), BF),
            pltpu.VMEM((8, 128, D), BF),
            pltpu.VMEM((D, 1024), BF),
            pltpu.VMEM((D, 2048), BF),
            pltpu.VMEM((512, 2048), BF),
            pltpu.VMEM((512, 1024), BF),
            pltpu.VMEM((512, 1024), BF),
            pltpu.VMEM((512, 512), BF),
            pltpu.VMEM((512, 2048), F32),
            pltpu.VMEM((4, 128, D), BF),
            pltpu.VMEM((4, 128, D), BF),
        ]
        + grad_arrays(BOTH[0])
        + grad_arrays(DOWN[0])
        + [pltpu.VMEM((128, D), F32), pltpu.VMEM((128, D), BF), pltpu.VMEM((128, D), BF)]
        + first_scratch(*BOTH)
        + first_scratch(*DOWN)
        + signals(200, 200, 16),
        compiler_params=settings(2),
        name="feed",
    )(*operands)


ATTN = (640, 256)


def leave_held():
    sizes = [(4, 128, D)]
    sizes += half_sums(*BOTH) + half_sums(*DOWN)
    sizes += [(4, 128, D), (D, 512), (512, 512), (16, 128, 384), (512, 512), (4, 128, D)]
    sizes += [(D, 768), (128, D)]
    return [(size, BF) for size in sizes] + [
        ((128, D), F32), ((128, D), F32), ((512, 256), F32), ((512, 256), F32)
    ]


def leave_kernel(*refs):
    gtok, gain, log_total, table = refs[:4]
    count = len(leave_held())
    held_in, refs = refs[4 : 4 + count], refs[4 + count :]
    o_all, s_all, gout, both_out, down_out, gains_out = refs[:6]
    held, refs = refs[6 : 6 + count], refs[6 + count :]
    f_part, both_sums, down_sums = held[0], held[1:5], held[5:9]
    d_all, wo, q, kv_all, heads, h1_all, wq, xtok, rise, after, cosine, sine = held[9:]
    dout, dq, total, dkv, kfar, knear, dkv_own, dqkv = refs[:8]
    heads_in, dqkv_in, part, far, near, far2, near2, summed, osend, ssend = refs[8:18]
    gsend, grow, gcol, gdp, main, rest = refs[18:24]
    scratch, (send, recv, local) = refs[24:-3], refs[-3:]
    a_first, a_sums, a_second = scratch[:8], scratch[8:12], scratch[12:21]
    both_second, down_second = scratch[21:30], scratch[30:39]
    here = Place()
    wire = Wire(send, recv, local)
    def load(first, last):
        made = []
        for src, dst in zip(held_in[first:last], held[first:last]):
            dst = dst.at[pl.ds(0, 4)] if dst.shape != src.shape else dst
            made.append(wire.stay(src, dst))
        return made

    attention_loads = load(9, 14)
    greet(
        [here.in_row(s) for s in range(1, 8)]
        + ring_partners(here)
        + [here.at(dz=1), here.at(dz=-1), here.at(dx=2)]
        + [here.in_dp(s) for s in range(1, 4)]
    )
    wire.there(*attention_loads[:2])
    sums_loads = load(0, 9)

    @pl.loop(0, 2)
    def _(n):
        dout[:, columns(n)] = dot(tokens_of(d_all), wo[:, columns(n)]).astype(BF)

    wire.there(*attention_loads[2:])
    heads_swap = wire.copy(heads.at[:, columns(1 - here.core)], heads_in, here.pair())
    wire.there(*sums_loads)
    branch_sum = x_sum(wire, here, f_part, far, near, summed)
    next(branch_sum)
    sums = second_sums(wire, here, both_sums, both_second, *BOTH)
    sums += second_sums(wire, here, down_sums, down_second, *DOWN)
    for flow in sums:
        next(flow)
    d_paired = to_pair(wire, here, d_all)
    late_loads = load(14, count)

    def key_sums(half):
        block = lambda h: 2 * half + h
        return ring_sum(
            wire,
            here.y,
            here.at(dy=1),
            here.at(dy=-1),
            lambda i, h: [dkv.at[key_block(block(h), i)]],
            lambda h: [kfar.at[half, h]],
            lambda s, h: [knear.at[half, s, h]],
            lambda h: [dkv_own.at[pl.ds(128 * block(h), 128)]],
        )

    attention = attend_back(here, q, kv_all, table, log_total, dout, dq, total)
    next(attention)
    for flow in sums:
        next(flow)
    next(attention)
    dkv[8:16] = total[8:16].astype(BF)
    late_keys = key_sums(1)
    next(late_keys)
    next(attention)
    next(branch_sum)
    next(attention)
    next(late_keys)
    dkv[0:8] = total[0:8].astype(BF)
    keys = key_sums(0)
    next(keys)
    wire.there(*late_loads)
    side_by_side(*sums)
    both_share = grad_share(wire, here, both_second[-1], both_out, BOTH[0])
    down_share = grad_share(wire, here, down_second[-1], down_out, DOWN[0])
    next(both_share)
    next(down_share)
    h1_paired = to_pair(wire, here, h1_all)
    side_by_side(branch_sum)
    narrowed(osend, summed[...] + rise[...])
    for c in range(4):
        at = pl.ds(128 * c, 128)
        turn = cosine[at], -sine[at]
        second = turned(dq[at, 256:512], *turn)
        both = packed_pair(turned(dq[at, 0:256], *turn), pltpu.roll(second, 64, 1))
        dqkv[at, 0:384] = both.astype(BF)
    next(keys)
    wire.arrive(heads_swap, d_paired)
    weight_grads(
        d_all, lambda: heads[:, columns(here.core)], lambda: heads_in[...], main, rest, slice(384, 640)
    )
    lane = lax.broadcasted_iota(jnp.int32, (128, 256), 1)
    side_by_side(late_keys, keys)
    for c in range(4):
        at = pl.ds(128 * c, 128)
        key = turned(dkv_own[at, 0:256], cosine[at], -sine[at])
        value = jnp.where(lane < 64, 0.0, dkv_own[at, 128:384])
        dqkv[at, 384:768] = packed_pair(key, value).astype(BF)
    dqkv_swap = wire.copy(dqkv.at[:, columns(1 - here.core, 384)], dqkv_in, here.pair())
    back_to_width(lambda: dqkv[...], wq, part)

    def chain():
        yield from x_sum(wire, here, part, far2, near2, summed)
        left, gain_terms = norm_back(xtok[...].astype(F32), summed[...], gtok[0:1])
        gains = jnp.concatenate([gain_terms, gain[0:1], jnp.zeros((6, D), F32)], axis=0)
        narrowed_rows(gsend, gains)
        g = swap_rows(wire, here, gsend, grow)
        narrowed(ssend, left + after[...])
        wire.stay(ssend.at[here.row], s_all.at[here.row])
        swap_rows(wire, here, ssend, s_all)
        yield
        wire.arrive(*g)
        grow[here.row] = gsend[here.row]
        total = grow[0]
        for n in range(1, 8):
            total = total + grow[n]
        gcol[here.x] = total
        g = [wire.copy(gcol.at[here.x], gcol.at[here.x], here.at(dx=s)) for s in range(1, 4)]
        yield
        wire.arrive(*g)
        gdp[here.dp] = ((gcol[0] + gcol[1]) + gcol[2]) + gcol[3]
        g = [wire.copy(gdp.at[here.dp], gdp.at[here.dp], here.in_dp(s)) for s in range(1, 4)]
        yield
        wire.arrive(*g)
        gains_out[...] = ((gdp[0] + gdp[1]) + gdp[2]) + gdp[3]

    steps = chain()
    next(steps)
    side_by_side(both_share, down_share)
    wire.stay(osend.at[here.row], o_all.at[here.row])
    swap_rows(wire, here, osend, o_all)
    wire.arrive(dqkv_swap, h1_paired)
    weight_grads(
        h1_all, lambda: dqkv[:, columns(here.core, 384)], lambda: dqkv_in[...], main, rest, slice(0, 384)
    )
    first = first_sums(wire, here, (main, rest), a_first, a_sums, *ATTN)

    def sums():
        yield
        side_by_side(*first)
        second = second_sums(wire, here, a_sums, a_second, *ATTN)
        for flow in second:
            next(flow)
        yield
        for flow in second:
            next(flow)
        yield
        side_by_side(*second)
        yield from grad_share(wire, here, a_second[-1], gout, ATTN[0])

    for flow in first:
        next(flow)
    next(steps)
    for flow in first:
        next(flow)
    side_by_side(steps, sums())
    wire.finish()


def leave(*operands):
    held = [pltpu.VMEM(size, kind) for size, kind in leave_held()]
    for n in (9, 14):
        held[n] = pltpu.VMEM((8, 128, D), BF)
    return pl.pallas_call(
        leave_kernel,
        out_shape=[
            shape(BF, 8, 192, 128),
            shape(BF, 8, 192, 128),
            shape(BF, 2, 96, 2 * ATTN[0]),
            shape(BF, 2, 96, 2 * BOTH[0]),
            shape(BF, 2, 96, 2 * DOWN[0]),
            shape(F32, 8, 256),
        ],
        in_specs=[VM] * 4 + [ANY] * len(held),
        out_specs=[ANY] * 5 + [VM],
        scratch_shapes=held
        + [
            pltpu.VMEM((512, 512), BF),
            pltpu.VMEM((512, 512), F32),
            pltpu.VMEM((16, 128, 384), F32),
            pltpu.VMEM((16, 128, 384), BF),
            pltpu.VMEM((2, 2, 128, 384), BF),
            pltpu.VMEM((2, 2, 2, 128, 384), BF),
            pltpu.VMEM((512, 384), F32),
            pltpu.VMEM((512, 768), BF),
            pltpu.VMEM((512, 256), BF),
            pltpu.VMEM((512, 384), BF),
            pltpu.VMEM((4, 128, D), BF),
        ]
        + x_sum_scratch()
        + x_sum_scratch()
        + [
            pltpu.VMEM((128, D), F32),
            pltpu.VMEM((8, 192, 128), BF),
            pltpu.VMEM((8, 192, 128), BF),
            pltpu.VMEM((8, 8, 256), F32),
            pltpu.VMEM((8, 8, 256), F32),
            pltpu.VMEM((4, 8, 256), F32),
            pltpu.VMEM((4, 8, 256), F32),
        ]
        + grad_arrays(ATTN[0])
        + first_scratch(*ATTN)
        + [pltpu.VMEM(sizes, BF) for sizes in half_sums(*ATTN)]
        + second_scratch(*ATTN)
        + second_scratch(*BOTH)
        + second_scratch(*DOWN)
        + signals(240, 240, 32),
        compiler_params=settings(3),
        name="leave",
    )(*operands)


def step_rates():
    return (2.0 / D**0.5, 2.0 / max(HQ * HS // 64, 1) ** 0.5, 2.0 / D**0.5, 2.0 / FF**0.5, 0.4)


def adamw(state, at, gradient, step_rate, decay_rate):
    weight, first, second = state
    moment_one = beta_first * first[at] + (1.0 - beta_first) * gradient
    moment_two = beta_second * second[at] + (1.0 - beta_second) * gradient * gradient
    first[at] = moment_one
    second[at] = moment_two
    corrected = (moment_one * (1.0 / (1.0 - beta_first**STEP))) / (
        jnp.sqrt(moment_two * (1.0 / (1.0 - beta_second**STEP))) + adam_epsilon
    )
    old = weight[at]
    weight[at] = old - step_rate * (corrected + decay_rate * old)


def update_kernel(*refs):
    stream, cotangent, o_in, s_in, g_in, both_in, down_in, qkv_at, out_at = refs[:9]
    qkv, out, gate_up, down, gains = (refs[9 + 3 * n : 12 + 3 * n] for n in range(5))
    gains_tile = refs[24]
    o_out, s_out = refs[25:27]
    results = [refs[27 + 3 * n : 30 + 3 * n] for n in range(5)]
    xf, cf, ot, st, gb, fb, db, qs, os = refs[42:51]
    qkv_s, out_s, gate_s, down_s = (refs[51 + 3 * n : 54 + 3 * n] for n in range(4))
    local = refs[63]
    here = Place()
    wire = Wire(None, None, local)
    rate_qkv, rate_out, rate_gate_up, rate_down, rate_gains = step_rates()

    f_load = [wire.stay(both_in, fb)]
    for a, b in zip(gate_up, gate_s):
        f_load += [wire.stay(a.at[:, j], b.at[j]) for j in range(2)]
    d_load = [wire.stay(down_in, db)] + [wire.stay(a, b) for a, b in zip(down, down_s)]
    x_load = [wire.stay(a, b) for a, b in ((stream, xf), (o_in, ot), (cotangent, cf), (s_in, st))]
    a_load = [wire.stay(a, b) for a, b in ((g_in, gb), (qkv_at, qs), (out_at, os))]
    a_load += [wire.stay(a, b) for a, b in zip(qkv + out, qkv_s + out_s)]

    def feed_part(states, grads):
        @pl.loop(0, 4)
        def _(n):
            zh, k = lax.div(n, 2), lax.rem(n, 2)
            for start, size, begin in ((0, 64, 64 * zh), (64, 32, 128 + 32 * zh)):
                at = pl.ds(pl.multiple_of(begin, 32), size), columns(k, 512)
                for a, (state, rate) in enumerate(states):
                    lanes = columns(len(states) * k + a, 512)
                    gradient = grads[zh, start : start + size, lanes].astype(F32)
                    adamw(state, at, gradient, rate, weight_decay)

    wire.there(*f_load)
    feed_part([([b.at[j] for b in gate_s], rate_gate_up) for j in range(2)], fb)
    for a, b in zip(results[2], gate_s):
        for j in range(2):
            wire.stay(b.at[j], a.at[:, j])
    wire.there(*d_load)
    feed_part([(down_s, rate_down)], db)
    for a, b in zip(results[3], down_s):
        wire.stay(b, a)

    wire.there(*x_load)
    for held, tiles, result in ((xf, ot, o_out), (cf, st, s_out)):
        for y in range(4):
            for zl in range(2):
                tile = tiles[2 * y + zl].astype(F32)
                rest = jnp.concatenate([tile[128:192]] * 2, axis=0).T
                rest = jnp.where(low_lanes(64), rest[0:64], rest[64:128])
                at = pl.ds(128 * y, 128)
                held[zl, 0:128, at] = held[zl, 0:128, at] + tile[0:128].T
                held[zl, 128:192, at] = held[zl, 128:192, at] + rest
        wire.stay(held, result)

    wire.there(*a_load)

    def own_block(start, size):
        lanes = [pl.ds(ATTN[0] * k + start, size) for k in range(2)]
        parts = [(0, slice(0, 64)), (1, slice(0, 64)), (0, slice(64, 96)), (1, slice(64, 96))]
        return jnp.concatenate(
            [jnp.concatenate([gb[zh, at, l] for zh, at in parts], axis=0) for l in lanes], axis=1
        )

    gradient = dot(own_block(0, 384), qs[...])
    adamw(qkv_s, (slice(None), slice(None)), gradient, rate_qkv, weight_decay)
    gradient = dot(own_block(384, 256), os[...])
    adamw(out_s, (slice(None), slice(None)), gradient, rate_out, weight_decay)
    for a, b in zip(results[0] + results[1], qkv_s + out_s):
        wire.stay(b, a)

    tile = gains_tile[...]
    rest = own_half(here, tile[:, 128:])
    for old, new in zip(gains, results[4]):
        new[...] = old[...]
    adamw(results[4], (slice(None), slice(0, 128)), tile[0:2, 0:128], rate_gains, 0.0)
    adamw(results[4], (slice(None), slice(128, 192)), rest[0:2, 0:64], rate_gains, 0.0)
    wire.finish()


def update(*operands):
    sizes = [(192, 768)] * 3 + [(192, 384)] * 3 + [(192, 2, 1024)] * 3 + [(192, 1024)] * 3
    held = [(192, 768)] * 3 + [(192, 384)] * 3 + [(2, 192, 1024)] * 3 + [(192, 1024)] * 3
    return pl.pallas_call(
        update_kernel,
        out_shape=[shape(F32, 2, 192, 512)] * 2
        + [shape(F32, *size) for size in sizes]
        + [shape(F32, 2, 192)] * 3,
        in_specs=[ANY] * 21 + [VM] * 4,
        out_specs=[ANY] * 14 + [VM] * 3,
        scratch_shapes=[
            pltpu.VMEM((2, 192, 512), F32),
            pltpu.VMEM((2, 192, 512), F32),
            pltpu.VMEM((8, 192, 128), BF),
            pltpu.VMEM((8, 192, 128), BF),
            pltpu.VMEM((2, 96, 2 * ATTN[0]), BF),
            pltpu.VMEM((2, 96, 2 * BOTH[0]), BF),
            pltpu.VMEM((2, 96, 2 * DOWN[0]), BF),
            pltpu.VMEM((768, 768), BF),
            pltpu.VMEM((512, 384), BF),
        ]
        + [pltpu.VMEM(size, F32) for size in held]
        + signals(64),
        compiler_params=pltpu.CompilerParams(vmem_limit_bytes=60 << 20),
        name="update",
    )(*operands)


def body(
    stream,
    cotangent,
    segments,
    positions,
    qkv_weight,
    qkv_first,
    qkv_second,
    out_weight,
    out_first,
    out_second,
    gate_up_weight,
    gate_up_first,
    gate_up_second,
    down_weight,
    down_first,
    down_second,
    gains,
    gains_first,
    gains_second,
):
    frequency = rope_theta ** (-2.0 * (jnp.arange(256) % (HS // 2)).astype(F32) / HS)
    frequency = jnp.broadcast_to(frequency, (8, 256))
    qkv_at, out_at = qkv_order(), out_order()
    stream_turned, cotangent_turned = stream.transpose(1, 2, 0), cotangent.transpose(1, 2, 0)
    (
        h1_all, wq, wo, c_all, kv_all, down_own, w_both,
        q, heads, cosine, sine, xtok, ctok, rise, h2_own, log_total, gtok, table,
    ) = enter(
        stream_turned, cotangent_turned, qkv_weight, out_weight.T, gate_up_weight, down_weight.T,
        gains, positions, frequency, qkv_at, out_at,
    )
    after, gain_two, f_part, d_all, *sums = feed(
        h2_own, gtok, rise, xtok, ctok, down_own, w_both, c_all
    )
    o_tiles, s_tiles, attn_grads, both_grads, down_grads, gains_tile = leave(
        gtok, gain_two, log_total, table,
        f_part, *sums, d_all, wo, q, kv_all, heads, h1_all, wq, xtok, rise, after, cosine, sine,
    )
    made = update(
        stream_turned, cotangent_turned, o_tiles, s_tiles, attn_grads, both_grads, down_grads, qkv_at, out_at,
        qkv_weight, qkv_first, qkv_second,
        out_weight.T, out_first.T, out_second.T,
        gate_up_weight, gate_up_first, gate_up_second,
        down_weight.T, down_first.T, down_second.T,
        gains, gains_first, gains_second,
        gains_tile,
    )
    output, stream_grad = made[0].transpose(2, 0, 1), made[1].transpose(2, 0, 1)
    states = [made[2 + 3 * n : 5 + 3 * n] for n in range(5)]
    for n in (1, 3):
        states[n] = [a.T for a in states[n]]
    return (output, stream_grad, *(a for w, m, v in states for a in (m, v, w)))


def solution(mesh):
    tokens = P("col", "dp", "row")
    table = P("dp", None)
    wide, tall, pairs, both = P("row", "col"), P("col", "row"), P("row", None, "col"), P(None, "row")
    weights = (wide,) * 3 + (tall,) * 3 + (pairs,) * 3 + (tall,) * 3 + (both,) * 3
    return jax.shard_map(
        body,
        mesh=mesh,
        in_specs=(tokens, tokens, table, table, *weights),
        out_specs=(tokens, tokens, *weights),
        check_vma=False,
    )
```

```python
import functools

import jax
import jax.numpy as jnp
import numpy as np
from jax import lax
from jax.experimental import pallas as pl
from jax.experimental.pallas import tpu as pltpu
from jax.sharding import PartitionSpec as P

D = 1536
FF = 4096
HQ = 16
KVH = 8
HS = 96
STEP = 10
LEN = 2048
WINDOW = 1024

norm_epsilon = 1e-05
rope_theta = 100000.0
beta_first = 0.9
beta_second = 0.95
adam_epsilon = 1e-08
weight_decay = 0.1
score_scale = HS**-0.5

MESH = pl.DeviceIdType.MESH
BF = jnp.bfloat16
F32 = jnp.float32
VM = pl.BlockSpec(memory_space=pltpu.VMEM)
ANY = pl.BlockSpec(memory_space=pl.ANY)


def selection(source, count):
    chosen = np.zeros((count, len(source)), np.float32)
    chosen[source, np.arange(len(source))] = 1.0
    return jnp.asarray(chosen, BF)


def qkv_order():
    b = np.arange(768)
    return selection(b % 384 // HS * 192 + b // 384 * HS + b % HS, 768)


def out_order():
    b = np.arange(384)
    return selection(b % 192 // HS * 256 + 64 + b // 192 * HS + b % HS, 512)


class Place:
    def __init__(self):
        self.dp = lax.axis_index("dp")
        self.row = lax.axis_index("row")
        self.x = lax.axis_index("col")
        self.zh = lax.div(self.dp, 2)
        self.core = lax.rem(self.dp, 2)
        self.y = lax.div(self.row, 2)
        self.zl = lax.rem(self.row, 2)
        self.z = self.zh * 2 + self.zl

    def at(self, dx=0, dy=0, dz=0, dcore=0):
        x = lax.rem(self.x + (dx + 4), 4)
        y = lax.rem(self.y + (dy + 4), 4)
        z = lax.rem(self.z + (dz + 4), 4)
        core = lax.rem(self.core + dcore, 2)
        return (lax.div(z, 2) * 2 + core, y * 2 + lax.rem(z, 2), x)

    def pair(self):
        return self.at(dcore=1)

    def in_row(self, step):
        return (self.dp, lax.rem(self.row + step, 8), self.x)

    def in_dp(self, step):
        return (lax.rem(self.dp + step, 4), self.row, self.x)


def greet(devices):
    barrier = pltpu.get_barrier_semaphore()
    for device in devices:
        pl.semaphore_signal(barrier, inc=1, device_id=device, device_id_type=MESH)
    pl.semaphore_wait(barrier, len(devices))


class Wire:
    def __init__(self, send, recv, local=None):
        self.send, self.recv, self.local = send, recv, local
        self.sent, self.open, self.near, self.stays = [], {}, [], 0

    def copy(self, src, dst, device):
        n = len(self.sent)
        made = pltpu.make_async_remote_copy(
            src_ref=src,
            dst_ref=dst,
            send_sem=self.send.at[n],
            recv_sem=self.recv.at[n],
            device_id=device,
            device_id_type=MESH,
        )
        made.start()
        self.sent.append(made)
        self.open[n] = made
        return n

    def arrive(self, *numbers):
        for n in numbers:
            self.open.pop(n).wait_recv()

    def stay(self, src, dst):
        made = pltpu.make_async_copy(src, dst, self.local.at[self.stays])
        self.stays += 1
        made.start()
        self.near.append(made)
        return made

    def there(self, *stays):
        for made in stays:
            self.near = [other for other in self.near if other is not made]
            made.wait()

    def settle(self):
        self.arrive(*list(self.open))

    def finish(self):
        self.settle()
        for made in self.sent:
            made.wait_send()
        self.there(*list(self.near))


def around(me):
    return lax.rem(me + 3, 4), lax.rem(me + 1, 4), lax.rem(me + 2, 4)


def ring_gather(wire, me, right, left, own, slot):
    l, r, o = around(me)

    def send(src, dst, device):
        return [wire.copy(a, b, device) for a, b in zip(src, dst)]

    def pass_on(numbers, refs, device):
        passed = []
        for n, ref in zip(numbers, refs):
            wire.arrive(n)
            passed.append(wire.copy(ref, ref, device))
        return passed

    first = send(own(0), slot(me, 0), right), send(own(1), slot(me, 1), left)
    second = send(own(1), slot(me, 1), right), send(own(0), slot(me, 0), left)
    yield
    far = pass_on(first[0], slot(l, 0), right) + pass_on(first[1], slot(r, 1), left)
    yield
    wire.arrive(*second[0], *second[1])
    yield
    wire.arrive(*far)


def leading(ref):
    found = [()]
    for size in ref.shape[:-2]:
        found = [index + (n,) for index in found for n in range(size)]
    return found


def add_parts(out, refs):
    for index in leading(out):
        at = index + (slice(None), slice(None))
        total = refs[0][at].astype(F32)
        for ref in refs[1:]:
            total = total + ref[at].astype(F32)
        out[at] = total.astype(out.dtype)


def ring_sum(wire, me, right, left, part, far, near, out):
    l, r, o = around(me)

    def send(srcs, dsts, device):
        return [wire.copy(a, b, device) for a, b in zip(srcs, dsts)]

    far0 = send(part(o, 0), far(0), right)
    far1 = send(part(o, 1), far(1), left)
    to_right = send(part(r, 1), near(0, 1), right)
    to_left = send(part(l, 0), near(1, 0), left)
    yield
    for n, a, b, c in zip(far0, far(0), part(r, 0), near(0, 0)):
        wire.arrive(n)
        add_parts(a, [a, b])
        to_right.append(wire.copy(a, c, right))
    for n, a, b, c in zip(far1, far(1), part(l, 1), near(1, 1)):
        wire.arrive(n)
        add_parts(a, [a, b])
        to_left.append(wire.copy(a, c, left))
    yield
    wire.arrive(*to_right, *to_left)
    for h in range(2):
        for a, b, c, total in zip(part(me, h), near(0, h), near(1, h), out(h)):
            add_parts(total, [a, b, c])


def side_by_side(*flows):
    flows = list(flows)
    while flows:
        for flow in list(flows):
            try:
                next(flow)
            except StopIteration:
                flows.remove(flow)


def rows(ref, start, size, multiple):
    return ref.at[pl.ds(pl.multiple_of(start, multiple), size)]


def weight_gather(wire, here, own, whole, z_first=False):
    core, zl = here.core, here.zl
    right, left = here.at(dy=1), here.at(dy=-1)
    up, down = here.at(dz=1), here.at(dz=-1)
    l, r, o = around(here.y)

    def mine(j):
        start = (core * 64, core * 64 + 32, 128 + core * 32, 144 + core * 32)[j]
        return rows(own, start, (32, 32, 16, 16)[j], 16)

    def piece(y, j, lo):
        block = y * 2 + lo
        main, rest = block * 128 + core * 64, 1024 + block * 64 + core * 32
        start = (main, main + 32, rest, rest + 16)[j]
        return rows(whole, start, (32, 32, 16, 16)[j], 16)

    def to_pair(y, lo):
        block = y * 2 + lo
        for view in (
            rows(whole, block * 128 + core * 64, 64, 64),
            rows(whole, 1024 + block * 64 + core * 32, 32, 32),
        ):
            paired.append(wire.copy(view, view, here.pair()))

    paired = []

    def over(y, js, device, src=None):
        return [wire.copy((src or (lambda j: piece(y, j, zl)))(j), piece(y, j, zl), device) for j in js]

    y = here.y
    kept = (
        wire.stay(own.at[pl.ds(0, 128)], rows(whole, here.row * 128, 128, 128)),
        wire.stay(own.at[pl.ds(128, 64)], rows(whole, 1024 + here.row * 64, 64, 64)),
    )
    z_own = lambda: over(y, (0, 2), up, mine) + over(y, (1, 3), down, mine)
    if z_first:
        z_y = z_own()
        yield
    r_first, l_first = over(y, (0, 2), right, mine), over(y, (1, 3), left, mine)
    r_next, l_next = over(y, (1, 3), right, mine), over(y, (0, 2), left, mine)
    if not z_first:
        z_y = z_own()
    yield
    wire.arrive(*r_first)
    far = over(l, (0, 2), right)
    wire.arrive(*l_first)
    far += over(r, (1, 3), left)
    z_l = over(l, (0, 2), up)
    z_r = over(r, (1, 3), down)
    yield
    wire.arrive(*r_next)
    z_l += over(l, (1, 3), down)
    to_pair(l, zl)
    wire.arrive(*l_next)
    z_r += over(r, (0, 2), up)
    to_pair(r, zl)
    yield
    wire.arrive(*far)
    z_o = over(o, (0, 2), up) + over(o, (1, 3), down)
    to_pair(o, zl)
    yield
    for block, numbers in ((y, z_y), (l, z_l), (r, z_r), (o, z_o)):
        wire.arrive(*numbers)
        to_pair(block, 1 - zl)
        yield
    wire.arrive(*paired)
    wire.there(*kept)


def token_pieces(half):
    return [pl.ds(64 * half + n, 16) for n in range(0, 64, 16)]


def share(wire, here, out):
    half = lambda i, h: [out.at[i, at] for at in token_pieces(h)]
    return ring_gather(
        wire, here.x, here.at(dx=1), here.at(dx=-1), lambda h: half(here.x, h), half
    )


def to_pair(wire, here, out):
    return wire.copy(out.at[pl.ds(0, 4)], out.at[pl.ds(4, 4)], here.pair())


def x_sum(wire, here, part, far, near, out):
    at = token_pieces
    return ring_sum(
        wire,
        here.x,
        here.at(dx=1),
        here.at(dx=-1),
        lambda i, h: [part.at[i, n] for n in at(h)],
        lambda h: [far.at[n] for n in at(h)],
        lambda s, h: [near.at[s, n] for n in at(h)],
        lambda h: [out.at[n] for n in at(h)],
    )


def x_sum_scratch():
    return [pltpu.VMEM((128, D), BF), pltpu.VMEM((2, 128, D), BF)]


HIGHS = (64, 32)


def order_columns(width, cut, order):
    return (0, cut) if order == 0 else (cut, width - cut)


def first_scratch(width, cut):
    shapes = []
    for order in range(2):
        size = order_columns(width, cut, order)[1]
        for high in HIGHS:
            shapes += [
                pltpu.VMEM((2, 2, high, size), BF),
                pltpu.VMEM((2, 2, 2, high, size), BF),
            ]
    return shapes


def half_sums(width, cut):
    return [
        (2, 2, high, order_columns(width, cut, order)[1]) for order in range(2) for high in HIGHS
    ]


def second_scratch(width, cut):
    shapes = []
    for order in range(2):
        size = order_columns(width, cut, order)[1]
        for high in HIGHS:
            shapes += [
                pltpu.VMEM((2, high // 2, size), BF),
                pltpu.VMEM((2, 2, high // 2, size), BF),
            ]
    return shapes + [pltpu.VMEM((96, width), BF)]


def rings(here):
    y_ring = (here.y, here.at(dy=1), here.at(dy=-1))
    z_ring = (here.z, here.at(dz=1), here.at(dz=-1))
    return y_ring, z_ring


def first_sums(wire, here, grads, scratch, sums, width, cut):
    def flow(order):
        at = pl.ds(*order_columns(width, cut, order))
        buffers, out = scratch[4 * order : 4 * order + 4], sums[2 * order : 2 * order + 2]

        def of_z(ref, i, h):
            return ref.at[pl.ds(2 * h, 2), lax.rem(i, 2), lax.div(i, 2), :, at]

        def of_y(ref, i, h):
            return ref.at[i, h, :, :, at]

        pick = of_z if order == 0 else of_y
        return ring_sum(
            wire,
            *rings(here)[1 - order],
            lambda i, h: [pick(g, i, h) for g in grads],
            lambda h: [b.at[h] for b in buffers[0::2]],
            lambda s, h: [b.at[s, h] for b in buffers[1::2]],
            lambda h: [b.at[h] for b in out],
        )

    return flow(0), flow(1)


def second_sums(wire, here, sums, scratch, width, cut):
    fin = scratch[-1]

    def flow(order):
        at = pl.ds(*order_columns(width, cut, order))
        buffers, terms = scratch[4 * order : 4 * order + 4], sums[2 * order : 2 * order + 2]

        def part(i, h):
            high, low = lax.div(i, 2), lax.rem(i, 2)
            lead = (high, low) if order == 0 else (low, high)
            return [
                b.at[lead[0], lead[1], pl.ds(tall // 2 * h, tall // 2)]
                for b, tall in zip(terms, HIGHS)
            ]

        return ring_sum(
            wire,
            *rings(here)[order],
            part,
            lambda h: [b.at[h] for b in buffers[0::2]],
            lambda s, h: [b.at[s, h] for b in buffers[1::2]],
            lambda h: [
                fin.at[pl.ds(start + tall // 2 * h, tall // 2), at]
                for start, tall in zip((0, 64), HIGHS)
            ],
        )

    return flow(0), flow(1)


def grad_share(wire, here, fin, out, width):
    columns = pl.ds(pl.multiple_of(here.core * width, 128), width)
    mine = out.at[here.zh, :, columns]
    other = out.at[1 - here.zh, :, columns]
    wire.stay(fin, mine)
    wire.copy(fin, mine, here.pair())
    n = wire.copy(fin, mine, here.at(dz=2))
    yield
    wire.arrive(n)
    wire.copy(other, other, here.pair())


def swap_rows(wire, here, src, dst):
    return [
        wire.copy(src.at[lax.rem(here.row + s, 8)], dst.at[here.row], here.in_row(s))
        for s in range(1, 8)
    ]


def low_lanes(rows):
    return lax.broadcasted_iota(jnp.int32, (rows, 128), 1) < 64


def widened(ref):
    main = [ref[r, 0:128, :] for r in range(8)]
    rest = []
    for j in range(4):
        even, odd = ref[2 * j, 128:192, :].astype(F32), ref[2 * j + 1, 128:192, :].astype(F32)
        top = jnp.where(low_lanes(64), even, odd)
        bottom = pltpu.roll(jnp.where(low_lanes(64), odd, even), 64, 1)
        rest.append(jnp.concatenate([top, bottom], axis=0).astype(BF))
    return jnp.concatenate(main + rest, axis=1)


def widened_rows(ref, start, size):
    main = [ref[r, start : start + size, :] for r in range(8)]
    after = slice(start + size, start + 2 * size)
    rest = [ref[2 * j, after, :] + ref[2 * j + 1, after, :] for j in range(4)]
    return jnp.concatenate(main + rest, axis=1)


def narrowed(out, value):
    for r in range(8):
        out[r, 0:128, :] = value[:, 128 * r : 128 * r + 128].astype(BF)
        j = 1024 + 128 * (r // 2)
        top, bottom = value[0:64, j : j + 128], value[64:128, j : j + 128]
        if r % 2 == 0:
            rest = jnp.where(low_lanes(64), top, pltpu.roll(bottom, 64, 1))
        else:
            rest = jnp.where(low_lanes(64), pltpu.roll(top, 64, 1), bottom)
        out[r, 128:192, :] = rest.astype(BF)


def narrowed_rows(out, value):
    for r in range(8):
        out[r, :, 0:128] = value[:, 128 * r : 128 * r + 128]
        j = 1024 + 128 * (r // 2)
        out[r, :, 128:256] = value[:, j : j + 128]


def ring_partners(here):
    return [here.at(dx=1), here.at(dx=-1)]


def plane_partners(here):
    return [here.at(dy=1), here.at(dy=-1), here.at(dz=1), here.at(dz=-1)]


def dot(a, b, left=1, right=0):
    return lax.dot_general(a, b, (((left,), (right,)), ((), ())), preferred_element_type=F32)


def turned(values, cosine, sine):
    lane = lax.broadcasted_iota(jnp.int32, values.shape, 1)
    front = lax.rem(lane, HS) < HS // 2
    ahead, back = pltpu.roll(values, 256 - HS // 2, 1), pltpu.roll(values, HS // 2, 1)
    return values * cosine + jnp.where(front, -ahead, back) * sine


def packed_pair(a, b):
    return jnp.concatenate([a[:, :128], a[:, 128:] + b[:, :128], b[:, 128:]], axis=1)


def windows(y):
    return ((0, 4), (0, 8), (1 + y, 8), (5 + y, 8))


def allowed_keys(table, c, start, count):
    key = start * 128 + lax.broadcasted_iota(jnp.int32, (count * 128, 256), 0)
    return (key >= table[2 * c : 2 * c + 1]) & (key <= table[2 * c + 1 : 2 * c + 2])


def both_heads(ref, at):
    return jnp.concatenate([ref[at, 0:256], ref[at, 256:512]], axis=0)


def attend(here, q, kv, table, heads, log_total):
    lane = lax.broadcasted_iota(jnp.int32, (256, 256), 1)
    for c, (start, count) in enumerate(windows(here.y)):
        at = pl.ds(128 * c, 128)
        allowed = allowed_keys(table, c, start, count)
        q_both = both_heads(q, at)
        k = kv[pl.ds(start, count), :, 0:256].reshape(count * 128, 256)
        v = kv[pl.ds(start, count), :, 128:384].reshape(count * 128, 256)
        made = []
        for g in range(2):
            n = 2 * c + g
            q_one = jnp.where((lane >= HS) == (g == 1), q_both, jnp.zeros_like(q_both))
            scores = dot(k, q_one, 1, 1) * score_scale
            scores = jnp.where(allowed, scores, -1e30)
            top = jnp.max(scores, axis=0, keepdims=True)
            weights = jnp.exp(scores - top)
            total = jnp.sum(weights, axis=0, keepdims=True)
            shares = (weights * (1.0 / total)).astype(BF)
            made.append(dot(shares, v, 0, 0))
            log_total[n : n + 1] = top + jnp.log(total)
        out = jnp.where(lane < 64 + HS, made[0], made[1])
        out = jnp.where(lane < 64, 0.0, out).astype(BF)
        heads[at, 0:256] = out[:128]
        heads[at, 256:512] = out[128:]
        yield


def attend_back(here, q, kv, table, log_total, dout, dq, total):
    lane = lax.broadcasted_iota(jnp.int32, (256, 256), 1)
    total[...] = jnp.zeros_like(total)
    for c, (start, count) in reversed(list(enumerate(windows(here.y)))):
        at = pl.ds(128 * c, 128)
        blocks = pl.ds(start, count)
        allowed = allowed_keys(table, c, start, count)
        q_both, d_both = both_heads(q, at), both_heads(dout, at)
        k = kv[blocks, :, 0:256].reshape(count * 128, 256)
        v = kv[blocks, :, 128:384].reshape(count * 128, 256)
        made = []
        for g in range(2):
            n = 2 * c + g
            q_one = jnp.where((lane >= HS) == (g == 1), q_both, jnp.zeros_like(q_both))
            d_one = jnp.where((lane >= 64 + HS) == (g == 1), d_both, jnp.zeros_like(d_both))
            scores = dot(k, q_one, 1, 1) * score_scale
            shares = jnp.where(allowed, jnp.exp(scores - log_total[n : n + 1]), 0.0)
            dshares = dot(v, d_one, 1, 1)
            inner = jnp.sum(shares * dshares, axis=0, keepdims=True)
            dscores = (shares * (dshares - inner)).astype(BF)
            made.append(dot(dscores, k, 0, 0))
            dk = dot(dscores, q_one) * score_scale
            dv = dot(shares.astype(BF), d_one)
            total[blocks, :, 0:256] += dk.reshape(count, 128, 256)
            total[blocks, :, 128:384] += dv.reshape(count, 128, 256)
        out = jnp.where(lane < HS, made[0], made[1]) * score_scale
        dq[at, 0:256] = out[:128]
        dq[at, 256:512] = out[128:]
        yield


def tokens_of(ref, pair=0):
    return ref[4 * pair : 4 * pair + 4].reshape(512, D)


def columns(n, size=256):
    return pl.ds(pl.multiple_of(n * size, size), size)


def back_to_width(units, weights, out, token_at=slice(None)):
    @pl.loop(0, D // 256)
    def _(n):
        made = dot(units(), weights[columns(n), :], 1, 1)
        out[:, token_at, columns(n)] = made.astype(BF).reshape(4, made.shape[0] // 4, 256)


def weight_grads(tokens, own, pair, main, rest, at):
    def made(n):
        total = dot(tokens[0:4, :, columns(n)].reshape(512, 256), own(), 0, 0)
        return total + dot(tokens[4:8, :, columns(n)].reshape(512, 256), pair(), 0, 0)

    @pl.loop(0, 4)
    def _(n):
        value = made(n)
        main[n, :, :, :, at] = value.astype(BF).reshape(2, 2, 64, value.shape[1])

    @pl.loop(0, 2)
    def _(n):
        value = made(n + 4)
        rest[pl.ds(2 * n, 2), :, :, :, at] = value.astype(BF).reshape(2, 2, 2, 32, value.shape[1])


def norm_back(value, grad, gain):
    scale = lax.rsqrt(jnp.mean(value * value, axis=1, keepdims=True) + norm_epsilon)
    unit = value * scale
    scaled = grad * gain
    inner = jnp.mean(scaled * unit, axis=1, keepdims=True)
    return scale * (scaled - unit * inner), jnp.sum(grad * unit, axis=0, keepdims=True)


def normed(value, gain):
    scale = lax.rsqrt(jnp.mean(value * value, axis=1, keepdims=True) + norm_epsilon)
    return (value * scale * gain).astype(BF)


def key_block(c, y):
    return 4 * c + y


def pack_rows(here, out, values):
    for y in range(4):
        for zl in range(2):
            block = values[zl, :, 128 * y : 128 * y + 128]
            rest = block[128:]
            swapped = pltpu.roll(rest, 64, 1)
            first = jnp.where(here.zl == 0, rest, swapped)
            second = jnp.where(here.zl == 0, swapped, rest)
            out[2 * y + zl, 0:128, :] = block[:128].T.astype(BF)
            both = jnp.concatenate([first, second], axis=0).T
            out[2 * y + zl, 128:192, :] = both[0:64].astype(BF)


def own_half(here, rest):
    return jnp.where(here.zl == 0, rest, pltpu.roll(rest, 64, 1))


def enter_kernel(
    stream, cotangent, qkv_weight, out_weight, gate_up, down, gains, positions, frequency, qkv_at, out_at,
    h1_out, wq_out, wo_out, c_out, kv_out, down_out, w_both,
    q_out, heads_out, cosine_out, sine_out, xtok_out, ctok_out,
    rise, h2_own, log_total, gtok, table,
    q, heads, cosine, sine, xtok, ctok,
    xf, cf, qf, of, gf, df, qs, os, xin, cin, wq_own, wo_own, win,
    xbuf, cbuf, h1_all, c_all, wq, wo, part, far, near, kv_own, kv_all, qkv, gpad, send, recv, local,
):
    here = Place()
    wire = Wire(send, recv, local)
    x_load = wire.stay(stream, xf)
    greet(
        [here.in_row(s) for s in range(1, 8)]
        + ring_partners(here)
        + [here.at(dz=1), here.at(dz=-1), here.pair()]
    )
    gpad[...] = jnp.zeros_like(gpad)
    gpad[0:2, 0:192] = gains[...]
    g = gpad[...]
    high = g.astype(BF).astype(F32)
    rows4 = jnp.concatenate([high[0:2], (g - high)[0:2]], axis=0)
    rest = rows4[:, 128:]
    rest = jnp.where(here.zl == 0, rest, pltpu.roll(rest, 64, 1))
    rows16 = jnp.concatenate([rows4[:, :128], rest, jnp.zeros((8, 128), F32)], axis=0).astype(BF)
    wire.there(x_load)
    q_load = wire.stay(qkv_weight, qf), wire.stay(qkv_at, qs)
    for r in range(8):
        xin[r, 192:208, :] = rows16
    pack_rows(here, xin, xf)
    xs = swap_rows(wire, here, xin, xbuf)
    xbuf[here.row] = xin[here.row]
    o_load = wire.stay(out_weight, of), wire.stay(out_at, os)
    c_load = wire.stay(cotangent, cf)
    f_load = [wire.stay(gate_up.at[:, j], gf.at[j]) for j in range(2)] + [wire.stay(down, df)]

    wire.there(*q_load)
    wq_own[...] = dot(qf[...].astype(BF), qs[...], 1, 1).astype(BF)
    q_weights = weight_gather(wire, here, wq_own, wq)
    next(q_weights)
    wire.there(*o_load)
    wo_own[...] = dot(of[...].astype(BF), os[...], 1, 1).astype(BF)
    o_weights = weight_gather(wire, here, wo_own, wo)
    lane = lax.broadcasted_iota(jnp.int32, (128, 256), 1)
    for c in range(4):
        first = 512 * c + 128 * here.y
        place = positions[:, pl.ds(pl.multiple_of(first, 128), 128)]
        place = jnp.where(here.zl == 0, place[0:1], place[1:2])
        token = first + lax.broadcasted_iota(jnp.int32, (1, 128), 1)
        table[2 * c : 2 * c + 1, :] = jnp.concatenate([token - place] * 2, axis=1)
        table[2 * c + 1 : 2 * c + 2, :] = jnp.concatenate([token] * 2, axis=1)
        column = jnp.broadcast_to(place.astype(F32), (128, 128)).T[:, 0:1]
        angles = column * frequency[0:1]
        at = pl.ds(128 * c, 128)
        cosine[at, :] = jnp.where(lane < 2 * HS, jnp.cos(angles), 0.0)
        sine[at, :] = jnp.where(lane < 2 * HS, jnp.sin(angles), 0.0)
    wire.stay(cosine, cosine_out)
    wire.stay(sine, sine_out)
    wire.there(c_load)
    pack_rows(here, cin, cf)
    cbuf[here.row] = cin[here.row]

    next(q_weights)
    wire.arrive(*xs)
    x = widened(xbuf)
    xtok[...] = x
    wire.stay(xtok, xtok_out)
    g = widened_rows(xbuf, 192, 4).astype(F32)
    g = g[0:2] + g[2:4]
    gtok[...] = g
    h1_all[here.x] = normed(x.astype(F32), g[0:1])
    h1_flow = share(wire, here, h1_all)
    next(h1_flow)
    next(q_weights)
    wire.there(*f_load)
    for k in range(2):
        for j in range(2):
            at = 1024 * k + 512 * j
            win[:, at : at + 512] = gf[j, :, 512 * k : 512 * k + 512].astype(BF)
    win[:, 2048:3072] = df[...].astype(BF)
    wire.stay(win.at[:, pl.ds(2048, 1024)], down_out)
    next(q_weights)
    next(o_weights)
    cs = swap_rows(wire, here, cin, cbuf)
    next(h1_flow)
    for _ in range(4):
        next(q_weights)
    next(h1_flow)
    next(o_weights)
    side_by_side(h1_flow, q_weights)
    wire.stay(wq, wq_out)
    wire.stay(h1_all, h1_out)
    wire.arrive(*cs)
    c_value = widened(cbuf)
    ctok[...] = c_value
    wire.stay(ctok, ctok_out)
    c_all[here.x] = c_value
    c_flow = share(wire, here, c_all)
    next(c_flow)
    next(o_weights)

    @pl.loop(0, 3)
    def _(n):
        qkv[:, columns(n)] = dot(tokens_of(h1_all), wq[:, columns(n)])

    for c in range(4):
        at = pl.ds(128 * c, 128)
        turn = cosine[at], sine[at]
        key = turned(qkv[at, 384:640], *turn)
        value = jnp.where(lane < 64, 0.0, qkv[at, 512:768])
        kv = packed_pair(key, value).astype(BF)
        kv_own[c] = kv
        kv_all[key_block(c, here.y)] = kv

    keys = ring_gather(
        wire,
        here.y,
        here.at(dy=1),
        here.at(dy=-1),
        lambda h: [kv_own.at[2 * h + n] for n in range(2)],
        lambda i, h: [kv_all.at[key_block(2 * h + n, i)] for n in range(2)],
    )
    next(keys)
    for c in range(4):
        at = pl.ds(128 * c, 128)
        turn = cosine[at], sine[at]
        q[at, 0:256] = turned(qkv[at, 0:256], *turn).astype(BF)
        second = pltpu.roll(qkv[at, 128:384], 192, 1)
        q[at, 256:512] = turned(second, *turn).astype(BF)
    next(o_weights)
    next(c_flow)
    next(keys)
    for _ in range(4):
        next(o_weights)
    weights = weight_gather(wire, here, win.at[:, pl.ds(0, 2048)], w_both, True)
    next(weights)
    next(c_flow)
    side_by_side(keys, c_flow)
    next(weights)
    for _ in attend(here, q, kv_all, table, heads, log_total):
        pass
    side_by_side(o_weights)
    for held, out in ((c_all, c_out), (wo, wo_out), (kv_all, kv_out), (q, q_out)):
        wire.stay(held, out)
    wire.stay(heads, heads_out)
    back_to_width(lambda: heads[...], wo, part)
    chain = x_sum(wire, here, part, far, near, rise)
    next(chain)
    next(weights)
    next(weights)
    next(chain)
    next(weights)
    side_by_side(chain, weights)
    h2_own[...] = normed(rise[...] + xtok[...].astype(F32), gtok[1:2])
    wire.finish()


def shape(dtype, *sizes):
    return jax.ShapeDtypeStruct(sizes, dtype)


def signals(*counts):
    return [pltpu.SemaphoreType.DMA((n,)) for n in counts]


def settings(number):
    return pltpu.CompilerParams(
        collective_id=number, has_side_effects=True, vmem_limit_bytes=60 << 20
    )


def enter(*operands):
    return pl.pallas_call(
        enter_kernel,
        out_shape=[
            shape(BF, 4, 128, D),
            shape(BF, D, 768),
            shape(BF, D, 512),
            shape(BF, 4, 128, D),
            shape(BF, 16, 128, 384),
            shape(BF, 192, 1024),
            shape(BF, D, 2048),
            shape(BF, 512, 512),
            shape(BF, 512, 512),
            shape(F32, 512, 256),
            shape(F32, 512, 256),
            shape(BF, 128, D),
            shape(BF, 128, D),
            shape(F32, 128, D),
            shape(BF, 128, D),
            shape(F32, 8, 256),
            shape(F32, 2, D),
            shape(jnp.int32, 8, 256),
        ],
        in_specs=[ANY] * 6 + [VM] * 3 + [ANY] * 2,
        out_specs=[ANY] * 13 + [VM] * 5,
        scratch_shapes=[
            pltpu.VMEM((512, 512), BF),
            pltpu.VMEM((512, 512), BF),
            pltpu.VMEM((512, 256), F32),
            pltpu.VMEM((512, 256), F32),
            pltpu.VMEM((128, D), BF),
            pltpu.VMEM((128, D), BF),
            pltpu.VMEM((2, 192, 512), F32),
            pltpu.VMEM((2, 192, 512), F32),
            pltpu.VMEM((192, 768), F32),
            pltpu.VMEM((192, 384), F32),
            pltpu.VMEM((2, 192, 1024), F32),
            pltpu.VMEM((192, 1024), F32),
            pltpu.VMEM((768, 768), BF),
            pltpu.VMEM((512, 384), BF),
            pltpu.VMEM((8, 208, 128), BF),
            pltpu.VMEM((8, 192, 128), BF),
            pltpu.VMEM((192, 768), BF),
            pltpu.VMEM((192, 512), BF),
            pltpu.VMEM((192, 3072), BF),
            pltpu.VMEM((8, 208, 128), BF),
            pltpu.VMEM((8, 192, 128), BF),
            pltpu.VMEM((4, 128, D), BF),
            pltpu.VMEM((4, 128, D), BF),
            pltpu.VMEM((D, 768), BF),
            pltpu.VMEM((D, 512), BF),
            pltpu.VMEM((4, 128, D), BF),
        ]
        + x_sum_scratch()
        + [
            pltpu.VMEM((4, 128, 384), BF),
            pltpu.VMEM((16, 128, 384), BF),
            pltpu.VMEM((512, 768), F32),
            pltpu.VMEM((8, 256), F32),
        ]
        + signals(256, 256, 32),
        compiler_params=settings(1),
        name="enter",
    )(*operands)


BOTH = (1024, 512)
DOWN = (512, 256)


def feed_kernel(*refs):
    h2_own, gtok, rise_in, xtok_in, ctok_in, down_own, both_w, c_in = refs[:8]
    after_out, gain, f_out, d_out = refs[8:12]
    both_sums, down_sums = refs[12:16], refs[16:20]
    after, f_part, far, near, middle, summed, h2_all, c_all = refs[20:28]
    w_down, w_both, both, act, both_in, act_in, hidden, part2, d_all = refs[28:37]
    main, rest, down_main, down_rest = refs[37:41]
    rise, xtok, ctok = refs[41:44]
    both_first, down_first, (send, recv, local) = refs[44:52], refs[52:60], refs[60:]
    here = Place()
    wire = Wire(send, recv, local)
    greet(ring_partners(here) + plane_partners(here) + [here.pair()])
    h2_all[here.x] = h2_own[...]
    chain = share(wire, here, h2_all)
    next(chain)
    down = weight_gather(wire, here, down_own, w_down)
    next(down)
    loads = [wire.stay(a, b) for a, b in ((rise_in, rise), (xtok_in, xtok), (ctok_in, ctok))]
    loads += [wire.stay(c_in, c_all.at[pl.ds(0, 4)]), wire.stay(both_w, w_both)]
    next(chain)
    next(down)
    next(down)
    wire.there(loads[3])
    c_paired = to_pair(wire, here, c_all)
    next(down)
    next(chain)
    for _ in range(4):
        next(down)
    side_by_side(chain)
    wire.there(*loads[:3], loads[4])
    middle[...] = rise[...] + xtok[...].astype(F32)
    paired = [to_pair(wire, here, h2_all)]

    @pl.loop(0, 8)
    def _(n):
        hidden[:, columns(n)] = dot(tokens_of(h2_all), w_both[:, columns(n)])

    side_by_side(down)

    def unit_tiles(half):
        @pl.loop(0, 2)
        def _(n):
            at, down_at = columns(half * 4 + n), columns(half * 2 + n)
            up_at = columns(half * 4 + n + 2)
            gate, up = hidden[:, at], hidden[:, up_at]
            grad = dot(tokens_of(c_all), w_down[:, down_at])
            sigmoid = 1.0 / (1.0 + jnp.exp(-gate))
            silu = gate * sigmoid
            both[:, at] = (grad * up * sigmoid * (1.0 + gate * (1.0 - sigmoid))).astype(BF)
            both[:, up_at] = (grad * silu).astype(BF)
            act[:, down_at] = (silu * up).astype(BF)

    other = 1 - here.core
    unit_tiles(other)
    paired.append(wire.copy(both.at[:, columns(other, 1024)], both_in, here.pair()))
    act_swap = wire.copy(act.at[:, columns(other, 512)], act_in, here.pair())
    unit_tiles(here.core)
    back_to_width(lambda: both[...], w_both, part2)

    def backward():
        yield from x_sum(wire, here, part2, far, near, summed)
        left, gain_terms = norm_back(middle[...], summed[...], gtok[1:2])
        gain[...] = jnp.broadcast_to(gain_terms, gain.shape)
        after[...] = left
        d_all[here.x] = (left + ctok[...].astype(F32)).astype(BF)
        wire.stay(after, after_out)
        yield from share(wire, here, d_all)

    chain = backward()
    next(chain)
    wire.arrive(c_paired, act_swap)
    weight_grads(
        c_all, lambda: act[:, columns(here.core, 512)], lambda: act_in[...], down_main, down_rest, slice(None)
    )
    flows = first_sums(wire, here, (down_main, down_rest), down_first, down_sums, *DOWN)
    for flow in flows:
        next(flow)
    wire.arrive(*paired)
    weight_grads(
        h2_all, lambda: both[:, columns(here.core, 1024)], lambda: both_in[...], main, rest, slice(None)
    )
    both_flows = first_sums(wire, here, (main, rest), both_first, both_sums, *BOTH)
    for flow in both_flows:
        next(flow)
    next(chain)
    back_to_width(lambda: act[...], w_down, f_part)
    wire.stay(f_part, f_out)
    for flow in flows:
        next(flow)
    next(chain)
    for flow in both_flows:
        next(flow)
    next(chain)
    next(chain)
    side_by_side(chain)
    wire.stay(d_all, d_out)
    side_by_side(*flows, *both_flows)
    wire.finish()


def grad_shapes(width):
    return [(4, 2, 2, high, width) for high in HIGHS]


def grad_arrays(width):
    return [pltpu.VMEM(sizes, BF) for sizes in grad_shapes(width)]


def feed(*operands):
    return pl.pallas_call(
        feed_kernel,
        out_shape=[
            shape(F32, 128, D),
            shape(F32, 8, D),
            shape(BF, 4, 128, D),
            shape(BF, 4, 128, D),
        ]
        + [shape(BF, *sizes) for sizes in half_sums(*BOTH) + half_sums(*DOWN)],
        in_specs=[VM] * 2 + [ANY] * 6,
        out_specs=[ANY, VM] + [ANY] * 2 + [VM] * 8,
        scratch_shapes=[
            pltpu.VMEM((128, D), F32),
            pltpu.VMEM((4, 128, D), BF),
        ]
        + x_sum_scratch()
        + [
            pltpu.VMEM((128, D), F32),
            pltpu.VMEM((128, D), F32),
            pltpu.VMEM((8, 128, D), BF),
            pltpu.VMEM((8, 128, D), BF),
            pltpu.VMEM((D, 1024), BF),
            pltpu.VMEM((D, 2048), BF),
            pltpu.VMEM((512, 2048), BF),
            pltpu.VMEM((512, 1024), BF),
            pltpu.VMEM((512, 1024), BF),
            pltpu.VMEM((512, 512), BF),
            pltpu.VMEM((512, 2048), F32),
            pltpu.VMEM((4, 128, D), BF),
            pltpu.VMEM((4, 128, D), BF),
        ]
        + grad_arrays(BOTH[0])
        + grad_arrays(DOWN[0])
        + [pltpu.VMEM((128, D), F32), pltpu.VMEM((128, D), BF), pltpu.VMEM((128, D), BF)]
        + first_scratch(*BOTH)
        + first_scratch(*DOWN)
        + signals(200, 200, 16),
        compiler_params=settings(2),
        name="feed",
    )(*operands)


ATTN = (640, 256)


def leave_held():
    sizes = [(4, 128, D)]
    sizes += half_sums(*BOTH) + half_sums(*DOWN)
    sizes += [(4, 128, D), (D, 512), (512, 512), (16, 128, 384), (512, 512), (4, 128, D)]
    sizes += [(D, 768), (128, D)]
    return [(size, BF) for size in sizes] + [
        ((128, D), F32), ((128, D), F32), ((512, 256), F32), ((512, 256), F32)
    ]


def leave_kernel(*refs):
    gtok, gain, log_total, table = refs[:4]
    count = len(leave_held())
    held_in, refs = refs[4 : 4 + count], refs[4 + count :]
    o_all, s_all, gout, both_out, down_out, gains_out = refs[:6]
    held, refs = refs[6 : 6 + count], refs[6 + count :]
    f_part, both_sums, down_sums = held[0], held[1:5], held[5:9]
    d_all, wo, q, kv_all, heads, h1_all, wq, xtok, rise, after, cosine, sine = held[9:]
    dout, dq, total, dkv, kfar, knear, dkv_own, dqkv = refs[:8]
    heads_in, dqkv_in, part, far, near, far2, near2, summed, osend, ssend = refs[8:18]
    gsend, grow, gcol, gdp, main, rest = refs[18:24]
    scratch, (send, recv, local) = refs[24:-3], refs[-3:]
    a_first, a_sums, a_second = scratch[:8], scratch[8:12], scratch[12:21]
    both_second, down_second = scratch[21:30], scratch[30:39]
    here = Place()
    wire = Wire(send, recv, local)
    def load(first, last):
        made = []
        for src, dst in zip(held_in[first:last], held[first:last]):
            dst = dst.at[pl.ds(0, 4)] if dst.shape != src.shape else dst
            made.append(wire.stay(src, dst))
        return made

    attention_loads = load(9, 14)
    greet(
        [here.in_row(s) for s in range(1, 8)]
        + ring_partners(here)
        + [here.at(dz=1), here.at(dz=-1), here.at(dx=2)]
        + [here.in_dp(s) for s in range(1, 4)]
    )
    wire.there(*attention_loads[:2])
    sums_loads = load(0, 9)

    @pl.loop(0, 2)
    def _(n):
        dout[:, columns(n)] = dot(tokens_of(d_all), wo[:, columns(n)]).astype(BF)

    wire.there(*attention_loads[2:])
    heads_swap = wire.copy(heads.at[:, columns(1 - here.core)], heads_in, here.pair())
    wire.there(*sums_loads)
    branch_sum = x_sum(wire, here, f_part, far, near, summed)
    next(branch_sum)
    sums = second_sums(wire, here, both_sums, both_second, *BOTH)
    sums += second_sums(wire, here, down_sums, down_second, *DOWN)
    for flow in sums:
        next(flow)
    d_paired = to_pair(wire, here, d_all)
    late_loads = load(14, count)

    def key_sums(half):
        block = lambda h: 2 * half + h
        return ring_sum(
            wire,
            here.y,
            here.at(dy=1),
            here.at(dy=-1),
            lambda i, h: [dkv.at[key_block(block(h), i)]],
            lambda h: [kfar.at[half, h]],
            lambda s, h: [knear.at[half, s, h]],
            lambda h: [dkv_own.at[pl.ds(128 * block(h), 128)]],
        )

    attention = attend_back(here, q, kv_all, table, log_total, dout, dq, total)
    next(attention)
    wire.there(late_loads[0])
    h1_paired = to_pair(wire, here, h1_all)
    for flow in sums:
        next(flow)
    next(attention)
    dkv[8:16] = total[8:16].astype(BF)
    late_keys = key_sums(1)
    next(late_keys)
    next(attention)
    next(branch_sum)
    next(attention)
    next(late_keys)
    dkv[0:8] = total[0:8].astype(BF)
    keys = key_sums(0)
    next(keys)
    wire.there(*late_loads[1:])
    side_by_side(*sums)
    both_share = grad_share(wire, here, both_second[-1], both_out, BOTH[0])
    down_share = grad_share(wire, here, down_second[-1], down_out, DOWN[0])
    next(both_share)
    next(down_share)
    side_by_side(branch_sum)
    narrowed(osend, summed[...] + rise[...])
    for c in range(4):
        at = pl.ds(128 * c, 128)
        turn = cosine[at], -sine[at]
        second = turned(dq[at, 256:512], *turn)
        both = packed_pair(turned(dq[at, 0:256], *turn), pltpu.roll(second, 64, 1))
        dqkv[at, 0:384] = both.astype(BF)
    next(keys)
    wire.arrive(heads_swap, d_paired)
    weight_grads(
        d_all, lambda: heads[:, columns(here.core)], lambda: heads_in[...], main, rest, slice(384, 640)
    )
    lane = lax.broadcasted_iota(jnp.int32, (128, 256), 1)
    side_by_side(late_keys, keys)
    for c in range(4):
        at = pl.ds(128 * c, 128)
        key = turned(dkv_own[at, 0:256], cosine[at], -sine[at])
        value = jnp.where(lane < 64, 0.0, dkv_own[at, 128:384])
        dqkv[at, 384:768] = packed_pair(key, value).astype(BF)
    dqkv_swap = wire.copy(dqkv.at[:, columns(1 - here.core, 384)], dqkv_in, here.pair())
    back_to_width(lambda: dqkv[...], wq, part)

    def chain():
        yield from x_sum(wire, here, part, far2, near2, summed)
        left, gain_terms = norm_back(xtok[...].astype(F32), summed[...], gtok[0:1])
        gains = jnp.concatenate([gain_terms, gain[0:1], jnp.zeros((6, D), F32)], axis=0)
        narrowed_rows(gsend, gains)
        g = swap_rows(wire, here, gsend, grow)
        narrowed(ssend, left + after[...])
        wire.stay(ssend.at[here.row], s_all.at[here.row])
        swap_rows(wire, here, ssend, s_all)
        yield
        wire.arrive(*g)
        grow[here.row] = gsend[here.row]
        total = grow[0]
        for n in range(1, 8):
            total = total + grow[n]
        gcol[here.x] = total
        g = [wire.copy(gcol.at[here.x], gcol.at[here.x], here.at(dx=s)) for s in range(1, 4)]
        yield
        wire.arrive(*g)
        gdp[here.dp] = ((gcol[0] + gcol[1]) + gcol[2]) + gcol[3]
        g = [wire.copy(gdp.at[here.dp], gdp.at[here.dp], here.in_dp(s)) for s in range(1, 4)]
        yield
        wire.arrive(*g)
        gains_out[...] = ((gdp[0] + gdp[1]) + gdp[2]) + gdp[3]

    steps = chain()
    next(steps)
    side_by_side(both_share, down_share)
    wire.stay(osend.at[here.row], o_all.at[here.row])
    swap_rows(wire, here, osend, o_all)
    wire.arrive(dqkv_swap, h1_paired)
    weight_grads(
        h1_all, lambda: dqkv[:, columns(here.core, 384)], lambda: dqkv_in[...], main, rest, slice(0, 384)
    )
    first = first_sums(wire, here, (main, rest), a_first, a_sums, *ATTN)

    def sums():
        yield
        side_by_side(*first)
        second = second_sums(wire, here, a_sums, a_second, *ATTN)
        for flow in second:
            next(flow)
        yield
        for flow in second:
            next(flow)
        yield
        side_by_side(*second)
        yield from grad_share(wire, here, a_second[-1], gout, ATTN[0])

    for flow in first:
        next(flow)
    next(steps)
    for flow in first:
        next(flow)
    side_by_side(steps, sums())
    wire.finish()


def leave(*operands):
    held = [pltpu.VMEM(size, kind) for size, kind in leave_held()]
    for n in (9, 14):
        held[n] = pltpu.VMEM((8, 128, D), BF)
    return pl.pallas_call(
        leave_kernel,
        out_shape=[
            shape(BF, 8, 192, 128),
            shape(BF, 8, 192, 128),
            shape(BF, 2, 96, 2 * ATTN[0]),
            shape(BF, 2, 96, 2 * BOTH[0]),
            shape(BF, 2, 96, 2 * DOWN[0]),
            shape(F32, 8, 256),
        ],
        in_specs=[VM] * 4 + [ANY] * len(held),
        out_specs=[ANY] * 5 + [VM],
        scratch_shapes=held
        + [
            pltpu.VMEM((512, 512), BF),
            pltpu.VMEM((512, 512), F32),
            pltpu.VMEM((16, 128, 384), F32),
            pltpu.VMEM((16, 128, 384), BF),
            pltpu.VMEM((2, 2, 128, 384), BF),
            pltpu.VMEM((2, 2, 2, 128, 384), BF),
            pltpu.VMEM((512, 384), F32),
            pltpu.VMEM((512, 768), BF),
            pltpu.VMEM((512, 256), BF),
            pltpu.VMEM((512, 384), BF),
            pltpu.VMEM((4, 128, D), BF),
        ]
        + x_sum_scratch()
        + x_sum_scratch()
        + [
            pltpu.VMEM((128, D), F32),
            pltpu.VMEM((8, 192, 128), BF),
            pltpu.VMEM((8, 192, 128), BF),
            pltpu.VMEM((8, 8, 256), F32),
            pltpu.VMEM((8, 8, 256), F32),
            pltpu.VMEM((4, 8, 256), F32),
            pltpu.VMEM((4, 8, 256), F32),
        ]
        + grad_arrays(ATTN[0])
        + first_scratch(*ATTN)
        + [pltpu.VMEM(sizes, BF) for sizes in half_sums(*ATTN)]
        + second_scratch(*ATTN)
        + second_scratch(*BOTH)
        + second_scratch(*DOWN)
        + signals(240, 240, 32),
        compiler_params=settings(3),
        name="leave",
    )(*operands)


def step_rates():
    return (2.0 / D**0.5, 2.0 / max(HQ * HS // 64, 1) ** 0.5, 2.0 / D**0.5, 2.0 / FF**0.5, 0.4)


def adamw(state, at, gradient, step_rate, decay_rate):
    weight, first, second = state
    moment_one = beta_first * first[at] + (1.0 - beta_first) * gradient
    moment_two = beta_second * second[at] + (1.0 - beta_second) * gradient * gradient
    first[at] = moment_one
    second[at] = moment_two
    corrected = (moment_one * (1.0 / (1.0 - beta_first**STEP))) / (
        jnp.sqrt(moment_two * (1.0 / (1.0 - beta_second**STEP))) + adam_epsilon
    )
    old = weight[at]
    weight[at] = old - step_rate * (corrected + decay_rate * old)


def update_kernel(*refs):
    stream, cotangent, o_in, s_in, g_in, both_in, down_in, qkv_at, out_at = refs[:9]
    qkv, out, gate_up, down, gains = (refs[9 + 3 * n : 12 + 3 * n] for n in range(5))
    gains_tile = refs[24]
    o_out, s_out = refs[25:27]
    results = [refs[27 + 3 * n : 30 + 3 * n] for n in range(5)]
    xf, cf, ot, st, gb, fb, db, qs, os = refs[42:51]
    qkv_s, out_s, gate_s, down_s = (refs[51 + 3 * n : 54 + 3 * n] for n in range(4))
    local = refs[63]
    here = Place()
    wire = Wire(None, None, local)
    rate_qkv, rate_out, rate_gate_up, rate_down, rate_gains = step_rates()

    f_load = [wire.stay(both_in, fb)]
    for a, b in zip(gate_up, gate_s):
        f_load += [wire.stay(a.at[:, j], b.at[j]) for j in range(2)]
    d_load = [wire.stay(down_in, db)] + [wire.stay(a, b) for a, b in zip(down, down_s)]
    x_load = [wire.stay(a, b) for a, b in ((stream, xf), (o_in, ot), (cotangent, cf), (s_in, st))]
    a_load = [wire.stay(a, b) for a, b in ((g_in, gb), (qkv_at, qs), (out_at, os))]
    a_load += [wire.stay(a, b) for a, b in zip(qkv + out, qkv_s + out_s)]

    def feed_part(states, grads):
        @pl.loop(0, 4)
        def _(n):
            zh, k = lax.div(n, 2), lax.rem(n, 2)
            for start, size, begin in ((0, 64, 64 * zh), (64, 32, 128 + 32 * zh)):
                at = pl.ds(pl.multiple_of(begin, 32), size), columns(k, 512)
                for a, (state, rate) in enumerate(states):
                    lanes = columns(len(states) * k + a, 512)
                    gradient = grads[zh, start : start + size, lanes].astype(F32)
                    adamw(state, at, gradient, rate, weight_decay)

    wire.there(*f_load)
    feed_part([([b.at[j] for b in gate_s], rate_gate_up) for j in range(2)], fb)
    for a, b in zip(results[2], gate_s):
        for j in range(2):
            wire.stay(b.at[j], a.at[:, j])
    wire.there(*d_load)
    feed_part([(down_s, rate_down)], db)
    for a, b in zip(results[3], down_s):
        wire.stay(b, a)

    wire.there(*x_load)
    for held, tiles, result in ((xf, ot, o_out), (cf, st, s_out)):
        for y in range(4):
            for zl in range(2):
                tile = tiles[2 * y + zl].astype(F32)
                rest = jnp.concatenate([tile[128:192]] * 2, axis=0).T
                rest = jnp.where(low_lanes(64), rest[0:64], rest[64:128])
                at = pl.ds(128 * y, 128)
                held[zl, 0:128, at] = held[zl, 0:128, at] + tile[0:128].T
                held[zl, 128:192, at] = held[zl, 128:192, at] + rest
        wire.stay(held, result)

    wire.there(*a_load)

    def own_block(start, size):
        lanes = [pl.ds(ATTN[0] * k + start, size) for k in range(2)]
        parts = [(0, slice(0, 64)), (1, slice(0, 64)), (0, slice(64, 96)), (1, slice(64, 96))]
        return jnp.concatenate(
            [jnp.concatenate([gb[zh, at, l] for zh, at in parts], axis=0) for l in lanes], axis=1
        )

    gradient = dot(own_block(0, 384), qs[...])
    adamw(qkv_s, (slice(None), slice(None)), gradient, rate_qkv, weight_decay)
    gradient = dot(own_block(384, 256), os[...])
    adamw(out_s, (slice(None), slice(None)), gradient, rate_out, weight_decay)
    for a, b in zip(results[0] + results[1], qkv_s + out_s):
        wire.stay(b, a)

    tile = gains_tile[...]
    rest = own_half(here, tile[:, 128:])
    for old, new in zip(gains, results[4]):
        new[...] = old[...]
    adamw(results[4], (slice(None), slice(0, 128)), tile[0:2, 0:128], rate_gains, 0.0)
    adamw(results[4], (slice(None), slice(128, 192)), rest[0:2, 0:64], rate_gains, 0.0)
    wire.finish()


def update(*operands):
    sizes = [(192, 768)] * 3 + [(192, 384)] * 3 + [(192, 2, 1024)] * 3 + [(192, 1024)] * 3
    held = [(192, 768)] * 3 + [(192, 384)] * 3 + [(2, 192, 1024)] * 3 + [(192, 1024)] * 3
    return pl.pallas_call(
        update_kernel,
        out_shape=[shape(F32, 2, 192, 512)] * 2
        + [shape(F32, *size) for size in sizes]
        + [shape(F32, 2, 192)] * 3,
        in_specs=[ANY] * 21 + [VM] * 4,
        out_specs=[ANY] * 14 + [VM] * 3,
        scratch_shapes=[
            pltpu.VMEM((2, 192, 512), F32),
            pltpu.VMEM((2, 192, 512), F32),
            pltpu.VMEM((8, 192, 128), BF),
            pltpu.VMEM((8, 192, 128), BF),
            pltpu.VMEM((2, 96, 2 * ATTN[0]), BF),
            pltpu.VMEM((2, 96, 2 * BOTH[0]), BF),
            pltpu.VMEM((2, 96, 2 * DOWN[0]), BF),
            pltpu.VMEM((768, 768), BF),
            pltpu.VMEM((512, 384), BF),
        ]
        + [pltpu.VMEM(size, F32) for size in held]
        + signals(64),
        compiler_params=pltpu.CompilerParams(vmem_limit_bytes=60 << 20),
        name="update",
    )(*operands)


def body(
    stream,
    cotangent,
    segments,
    positions,
    qkv_weight,
    qkv_first,
    qkv_second,
    out_weight,
    out_first,
    out_second,
    gate_up_weight,
    gate_up_first,
    gate_up_second,
    down_weight,
    down_first,
    down_second,
    gains,
    gains_first,
    gains_second,
):
    frequency = rope_theta ** (-2.0 * (jnp.arange(256) % (HS // 2)).astype(F32) / HS)
    frequency = jnp.broadcast_to(frequency, (8, 256))
    qkv_at, out_at = qkv_order(), out_order()
    stream_turned, cotangent_turned = stream.transpose(1, 2, 0), cotangent.transpose(1, 2, 0)
    (
        h1_all, wq, wo, c_all, kv_all, down_own, w_both,
        q, heads, cosine, sine, xtok, ctok, rise, h2_own, log_total, gtok, table,
    ) = enter(
        stream_turned, cotangent_turned, qkv_weight, out_weight.T, gate_up_weight, down_weight.T,
        gains, positions, frequency, qkv_at, out_at,
    )
    after, gain_two, f_part, d_all, *sums = feed(
        h2_own, gtok, rise, xtok, ctok, down_own, w_both, c_all
    )
    o_tiles, s_tiles, attn_grads, both_grads, down_grads, gains_tile = leave(
        gtok, gain_two, log_total, table,
        f_part, *sums, d_all, wo, q, kv_all, heads, h1_all, wq, xtok, rise, after, cosine, sine,
    )
    made = update(
        stream_turned, cotangent_turned, o_tiles, s_tiles, attn_grads, both_grads, down_grads, qkv_at, out_at,
        qkv_weight, qkv_first, qkv_second,
        out_weight.T, out_first.T, out_second.T,
        gate_up_weight, gate_up_first, gate_up_second,
        down_weight.T, down_first.T, down_second.T,
        gains, gains_first, gains_second,
        gains_tile,
    )
    output, stream_grad = made[0].transpose(2, 0, 1), made[1].transpose(2, 0, 1)
    states = [made[2 + 3 * n : 5 + 3 * n] for n in range(5)]
    for n in (1, 3):
        states[n] = [a.T for a in states[n]]
    return (output, stream_grad, *(a for w, m, v in states for a in (m, v, w)))


def solution(mesh):
    tokens = P("col", "dp", "row")
    table = P("dp", None)
    wide, tall, pairs, both = P("row", "col"), P("col", "row"), P("row", None, "col"), P(None, "row")
    weights = (wide,) * 3 + (tall,) * 3 + (pairs,) * 3 + (tall,) * 3 + (both,) * 3
    return jax.shard_map(
        body,
        mesh=mesh,
        in_specs=(tokens, tokens, table, table, *weights),
        out_specs=(tokens, tokens, *weights),
        check_vma=False,
    )
```
